128 devices in a mesh: dp: 8 (over x, core), mp: 16 (over y, z).
Axes of the slice: x: 4, y: 4, z: 4, core: 2. Of those that a mesh axis runs over, the one named last changes fastest.
Arguments:
- queries: bfloat16 [1024, 4096], P('dp'), may hold values from -103 to 103
- new_kv: bfloat16 [2, 1024, 1024], P(None, 'dp'), may hold values from -6 to 6
- residual: bfloat16 [1024, 4096], P('dp', 'mp'), may hold values from -2.4 to 2.4
- out_weight: bfloat16 [4096, 4096], P('mp'), may hold values from -0.125 to 0.125
- norm_gain: float32 [4096], replicated, may hold values from 0.5 to 1.5
- router: bfloat16 [4096, 8], replicated, may hold values from -0.09375 to 0.09375
- expert_in: bfloat16 [8, 2, 8192, 4096], P('dp', None, 'mp'), may hold values from -0.09375 to 0.09375
- expert_out: bfloat16 [8, 8192, 4096], P('dp', 'mp'), may hold values from -0.09375 to 0.09375
- node_cache: bfloat16 [2, 768, 16, 64, 128], P(None, 'dp', 'mp'), may hold values from -6 to 6
- leaf_cache: bfloat16 [2, 1024, 16, 64, 128], P(None, 'dp', 'mp'), may hold values from -6 to 6
- slot_request: int32 [1024], replicated, may hold values from 0 to 1023, each once
- request_branch: int32 [1024], replicated, may hold values from 0 to 63, as said below
- branch_parent: int32 [64], replicated, may hold values from 0 to 15, as said below
- root_owner: int32 [16], replicated, may hold values from 0 to 7, as said below
- branch_owner: int32 [64], replicated, may hold values from 0 to 7, as said below
- root_pages: int32 [16, 32], replicated, may hold values from 0 to 95, as said below
- branch_pages: int32 [64, 4], replicated, may hold values from 0 to 95, as said below
- root_len: int32 [16], replicated, may hold values from 1 to 4096, as said below
- branch_len: int32 [64], replicated, may hold values from 1 to 512
- leaf_len: int32 [1024], P('dp'), may hold values from 1 to 128
- routes: int32 [1024, 2], P('dp'), may hold values from 0 to 7, all different within a row; in each aligned block of 128 rows (0 to 127, 128 to 255, ...) at most 64 rows name the same one
Outputs:
- layer_out: bfloat16 [1024, 4096], P('dp', 'mp')
The draws below stay inside these ranges and needn't reach their ends.
Inputs may be any that keep to these rules, and one draw needn't show every extreme that they name: `request_branch`: at most 32 requests share a branch, and some branch has exactly 32. `branch_parent`: every root has exactly 4 branches. `root_owner`: every index of dp holds exactly 2 roots. `branch_owner`: every index of dp holds exactly 8 branches. `root_pages`: no slot of an owner's pool serves two pages of its nodes. `branch_pages`: no slot of an owner's pool serves two pages of its nodes. `root_len`: some root has 32 full pages.
All inputs are finite; a program needn't handle non-finite values.
Results may differ from the reference program's by a relative error of at most 0.034.
Values may be sent and summed in bfloat16 or wider, within the bound.
A program may use at most 576 MiB of HBM per device.

```python
import math
import jax
import jax.numpy as jnp
import numpy as np
from jax import lax

D = 4096
HEADS = 32
KVH = 8
HD = 128
EXPERTS = 8
TOP = 2
FF = 8192
PAGE = 128
R_DEV = 128
ROOT_DEV = 2
ROOT_PG = 32
BR_PG = 4
REQS = 1024
ROOTS = 16
BRANCHES = 64
KIDS = 4
BR_CAP = 32
E_CAP = 64
POOL_DEV = 96
POOL = 768
PARTS_SIZE = 2
N_DP = 8


def tree_tables(key):
    table_keys = jax.random.split(jax.random.fold_in(key, 7), 4)
    root_order = jax.random.permutation(table_keys[0], ROOTS)
    branch_order = jax.random.permutation(table_keys[1], BRANCHES)
    parent_order = jax.random.permutation(table_keys[2], BRANCHES)
    pool_orders = jax.vmap(lambda pool_key: jax.random.permutation(pool_key, POOL_DEV))(jax.random.split(table_keys[3], N_DP))
    root_owner = root_order % N_DP
    branch_owner = branch_order % N_DP
    root_slots = (root_order // N_DP)[:, None] * ROOT_PG + jnp.arange(ROOT_PG)[None, :]
    branch_slots = ROOT_DEV * ROOT_PG + (branch_order // N_DP)[:, None] * BR_PG + jnp.arange(BR_PG)[None, :]
    root_pages = pool_orders[root_owner[:, None], root_slots]
    branch_pages = pool_orders[branch_owner[:, None], branch_slots]
    branch_parent = parent_order // KIDS
    return (root_owner, branch_owner, root_pages, branch_pages, branch_parent)


def draw_root_owner(key, part):
    return tree_tables(key)[0].astype(jnp.int32)


def draw_branch_owner(key, part):
    return tree_tables(key)[1].astype(jnp.int32)


def draw_root_pages(key, part):
    return tree_tables(key)[2].astype(jnp.int32)


def draw_branch_pages(key, part):
    return tree_tables(key)[3].astype(jnp.int32)


def draw_branch_parent(key, part):
    return tree_tables(key)[4].astype(jnp.int32)


def draw_request_branch(key, part):
    pick_key, shuffle_key, label_key = jax.random.split(jax.random.fold_in(key, 11), 3)
    spare = BRANCHES * BR_CAP - BR_CAP
    picks = jax.random.permutation(pick_key, spare)[:REQS - BR_CAP] + BR_CAP
    places = jnp.concatenate([jnp.arange(BR_CAP), picks])
    places = jax.random.permutation(shuffle_key, places)
    relabel = jax.random.permutation(label_key, BRANCHES)
    return relabel[places // BR_CAP].astype(jnp.int32)


def draw_root_len(key, part):
    shift_key, cut_key, full_key = jax.random.split(jax.random.fold_in(key, 13), 3)
    longest = ROOT_PG * PAGE
    full_root = jax.random.randint(full_key, (), 0, ROOTS)
    short_root = (full_root + 1) % ROOTS
    shifts = jax.random.randint(shift_key, (ROOTS,), 0, 7)
    shifts = jnp.where(jnp.arange(ROOTS) == short_root, 6, shifts)
    ceiling = jnp.maximum(jnp.right_shift(jnp.full((ROOTS,), longest, jnp.int32), shifts), 1)
    trimmed = jax.random.randint(cut_key, (ROOTS,), 0, ceiling // 2 + 1)
    return jnp.where(jnp.arange(ROOTS) == full_root, longest, ceiling - trimmed).astype(jnp.int32)


def draw_queries(key, part):
    base_key = jax.random.fold_in(key, 0)
    values = 2.0 * jnp.clip(jax.random.normal(base_key, (REQS, HEADS * HD), jnp.float32), -5.0, 5.0)
    return values.astype(jnp.bfloat16)


def draw_residual(key, part):
    column = jnp.arange(D, dtype=jnp.float32) / D
    values = 0.15 * jnp.clip(jax.random.normal(key, (REQS, D), jnp.float32), -5.0, 5.0) * jnp.exp(1.1 * column)[None, :]
    return values.astype(jnp.bfloat16)


def place_ends(array, own_key, smallest, high):
    dims = array.shape
    spot = [jax.random.randint(jax.random.fold_in(own_key, axis), (), 0, dims[axis]) for axis in range(len(dims))]
    array = array.at[tuple(spot)].set(smallest)
    longest = dims.index(max(dims))
    spot[longest] = (spot[longest] + 1) % dims[longest]
    return array.at[tuple(spot)].set(high)


def spiked(result, stream_key, source, target, blocks, factor):
    def block_of(position):
        return (jnp.arange(result.shape[position]) // (result.shape[position] // blocks)).reshape((-1,) + (1,) * (result.ndim - 1 - position))

    near = jax.random.permutation(stream_key, blocks)[block_of(target)]
    far = (block_of(target) + blocks // 2) % blocks
    return jnp.where((block_of(source) == near) | (block_of(source) == far), factor * result, result)


def level_of(stream_key, extent, cuts, smallest, largest):
    factor_of, own = 1.0, jax.random.fold_in(stream_key, 6)
    for dim, blocks in cuts:
        draws = jnp.exp(jax.random.uniform(jax.random.fold_in(own, dim), (blocks,), jnp.float32, smallest / len(cuts), largest / len(cuts)))
        factor_of = factor_of * jnp.repeat(draws, extent[dim] // blocks).reshape([-1 if axis == dim else 1 for axis in range(len(extent))])
    return factor_of


def deal_out(key, own, number, rows, number_of, top, limit, slope):
    order = jax.random.permutation(key, number_of)
    packed, usual = load_shares(number_of, rows * top, limit, slope, True), load_shares(number_of, rows * top, limit, slope, False)
    places = jnp.arange(number_of)

    def named(sizes, offset_by):
        used = int((sizes > 0).sum())
        fixed = max(1, used // 4)
        shifted = fixed + (places - fixed + offset_by * (used - fixed)) % max(1, number_of - fixed)
        return jnp.zeros((number_of,), jnp.int32).at[order[jnp.where(places < fixed, places, shifted)]].set(jnp.asarray(sizes, jnp.int32))

    sizes = jnp.where(number % 4 == 0, named(packed, number // 4), named(usual, number - number // 4 - 1))
    mixed = jax.random.permutation(jax.random.fold_in(own, 3), number_of)
    donor, sink = mixed[0:number_of // 2 * 2:2], mixed[1:number_of // 2 * 2:2]
    slack = jnp.minimum(sizes[donor] - 1, limit - sizes[sink]) // 2
    slack = jnp.where((donor == order[0]) | (sink == order[0]) | (sizes[sink] == 0), 0, jnp.maximum(slack, 0))
    shifted = jax.random.randint(jax.random.fold_in(own, 4), (number_of // 2,), 0, 1 << 20) % (slack + 1)
    sizes = sizes.at[donor].add(-shifted).at[sink].add(shifted)
    members = jnp.searchsorted(jnp.cumsum(sizes), jnp.arange(rows * top), side="right").astype(jnp.int32)
    listing = members.reshape(top, rows).T
    listing = listing[jax.random.permutation(jax.random.fold_in(own, 1), rows)]
    offset_by = jax.random.randint(jax.random.fold_in(own, 2), (rows, 1), 0, top)
    return jnp.take_along_axis(listing, (jnp.arange(top)[None, :] + offset_by) % top, axis=1)


def load_shares(count, total, limit, slope, full):
    loads = [(1 << 20) // math.isqrt(grade ** slope) + 1 for grade in range(1, count + 1)]
    largest = limit if full else min(limit, max(-(-total // count), total * loads[0] // sum(loads)))
    least = 1 if total - largest >= count - 1 else 0
    holding, spare = [largest] + [least] * (count - 1), total - largest - least * (count - 1)
    while spare > 0:
        candidates = [i for i in range(1, count) if holding[i] < largest] or [i for i in range(1, count) if holding[i] < limit]
        pool, remaining = sum([loads[i] for i in candidates]), spare
        for i in candidates:
            more = min(limit - holding[i], max(1, remaining * loads[i] // pool), spare)
            holding[i] = holding[i] + more
            spare = spare - more
    return np.array(holding)


def gaussian(stream_key, extent, deviation, limit, cuts=(), held_as=jnp.bfloat16):
    drawn = jax.random.normal(stream_key, extent, jnp.float32) * deviation
    if len(cuts) > 0:
        drawn = level_of(stream_key, extent, cuts, -0.22, 0.18) * drawn
    return jnp.clip(drawn, min=-limit, max=limit).astype(held_as)


def gaussian_with(own_key, extent, spread, bound, cuts, heavy, held_as=jnp.bfloat16):
    drawn = spread * jax.random.normal(own_key, extent, jnp.float32)
    if cuts:
        drawn = drawn * level_of(own_key, extent, cuts, -0.22, 0.18)
    return jnp.clip(spiked(drawn, jax.random.fold_in(own_key, 3), *heavy), -bound, bound).astype(held_as)


def setup_inputs(seed: int = 0) -> dict:
    streams_of = jax.random.split(jax.random.key(seed), 22)
    queries = draw_queries(jax.random.fold_in(streams_of[21], 71), 0)
    new_kv = gaussian(streams_of[1], (2, REQS, KVH * HD), 1.0, 6.0, ((1, 8),))
    residual = draw_residual(jax.random.fold_in(streams_of[21], 71), 0)
    out_weight = gaussian_with(streams_of[3], (HEADS * HD, D), (HEADS * HD) ** -0.5, 0.125, ((0, 16),), (0, 1, 16, 2.0))
    norm_gain = jnp.clip(1.0 + 0.1 * jax.random.normal(streams_of[4], (D,), jnp.float32), 0.5, 1.5)
    router = gaussian(streams_of[5], (D, EXPERTS), D ** -0.5, 0.09375)
    expert_in = gaussian(streams_of[6], (EXPERTS, 2, FF, D), D ** -0.5, 0.09375, ((0, 8), (2, 16)))
    expert_out = gaussian_with(streams_of[7], (EXPERTS, FF, D), FF ** -0.5, 0.09375, ((0, 8), (1, 16)), (1, 2, 16, 2.0))
    node_cache = gaussian(streams_of[8], (2, POOL, KVH * PARTS_SIZE, PAGE // PARTS_SIZE, HD), 1.0, 6.0, ((1, 8), (2, 16)))
    leaf_cache = gaussian(streams_of[9], (2, REQS, KVH * PARTS_SIZE, PAGE // PARTS_SIZE, HD), 1.0, 6.0, ((1, 8), (2, 16)))
    slot_request = jax.random.permutation(streams_of[10], REQS).astype(jnp.int32)
    request_branch = draw_request_branch(jax.random.fold_in(streams_of[21], 71), 0)
    branch_parent = draw_branch_parent(jax.random.fold_in(streams_of[21], 71), 0)
    root_owner = draw_root_owner(jax.random.fold_in(streams_of[21], 71), 0)
    branch_owner = draw_branch_owner(jax.random.fold_in(streams_of[21], 71), 0)
    root_pages = draw_root_pages(jax.random.fold_in(streams_of[21], 71), 0)
    branch_pages = draw_branch_pages(jax.random.fold_in(streams_of[21], 71), 0)
    root_len = draw_root_len(jax.random.fold_in(streams_of[21], 71), 0)
    branch_len = place_ends(jax.random.randint(streams_of[18], (BRANCHES,), 1, BR_PG * PAGE + 1), jax.random.fold_in(streams_of[18], 1), 1, BR_PG * PAGE).astype(jnp.int32)
    leaf_len = place_ends(jax.random.randint(streams_of[19], (REQS,), 1, PAGE + 1), jax.random.fold_in(streams_of[19], 1), 1, PAGE).astype(jnp.int32)
    routes_keys = jax.random.split(jax.random.fold_in(streams_of[20], 1), REQS // R_DEV)
    routes_turns = jax.random.permutation(jax.random.fold_in(streams_of[20], 3), REQS // R_DEV)
    routes = jax.vmap(lambda own, number: deal_out(jax.random.fold_in(streams_of[20], 2), own, number, R_DEV, EXPERTS, TOP, E_CAP, 2))(routes_keys, routes_turns).reshape((REQS, TOP))
    return {"queries": queries, "new_kv": new_kv, "residual": residual, "out_weight": out_weight, "norm_gain": norm_gain, "router": router, "expert_in": expert_in, "expert_out": expert_out, "node_cache": node_cache, "leaf_cache": leaf_cache, "slot_request": slot_request, "request_branch": request_branch, "branch_parent": branch_parent, "root_owner": root_owner, "branch_owner": branch_owner, "root_pages": root_pages, "branch_pages": branch_pages, "root_len": root_len, "branch_len": branch_len, "leaf_len": leaf_len, "routes": routes}


MASKED_SCORE = -1e+30
NORM_EPS = 1e-05

def rounded(weights):
    return lax.optimization_barrier(weights.astype(jnp.bfloat16)).astype(jnp.float32)

def level_partial(group_queries, key_block, value_block, usable):
    scores = jnp.einsum('ghd,gpld->gphl', group_queries.astype(jnp.float32), key_block.astype(jnp.float32)) * HD ** (-0.5)
    usable = usable[None, :, None, :]
    masked_scores = jnp.where(usable, scores, MASKED_SCORE)
    row_max = lax.optimization_barrier(jnp.max(masked_scores, axis=-1))
    weights = jnp.where(usable, jnp.exp(masked_scores - row_max[..., None]), 0.0)
    weight_total = lax.optimization_barrier(jnp.sum(weights, axis=-1))
    weighted_sum = jnp.einsum('gphl,gpld->gphd', rounded(weights), value_block.astype(jnp.float32))
    return (weighted_sum, row_max, weight_total)

def token_places(page_count):
    token_width = PAGE // PARTS_SIZE
    page_starts = jnp.arange(page_count, dtype=jnp.int32)[:, None] * PAGE
    inside = jnp.arange(token_width, dtype=jnp.int32)[None, :]
    return jnp.stack([(page_starts + part_index * token_width + inside).reshape(-1) for part_index in range(PARTS_SIZE)])

def node_blocks(node_cache, owner, page_list):
    page_ids = (owner * POOL_DEV + page_list).astype(jnp.int32)
    chosen = jnp.take(node_cache, page_ids, axis=1)
    chosen = chosen.reshape(2, page_list.shape[0], KVH, PARTS_SIZE, PAGE // PARTS_SIZE, HD)
    return jnp.transpose(chosen, (0, 2, 3, 1, 4, 5)).reshape(2, KVH, PARTS_SIZE, -1, HD)

def reference(queries, new_kv, residual, out_weight, norm_gain, router, expert_in, expert_out, node_cache, leaf_cache, slot_request, request_branch, branch_parent, root_owner, branch_owner, root_pages, branch_pages, root_len, branch_len, leaf_len, routes):
    requests = queries.shape[0]
    group_size = HEADS // KVH

    def request_output(slot_index):
        request = slot_request[slot_index]
        branch = request_branch[request]
        root_node = branch_parent[branch]
        group_queries = queries[slot_index].reshape(KVH, group_size, HD)
        root_kv = node_blocks(node_cache, root_owner[root_node], root_pages[root_node])
        root_part = level_partial(group_queries, root_kv[0], root_kv[1], token_places(ROOT_PG) < root_len[root_node])
        branch_kv = node_blocks(node_cache, branch_owner[branch], branch_pages[branch])
        branch_part = level_partial(group_queries, branch_kv[0], branch_kv[1], token_places(BR_PG) < branch_len[branch])
        leaf_kv = leaf_cache[:, slot_index].reshape(2, KVH, PARTS_SIZE, PAGE // PARTS_SIZE, HD)
        leaf_part = level_partial(group_queries, leaf_kv[0], leaf_kv[1], token_places(1) < leaf_len[slot_index])
        fresh_keys = new_kv[0, slot_index].reshape(KVH, HD).astype(jnp.float32)
        fresh_values = new_kv[1, slot_index].reshape(KVH, HD).astype(jnp.float32)
        self_score = jnp.einsum('ghd,gd->gh', group_queries.astype(jnp.float32), fresh_keys) * HD ** (-0.5)
        sums = jnp.concatenate([root_part[0], branch_part[0], leaf_part[0]], axis=1)
        maxima = jnp.concatenate([root_part[1], branch_part[1], leaf_part[1]], axis=1)
        totals = jnp.concatenate([root_part[2], branch_part[2], leaf_part[2]], axis=1)
        common_max = jnp.maximum(lax.optimization_barrier(jnp.max(maxima, axis=1)), self_score)
        factors = jnp.exp(maxima - common_max[:, None, :])
        self_factor = jnp.exp(self_score - common_max)
        weighted = lax.optimization_barrier(jnp.sum(sums * factors[..., None], axis=1)) + self_factor[..., None] * fresh_values[:, None, :]
        weight_total = lax.optimization_barrier(jnp.sum(totals * factors, axis=1)) + self_factor
        return (weighted / weight_total[..., None]).reshape(HEADS * HD).astype(jnp.bfloat16)

    def block_output(block_slots):
        return jax.vmap(request_output)(block_slots)
    slot_blocks = jnp.arange(requests, dtype=jnp.int32).reshape(-1, 16)
    attended = lax.map(block_output, slot_blocks).reshape(requests, HEADS * HD)
    attention_out = jnp.dot(attended, out_weight, preferred_element_type=jnp.float32)
    hidden = residual.astype(jnp.float32) + attention_out
    inv_rms = lax.rsqrt(lax.optimization_barrier(jnp.mean(hidden * hidden, axis=1)) + NORM_EPS)
    normed = (hidden * inv_rms[:, None] * norm_gain[None, :]).astype(jnp.bfloat16)
    logits = jnp.dot(normed, router, preferred_element_type=jnp.float32)
    chosen = jnp.take_along_axis(logits, routes, axis=1)
    gate_weights = jax.nn.softmax(chosen, axis=1)
    flat_routes = routes.reshape(-1)
    pair_count = flat_routes.shape[0]
    pair_order = jnp.argsort(flat_routes, stable=True).astype(jnp.int32)
    expert_counts = lax.optimization_barrier(jnp.sum((flat_routes[None, :] == jnp.arange(EXPERTS, dtype=jnp.int32)[:, None]).astype(jnp.int32), axis=1))
    expert_starts = jnp.cumsum(expert_counts) - expert_counts
    capacity = N_DP * E_CAP

    def expert_step(outputs, expert):
        offsets = jnp.arange(capacity, dtype=jnp.int32)
        live = offsets < expert_counts[expert]
        spots = jnp.minimum(expert_starts[expert] + offsets, pair_count - 1).astype(jnp.int32)
        pairs = jnp.where(live, jnp.take(pair_order, spots), pair_count).astype(jnp.int32)
        token_rows = jnp.take(normed, pairs // TOP, axis=0, mode='fill', fill_value=0)
        gate_up = expert_in[expert]
        gate_part = jnp.dot(token_rows, gate_up[0].T, preferred_element_type=jnp.float32)
        up_part = jnp.dot(token_rows, gate_up[1].T, preferred_element_type=jnp.float32)
        expert_hidden = (jax.nn.silu(gate_part) * up_part).astype(jnp.bfloat16)
        expert_result = jnp.dot(expert_hidden, expert_out[expert], preferred_element_type=jnp.float32).astype(jnp.bfloat16)
        return (outputs.at[pairs].set(expert_result, mode='drop'), None)
    outputs, ignored = lax.scan(expert_step, jnp.zeros((pair_count, D), jnp.bfloat16), jnp.arange(EXPERTS, dtype=jnp.int32))
    results = outputs.reshape(requests, TOP, D).astype(jnp.float32)
    layer_out = hidden + lax.optimization_barrier(jnp.sum(gate_weights[:, :, None] * results, axis=1))
    return layer_out.astype(jnp.bfloat16)
```

```python
import jax
import jax.numpy as jnp
from jax import lax
from jax.experimental import pallas as pl
from jax.experimental.pallas import tpu as pltpu
from jax.sharding import PartitionSpec as P

EXPERTS = 8
PAGE = 128
ROOT_DEV = 2
BR_DEV = 8
BR_CAP = 32
E_CAP = 64

MASKED_SCORE = -1e30
NORM_EPS = 1e-05

BF = jnp.bfloat16
F32 = jnp.float32
MESH = pl.DeviceIdType.MESH
ROWS = 128
PART_ROWS = ((0, 48), (48, 48), (96, 32))
AXES = ("x", "y", "z")


def place():
    dp = lax.axis_index("dp")
    mp = lax.axis_index("mp")
    return {"x": dp // 2, "c": dp % 2, "y": mp // 4, "z": mp % 4}


def device_of(at, **moved):
    at = {**at, **moved}
    return (at["x"] * 2 + at["c"], at["y"] * 4 + at["z"])


def step_along(at, axis, by):
    return device_of(at, **{axis: (at[axis] + by) % 4})


def greet(peers):
    barrier = pltpu.get_barrier_semaphore()
    for peer in peers:
        pl.semaphore_signal(barrier, inc=1, device_id=peer, device_id_type=MESH)
    pl.semaphore_wait(barrier, len(peers))


def remote(src, dst, sems, key, device):
    return pltpu.make_async_remote_copy(
        src_ref=src,
        dst_ref=dst,
        send_sem=sems[0].at[key],
        recv_sem=sems[1].at[key],
        device_id=device,
        device_id_type=MESH,
    )


def all_peers(at):
    return [step_along(at, axis, by) for axis in AXES for by in (1, 3)] + [
        device_of(at, c=1 - at["c"])
    ]


def gather_kernel(own_ref, buf_ref, local_sem, send_sem, recv_sem):
    at = place()
    sems = (send_sem, recv_sem)
    greet(all_peers(at))
    sibling = device_of(at, c=1 - at["c"])

    def slab(part, order, phase, value, half, core):
        index = {"x": at["x"], "y": at["y"], "z": at["z"]}
        for axis in order[:phase]:
            index[axis] = slice(None)
        index[order[phase]] = value
        row, rows = PART_ROWS[part]
        return buf_ref.at[
            index["x"],
            core,
            index["y"],
            index["z"],
            half,
            pl.ds(row, rows),
            :,
        ]

    both = slice(None)
    mine = buf_ref.at[at["x"], at["c"], at["y"], at["z"]]
    local = pltpu.make_async_copy(own_ref, mine, local_sem)
    local.start()
    orders = [AXES[part:] + AXES[:part] for part in range(3)]
    started = []

    def send(src, dst, key, device):
        copy = remote(src, dst, sems, key, device)
        copy.start()
        started.append(copy)

    def arrive(ref, key):
        remote(ref, ref, sems, key, sibling).wait_recv()

    core = at["c"]
    for phase in range(3):
        for part in range(3):
            order = orders[part]
            axis = order[phase]
            v = at[axis]
            key = part * 16 + phase * 4
            ref = slab(part, order, phase, v, both, core)
            if phase == 0:
                row, rows = PART_ROWS[part]
                src = own_ref.at[:, pl.ds(row, rows), :]
            else:
                src = ref
            send(src, ref, key, step_along(at, axis, 1))
            send(src, ref, key + 1, step_along(at, axis, 3))
            if phase == 2:
                send(src, ref, part * 16 + 12, sibling)
        for part in range(3):
            order = orders[part]
            axis = order[phase]
            v = at[axis]
            key = part * 16 + phase * 4
            low = slab(part, order, phase, (v + 3) % 4, both, core)
            arrive(low, key)
            first = slab(part, order, phase, (v + 3) % 4, 0, core)
            send(first, first, key + 2, step_along(at, axis, 1))
            high = slab(part, order, phase, (v + 1) % 4, both, core)
            arrive(high, key + 1)
            second = slab(part, order, phase, (v + 1) % 4, 1, core)
            send(second, second, key + 3, step_along(at, axis, 3))
            if phase == 2:
                send(low, low, part * 16 + 13, sibling)
                send(high, high, part * 16 + 14, sibling)
        if phase == 0:
            local.wait()
        for part in range(3):
            order = orders[part]
            axis = order[phase]
            v = at[axis]
            key = part * 16 + phase * 4
            far = (v + 2) % 4
            arrive(slab(part, order, phase, far, 0, core), key + 2)
            arrive(slab(part, order, phase, far, 1, core), key + 3)
            if phase == 2:
                ref = slab(part, order, phase, far, both, core)
                send(ref, ref, part * 16 + 15, sibling)
    for part in range(3):
        order = orders[part]
        v = at[order[2]]
        for key, by in ((12, 0), (13, 3), (14, 1), (15, 2)):
            arrive(slab(part, order, 2, (v + by) % 4, both, 1 - core), part * 16 + key)
    for copy in started:
        copy.wait_send()


def gather_rows(own):
    return pl.pallas_call(
        gather_kernel,
        out_shape=jax.ShapeDtypeStruct((4, 2, 4, 4, 2, ROWS, 128), BF),
        in_specs=[pl.BlockSpec(memory_space=pl.ANY)],
        out_specs=pl.BlockSpec(memory_space=pl.ANY),
        scratch_shapes=[
            pltpu.SemaphoreType.DMA,
            pltpu.SemaphoreType.DMA((48,)),
            pltpu.SemaphoreType.DMA((48,)),
        ],
        compiler_params=pltpu.CompilerParams(collective_id=1, has_side_effects=True),
        name="gather_rows",
    )(own)


FF_STEPS = 2


def expert_kernel(
    buf_ref, rank_ref, other_ref, mine_ref, gain_ref, router_ref, up_ref, down_ref,
    out_ref, rows_ref, gate_ref, total_ref, block_ref, block_sem,
):
    step = pl.program_id(0)
    cap = E_CAP

    def fetch(block, slot):
        return pltpu.make_async_copy(
            buf_ref.at[block // 2, block % 2], block_ref.at[slot], block_sem.at[slot]
        )

    @pl.when(step == 0)
    def _():
        fetch(0, 0).start()

        def body(block, _):
            slot = lax.rem(block, 2)

            @pl.when(block < 7)
            def _():
                fetch(block + 1, 1 - slot).start()

            fetch(block, slot).wait()
            pick = (
                lax.broadcasted_iota(jnp.int32, (cap, ROWS), 0) == rank_ref[pl.ds(block, 1), :]
            ).astype(BF)
            squares = jnp.zeros((cap, 1), F32)
            pieces = []
            for y in range(4):
                for z in range(4):
                    whole = jnp.concatenate([block_ref[slot, y, z, 0], block_ref[slot, y, z, 1]], axis=1)
                    piece = jnp.dot(pick, whole, preferred_element_type=F32)
                    squares += jnp.sum(piece * piece, axis=1, keepdims=True)
                    pieces.append(piece.astype(BF))
            scale = lax.rsqrt(squares / (32.0 * 128.0) + NORM_EPS)
            base = pl.multiple_of(block * cap, cap)
            for i, piece in enumerate(pieces):
                cols = pl.ds(i * 256, 256)
                rows_ref[pl.ds(base, cap), cols] = (
                    piece.astype(F32) * scale * gain_ref[0:1, cols]
                ).astype(BF)
            return 0

        lax.fori_loop(0, 8, body, 0)
        logits = jnp.dot(rows_ref[...], router_ref[...], preferred_element_type=F32)
        lane = lax.broadcasted_iota(jnp.int32, logits.shape, 1)
        here = jnp.sum(jnp.where(lane == mine_ref[0, 0], logits, 0.0), axis=1, keepdims=True)
        there = jnp.sum(jnp.where(lane == other_ref[...], logits, 0.0), axis=1, keepdims=True)
        most = jnp.maximum(here, there)
        here = jnp.exp(here - most)
        there = jnp.exp(there - most)
        gate_ref[...] = jnp.broadcast_to(here / (here + there), gate_ref.shape)

    width = up_ref.shape[1]
    contract = (((1,), (1,)), ((), ()))
    gate = lax.dot_general(rows_ref[...], up_ref[0], contract, preferred_element_type=F32)
    up = lax.dot_general(rows_ref[...], up_ref[1], contract, preferred_element_type=F32)
    hidden = (gate / (1.0 + jnp.exp(-gate)) * up).astype(BF)

    def piece(i, last):
        partial = jnp.dot(hidden, down_ref[:, i * 256 : (i + 1) * 256], preferred_element_type=F32)
        if FF_STEPS > 1:
            if last:
                partial += total_ref[i]
            else:
                total_ref[i] = partial
        if last:
            scaled = (partial * gate_ref[:, 0:1]).astype(BF)
            for half in range(2):
                out_ref[:, i, half] = scaled[:, half * 128 : (half + 1) * 128].reshape(8, cap, 128)

    for last in (False, True):
        @pl.when((step == FF_STEPS - 1) == last)
        def _():
            for i in range(16):
                piece(i, last)


def run_experts(buf, rank, other, mine, gain, router, expert_in, expert_out):
    width = expert_in.shape[1] // FF_STEPS
    deep = expert_in.shape[2]
    return pl.pallas_call(
        expert_kernel,
        grid=(FF_STEPS,),
        out_shape=jax.ShapeDtypeStruct((8, 16, 2, E_CAP, 128), BF),
        in_specs=[
            pl.BlockSpec(memory_space=pl.ANY),
            pl.BlockSpec((8, ROWS), lambda f: (0, 0)),
            pl.BlockSpec((8 * E_CAP, 1), lambda f: (0, 0)),
            pl.BlockSpec(memory_space=pltpu.SMEM),
            pl.BlockSpec((1, deep), lambda f: (0, 0)),
            pl.BlockSpec((deep, EXPERTS), lambda f: (0, 0)),
            pl.BlockSpec((2, width, deep), lambda f: (0, f, 0)),
            pl.BlockSpec((width, deep), lambda f: (f, 0)),
        ],
        out_specs=pl.BlockSpec((8, 16, 2, E_CAP, 128), lambda f: (0, 0, 0, 0, 0)),
        scratch_shapes=[
            pltpu.VMEM((8 * E_CAP, deep), BF),
            pltpu.VMEM((8 * E_CAP, 128), F32),
            pltpu.VMEM((16, 8 * E_CAP, 256), F32),
            pltpu.VMEM((2, 4, 4, 2, ROWS, 128), BF),
            pltpu.SemaphoreType.DMA((2,)),
        ],
        compiler_params=pltpu.CompilerParams(
            vmem_limit_bytes=56 * 2**20, dimension_semantics=("arbitrary",)
        ),
        cost_estimate=pl.CostEstimate(
            flops=6 * 512 * 512 * 4096, bytes_accessed=25 * 2**20, transcendentals=512 * 512
        ),
        name="run_experts",
    )(buf, rank, other, mine, gain, router, expert_in, expert_out)


def return_kernel(
    part_ref, rank_ref, kept_ref, out_ref,
    theirs_ref, sum_ref, half1, full1, half2, full2, half3, full3, sib_send, sib_recv, send_sem, recv_sem,
):
    at = place()
    greet(all_peers(at))
    sems = (send_sem, recv_sem)
    sibling = device_of(at, c=1 - at["c"])
    core = at["c"]
    cross = pltpu.make_async_remote_copy(
        src_ref=part_ref.at[:, 1 - core],
        dst_ref=theirs_ref,
        send_sem=sib_send,
        recv_sem=sib_recv,
        device_id=sibling,
        device_id_type=MESH,
    )
    cross.start()
    cross.wait()
    lane = lax.broadcasted_iota(jnp.int32, (ROWS, E_CAP), 1)
    for x in range(4):
        spread = jnp.concatenate(
            [
                (rank_ref[x, 0] == lane).astype(BF),
                (rank_ref[x, 1] == lane).astype(BF),
            ],
            axis=1,
        )

        def body(i, _):
            y, z = i // 4, lax.rem(i, 4)
            for half in range(2):
                both = jnp.concatenate(
                    [part_ref[x, core, i, half], theirs_ref[x, i, half]], axis=0
                )
                sum_ref[x, y, z, half] = jnp.dot(
                    spread, both, preferred_element_type=F32
                ).astype(BF)
            return 0

        lax.fori_loop(0, 16, body, 0)

    started = []

    def send(src, dst, key, device):
        copy = remote(src, dst, sems, key, device)
        copy.start()
        started.append(copy)

    def arrive(ref, key):
        remote(ref, ref, sems, key, sibling).wait_recv()

    def finish(row, rows, half, total):
        spot = (pl.ds(row, rows), pl.ds(half * 128, 128))
        out_ref[spot] = (kept_ref[spot] + total).astype(BF)

    ring_reduce(
        at, sum_ref, AXES, [AXES[part:] + AXES[:part] for part in range(3)], PART_ROWS,
        (half1, half2, half3), (full1, full2, full3), send, arrive, 0, finish,
    )
    for copy in started:
        copy.wait_send()


def return_rows(partial, rank, kept):
    return pl.pallas_call(
        return_kernel,
        out_shape=jax.ShapeDtypeStruct((ROWS, 256), BF),
        in_specs=[pl.BlockSpec(memory_space=pltpu.VMEM)] * 3,
        out_specs=pl.BlockSpec(memory_space=pltpu.VMEM),
        scratch_shapes=[
            pltpu.VMEM((4, 16, 2, E_CAP, 128), BF),
            pltpu.VMEM((4, 4, 4, 2, ROWS, 128), BF),
            pltpu.VMEM((2, 4, 4, ROWS, 128), BF),
            pltpu.VMEM((2, 4, 4, 2, ROWS, 128), BF),
            pltpu.VMEM((2, 4, ROWS, 128), BF),
            pltpu.VMEM((2, 4, 2, ROWS, 128), BF),
            pltpu.VMEM((2, ROWS, 128), BF),
            pltpu.VMEM((2, 2, ROWS, 128), BF),
            pltpu.SemaphoreType.DMA,
            pltpu.SemaphoreType.DMA,
            pltpu.SemaphoreType.DMA((36,)),
            pltpu.SemaphoreType.DMA((36,)),
        ],
        compiler_params=pltpu.CompilerParams(
            collective_id=2, has_side_effects=True, vmem_limit_bytes=48 * 2**20
        ),
        name="return_rows",
    )(partial, rank, kept)


LOG2E = 1.4426950408889634


def query_kernel(queries_ref, all_ref, local_sem, send_sem, recv_sem):
    at = place()
    sems = (send_sem, recv_sem)
    sibling = device_of(at, c=1 - at["c"])
    right, left = step_along(at, "x", 1), step_along(at, "x", 3)
    greet([right, left, sibling])
    x, core = at["x"], at["c"]
    kv_head = lax.axis_index("mp") // 2
    own = queries_ref.at[:, pl.ds(pl.multiple_of(kv_head * 512, 512), 512)]
    local = pltpu.make_async_copy(own, all_ref.at[x, core], local_sem)
    local.start()
    started = []

    def send(src, dst, key, device):
        copy = remote(src, dst, sems, key, device)
        copy.start()
        started.append(copy)

    def arrive(ref, key):
        remote(ref, ref, sems, key, sibling).wait_recv()

    low, high, far = (x + 3) % 4, (x + 1) % 4, (x + 2) % 4
    upper, lower = pl.ds(0, 64), pl.ds(64, 64)
    mine = all_ref.at[x, core]
    send(own, mine, 0, right)
    send(own, mine, 1, left)
    send(own, mine, 4, sibling)
    from_low, from_high = all_ref.at[low, core], all_ref.at[high, core]
    arrive(from_low, 0)
    first = all_ref.at[low, core, upper]
    send(first, first, 2, right)
    arrive(from_high, 1)
    second = all_ref.at[high, core, lower]
    send(second, second, 3, left)
    send(from_low, from_low, 5, sibling)
    send(from_high, from_high, 6, sibling)
    for key, rows in ((2, upper), (3, lower)):
        ref = all_ref.at[far, core, rows]
        arrive(ref, key)
        send(ref, ref, key + 5, sibling)
    for key, ref in (
        (4, all_ref.at[x, 1 - core]),
        (5, all_ref.at[low, 1 - core]),
        (6, all_ref.at[high, 1 - core]),
        (7, all_ref.at[far, 1 - core, upper]),
        (8, all_ref.at[far, 1 - core, lower]),
    ):
        arrive(ref, key)
    local.wait()
    for copy in started:
        copy.wait_send()


def gather_queries(queries):
    return pl.pallas_call(
        query_kernel,
        out_shape=jax.ShapeDtypeStruct((4, 2, ROWS, 512), BF),
        in_specs=[pl.BlockSpec(memory_space=pl.ANY)],
        out_specs=pl.BlockSpec(memory_space=pl.ANY),
        scratch_shapes=[
            pltpu.SemaphoreType.DMA,
            pltpu.SemaphoreType.DMA((9,)),
            pltpu.SemaphoreType.DMA((9,)),
        ],
        compiler_params=pltpu.CompilerParams(collective_id=3, has_side_effects=True),
        name="gather_queries",
    )(queries)


SCALE2 = LOG2E * 128 ** (-0.5)
BY_ROW = (((1,), (1,)), ((), ()))


def node_kernel(
    local_ref, branch_id_ref, root_pages_ref, branch_pages_ref, root_len_ref, branch_len_ref, part_ref,
    all_ref, pages_ref, code_row_ref, code_col_ref,
    sum_ref, stat_ref,
    query_ref, acc_ref, max_ref, total_ref, node_sum_ref, node_stat_ref,
):
    part = part_ref[0]
    lane = lax.broadcasted_iota(jnp.int32, (1, 128), 1)

    def pick(kind, base, count):
        wanted = lax.broadcasted_iota(jnp.int32, (count, 1024), 0) + base
        chosen = (wanted == code_row_ref[kind : kind + 1, :]).astype(BF)
        return jnp.dot(chosen, all_ref[...], preferred_element_type=F32).astype(BF)

    def put(row, rows):
        stats = jnp.zeros((rows, 128), F32)
        for h in range(4):
            span = pl.ds(h * rows, rows)
            node_sum_ref[pl.ds(row, rows), h * 128 : (h + 1) * 128] = acc_ref[span, :].astype(BF)
            stats = jnp.where(lane == h, max_ref[span, 0:1], stats)
            stats = jnp.where(lane == 4 + h, total_ref[span, 0:1], stats)
        node_stat_ref[pl.ds(row, rows), :] = stats

    chunk = 8
    for k in range(ROOT_DEV):
        root = local_ref[k]
        length = root_len_ref[root]
        picked = pick(0, k * 128, 128)
        for h in range(4):
            query_ref[h * 128 : (h + 1) * 128, :] = picked[:, h * 128 : (h + 1) * 128]
        acc_ref[...] = jnp.zeros_like(acc_ref)
        max_ref[...] = jnp.full_like(max_ref, MASKED_SCORE)
        total_ref[...] = jnp.zeros_like(total_ref)
        used = (length - part * 64 + PAGE - 1) // PAGE
        steps = (used + chunk - 1) // chunk

        def body(i, _):
            ids = [root_pages_ref[root, i * chunk + j] for j in range(chunk)]
            keys = jnp.concatenate([pages_ref[0, page] for page in ids], axis=0)
            values = jnp.concatenate([pages_ref[1, page] for page in ids], axis=0)
            spot = lax.broadcasted_iota(jnp.int32, (1, chunk * 64), 1)
            spot = (i * chunk + spot // 64) * PAGE + part * 64 + spot % 64
            usable = spot < length
            for h in range(4):
                span = pl.ds(h * 128, 128)
                scores = lax.dot_general(query_ref[span, :], keys, BY_ROW, preferred_element_type=F32)
                scores = jnp.where(usable, scores * SCALE2, MASKED_SCORE)
                old = max_ref[span, 0:1]
                new = jnp.maximum(old, jnp.max(scores, axis=1, keepdims=True))
                weights = jnp.where(usable, jnp.exp2(scores - new), 0.0)
                fade = jnp.exp2(old - new)
                total = total_ref[span, 0:1] * fade + jnp.sum(weights, axis=1, keepdims=True)
                acc_ref[span, :] = acc_ref[span, :] * fade + jnp.dot(
                    weights.astype(BF), values, preferred_element_type=F32
                )
                max_ref[span, :] = jnp.broadcast_to(new, (128, 128))
                total_ref[span, :] = jnp.broadcast_to(total, (128, 128))
            return 0

        lax.fori_loop(0, steps, body, 0)
        put(k * 128, 128)

    def branch_body(b, _):
        branch = branch_id_ref[b]
        length = branch_len_ref[branch]
        picked = pick(1, b * 32, 32)
        stacked = jnp.concatenate([picked[:, h * 128 : (h + 1) * 128] for h in range(4)], axis=0)
        ids = [branch_pages_ref[branch, j] for j in range(4)]
        keys = jnp.concatenate([pages_ref[0, page] for page in ids], axis=0)
        values = jnp.concatenate([pages_ref[1, page] for page in ids], axis=0)
        spot = lax.broadcasted_iota(jnp.int32, (1, 256), 1)
        spot = (spot // 64) * PAGE + part * 64 + spot % 64
        usable = spot < length
        scores = lax.dot_general(stacked, keys, BY_ROW, preferred_element_type=F32)
        scores = jnp.where(usable, scores * SCALE2, MASKED_SCORE)
        top = jnp.max(scores, axis=1, keepdims=True)
        weights = jnp.where(usable, jnp.exp2(scores - top), 0.0)
        total = jnp.sum(weights, axis=1, keepdims=True)
        acc = jnp.dot(weights.astype(BF), values, preferred_element_type=F32)
        row = pl.multiple_of(256 + b * 32, 32)
        stats = jnp.zeros((32, 128), F32)
        for h in range(4):
            node_sum_ref[pl.ds(row, 32), h * 128 : (h + 1) * 128] = acc[h * 32 : (h + 1) * 32].astype(BF)
            stats = jnp.where(lane == h, top[h * 32 : (h + 1) * 32], stats)
            stats = jnp.where(lane == 4 + h, total[h * 32 : (h + 1) * 32], stats)
        node_stat_ref[pl.ds(row, 32), :] = stats
        return 0

    lax.fori_loop(0, BR_DEV, branch_body, 0)

    def spread_body(block, _):
        parts = []
        wanted = lax.broadcasted_iota(jnp.int32, (ROWS, 256), 1)
        for kind in range(2):
            code = code_col_ref[block, :, kind : kind + 1]
            chosen = wanted == code
            rows = slice(kind * 256, kind * 256 + 256)
            sums = jnp.dot(chosen.astype(BF), node_sum_ref[rows, :], preferred_element_type=F32)
            stats = jnp.dot(
                chosen.astype(F32),
                node_stat_ref[rows, :],
                preferred_element_type=F32,
                precision=lax.Precision.HIGHEST,
            )
            stats = jnp.where((lane < 4) & (code < 0), MASKED_SCORE, stats)
            parts.append((sums, stats))
        merged, stats = merge_blocks(parts[0], parts[1], 4)
        sum_ref[block] = merged.astype(BF)
        stat_ref[block] = stats
        return 0

    lax.fori_loop(0, 8, spread_body, 0)


def merge_blocks(one, two, heads):
    sums_one, stats_one = one
    sums_two, stats_two = two
    lane = lax.broadcasted_iota(jnp.int32, (1, 128), 1)
    pieces = []
    stats = jnp.zeros_like(stats_one)
    for h in range(heads):
        span = slice(h * 128, (h + 1) * 128)
        top_one, top_two = stats_one[:, h : h + 1], stats_two[:, h : h + 1]
        top = jnp.maximum(top_one, top_two)
        factor_one, factor_two = jnp.exp2(top_one - top), jnp.exp2(top_two - top)
        pieces.append(
            sums_one[:, span].astype(F32) * factor_one + sums_two[:, span].astype(F32) * factor_two
        )
        total = stats_one[:, 4 + h : 5 + h] * factor_one + stats_two[:, 4 + h : 5 + h] * factor_two
        stats = jnp.where(lane == h, top, stats)
        stats = jnp.where(lane == 4 + h, total, stats)
    return jnp.concatenate(pieces, axis=1), stats


def node_partials(local_roots, local_branches, tables, part, all_queries, pages, codes):
    return pl.pallas_call(
        node_kernel,
        out_shape=(
            jax.ShapeDtypeStruct((8, ROWS, 512), BF),
            jax.ShapeDtypeStruct((8, ROWS, 128), F32),
        ),
        in_specs=[pl.BlockSpec(memory_space=pltpu.SMEM)] * 7 + [pl.BlockSpec(memory_space=pltpu.VMEM)] * 4,
        out_specs=(pl.BlockSpec(memory_space=pltpu.VMEM),) * 2,
        scratch_shapes=[
            pltpu.VMEM((512, 128), BF),
            pltpu.VMEM((512, 128), F32),
            pltpu.VMEM((512, 128), F32),
            pltpu.VMEM((512, 128), F32),
            pltpu.VMEM((512, 512), BF),
            pltpu.VMEM((512, 128), F32),
        ],
        compiler_params=pltpu.CompilerParams(vmem_limit_bytes=40 * 2**20),
        name="node_partials",
    )(local_roots, local_branches, *tables, part, all_queries, pages, codes, codes.T.reshape(8, ROWS, 2))


def attend_kernel(
    sum_ref, stat_ref, query_ref, own_query_ref, leaf_ref, leaf_len_ref, fresh_ref, weight_ref, residual_ref,
    hidden_ref, narrow_ref,
    their_sum, their_stat, run_sum, run_stat, land_sum, land_stat, last_sum, last_stat,
    leaf_sum, leaf_stat, side_sum, side_stat, give_sum,
    proj_ref, half1, full1, half2, full2, send_sem, recv_sem,
):
    at = place()
    sems = (send_sem, recv_sem)
    sibling = device_of(at, c=1 - at["c"])
    beside = {**at, "z": at["z"] + 1 - 2 * (at["z"] % 2)}
    right, left = step_along(at, "x", 1), step_along(at, "x", 3)
    greet(all_peers(at))
    x, core = at["x"], at["c"]
    part = at["z"] % 2
    started = []

    def send(src, dst, key, device):
        copy = remote(src, dst, sems, key, device)
        copy.start()
        started.append(copy)

    def arrive(ref, key):
        remote(ref, ref, sems, key, sibling).wait_recv()

    send(sum_ref.at[:, 1 - core], their_sum, 0, sibling)
    send(stat_ref.at[:, 1 - core], their_stat, 1, sibling)
    lane = lax.broadcasted_iota(jnp.int32, (1, 128), 1)

    def leaf_body(i, _):
        base = pl.multiple_of(i * 8, 8)
        span = pl.ds(base, 8)
        heads = [query_ref[span, h * 128 : (h + 1) * 128] for h in range(4)]
        stacked = jnp.concatenate(heads, axis=0)
        keys = leaf_ref[0, span].reshape(512, 128)
        values = leaf_ref[1, span].reshape(512, 128)
        scores = lax.dot_general(
            stacked.astype(BF), keys, BY_ROW, preferred_element_type=F32
        )
        row = lax.broadcasted_iota(jnp.int32, (32, 512), 0) % 8
        col = lax.broadcasted_iota(jnp.int32, (32, 512), 1)
        lengths = jnp.concatenate([leaf_len_ref[span, 0:1]] * 4, axis=0)
        usable = (row == col // 64) & (part * 64 + col % 64 < lengths)
        scores = jnp.where(usable, scores * SCALE2, MASKED_SCORE)
        top = jnp.max(scores, axis=1, keepdims=True)
        weights = jnp.where(usable, jnp.exp2(scores - top), 0.0)
        total = jnp.sum(weights, axis=1, keepdims=True)
        acc = jnp.dot(weights.astype(BF), values, preferred_element_type=F32)
        stats = jnp.zeros((8, 128), F32)
        for h in range(4):
            leaf_sum[span, h * 128 : (h + 1) * 128] = acc[h * 8 : (h + 1) * 8]
            stats = jnp.where(lane == h, top[h * 8 : (h + 1) * 8], stats)
            stats = jnp.where(lane == 4 + h, total[h * 8 : (h + 1) * 8], stats)
        leaf_stat[span, :] = stats
        return 0

    lax.fori_loop(0, 16, leaf_body, 0)
    arrive(their_sum, 0)
    arrive(their_stat, 1)

    def cross_body(i, _):
        value = lax.rem(x + 2 + i, 4)
        merged, stats = merge_blocks(
            (sum_ref[value, core], stat_ref[value, core]), (their_sum[value], their_stat[value]), 4
        )
        run_sum[value] = merged.astype(BF)
        run_stat[value] = stats
        return 0

    def cross_merge(by):
        cross_body(by - 2, 0)

    low, high, far = (x + 3) % 4, (x + 1) % 4, (x + 2) % 4
    upper, lower = pl.ds(0, 64), pl.ds(64, 64)
    cross_merge(2)
    for key, rows, device in ((2, upper, right), (4, lower, left)):
        send(run_sum.at[far, rows], land_sum.at[rows], key, device)
        send(run_stat.at[far, rows], land_stat.at[rows], key + 1, device)
    cross_merge(3)
    cross_merge(4)
    cross_merge(5)
    for key, rows, value, device, side in ((2, upper, high, right, 0), (4, lower, low, left, 1)):
        arrive(land_sum.at[rows], key)
        arrive(land_stat.at[rows], key + 1)
        merged, stats = merge_blocks(
            (run_sum[value, rows], run_stat[value, rows]), (land_sum[rows], land_stat[rows]), 4
        )
        run_sum[value, rows] = merged.astype(BF)
        run_stat[value, rows] = stats
        send(run_sum.at[value], last_sum.at[side], key + 4, device)
        send(run_stat.at[value], last_stat.at[side], key + 5, device)
    sums, stats = merge_blocks((run_sum[x], run_stat[x]), (leaf_sum[...], leaf_stat[...]), 4)
    for side, key in ((0, 6), (1, 8)):
        arrive(last_sum.at[side], key)
        arrive(last_stat.at[side], key + 1)
        sums, stats = merge_blocks((sums, stats), (last_sum[side], last_stat[side]), 4)
    first = part == 0
    give_sum[...] = jnp.where(first, sums[:, 256:], sums[:, :256]).astype(BF)
    leaf_stat[...] = stats
    send(give_sum, side_sum, 10, device_of(beside))
    send(leaf_stat, side_stat, 11, device_of(beside))
    kept = jnp.where(first, sums[:, :256], sums[:, 256:])
    fresh_key = fresh_ref[0].astype(F32)
    fresh_value = fresh_ref[1].astype(F32)
    own_scores = [
        jnp.sum(own_query_ref[:, h * 128 : (h + 1) * 128].astype(F32) * fresh_key, axis=1, keepdims=True)
        * SCALE2
        for h in range(2)
    ]
    arrive(side_sum, 10)
    arrive(side_stat, 11)
    theirs = side_stat[...]
    pieces = []
    for h in range(2):
        span = slice(h * 128, (h + 1) * 128)

        def column(from_stats, offset):
            return jnp.where(
                first,
                from_stats[:, offset + h : offset + h + 1],
                from_stats[:, offset + 2 + h : offset + 3 + h],
            )

        top_one, top_two = column(stats, 0), column(theirs, 0)
        top = jnp.maximum(jnp.maximum(top_one, top_two), own_scores[h])
        factor_one, factor_two = jnp.exp2(top_one - top), jnp.exp2(top_two - top)
        factor_own = jnp.exp2(own_scores[h] - top)
        weighted = (
            kept[:, span] * factor_one
            + side_sum[:, span].astype(F32) * factor_two
            + factor_own * fresh_value
        )
        total = column(stats, 4) * factor_one + column(theirs, 4) * factor_two + factor_own
        pieces.append((weighted / total).astype(BF))
    attended = jnp.concatenate(pieces, axis=1)
    for i in range(16):
        product = jnp.dot(
            attended, weight_ref[:, i * 256 : (i + 1) * 256], preferred_element_type=F32
        ).astype(BF)
        for half in range(2):
            proj_ref[i // 4, i % 4, half] = product[:, half * 128 : (half + 1) * 128]

    def finish(row, rows, half, total):
        cols = pl.ds(half * 128, 128)
        total += residual_ref[pl.ds(row, rows), cols].astype(F32)
        hidden_ref[pl.ds(row, rows), cols] = total
        narrow_ref[half, pl.ds(row, rows), :] = total.astype(BF)

    ring_reduce(
        at, proj_ref, ("y", "z"), (("y", "z"), ("z", "y")), ((0, 64), (64, 64)),
        (half1, half2), (full1, full2), send, arrive, 12, finish,
    )
    for copy in started:
        copy.wait_send()


def attend(sums, stats, queries, own_queries, leaf, leaf_len, fresh, out_weight, residual):
    return pl.pallas_call(
        attend_kernel,
        out_shape=(
            jax.ShapeDtypeStruct((ROWS, 256), F32),
            jax.ShapeDtypeStruct((2, ROWS, 128), BF),
        ),
        in_specs=[pl.BlockSpec(memory_space=pltpu.VMEM)] * 9,
        out_specs=(pl.BlockSpec(memory_space=pltpu.VMEM),) * 2,
        scratch_shapes=[
            pltpu.VMEM((4, ROWS, 512), BF),
            pltpu.VMEM((4, ROWS, 128), F32),
            pltpu.VMEM((4, ROWS, 512), BF),
            pltpu.VMEM((4, ROWS, 128), F32),
            pltpu.VMEM((ROWS, 512), BF),
            pltpu.VMEM((ROWS, 128), F32),
            pltpu.VMEM((2, ROWS, 512), BF),
            pltpu.VMEM((2, ROWS, 128), F32),
            pltpu.VMEM((ROWS, 512), F32),
            pltpu.VMEM((ROWS, 128), F32),
            pltpu.VMEM((ROWS, 256), BF),
            pltpu.VMEM((ROWS, 128), F32),
            pltpu.VMEM((ROWS, 256), BF),
            pltpu.VMEM((4, 4, 2, ROWS, 128), BF),
            pltpu.VMEM((2, 4, ROWS, 128), BF),
            pltpu.VMEM((2, 4, 2, ROWS, 128), BF),
            pltpu.VMEM((2, ROWS, 128), BF),
            pltpu.VMEM((2, 2, ROWS, 128), BF),
            pltpu.SemaphoreType.DMA((28,)),
            pltpu.SemaphoreType.DMA((28,)),
        ],
        compiler_params=pltpu.CompilerParams(
            collective_id=4, has_side_effects=True, vmem_limit_bytes=48 * 2**20
        ),
        name="attend",
    )(sums, stats, queries, own_queries, leaf, leaf_len, fresh, out_weight, residual)


def ring_reduce(at, sum_ref, dims, orders, part_rows, halves, fulls, send, arrive, base, finish):
    phases = len(dims)
    both = slice(None)

    def view(part, phase, value, half):
        index = dict(at)
        for axis in orders[part][phase + 1 :]:
            index[axis] = slice(None)
        index[orders[part][phase]] = value
        row, rows = part_rows[part]
        return tuple(index[axis] for axis in dims) + (half, pl.ds(row, rows), slice(None))

    def landing(part, phase, direction, half):
        row, rows = part_rows[part]
        free = (slice(None),) * (phases - 1 - phase)
        if half is None:
            return (halves[phase], (direction,) + free + (pl.ds(row, rows), slice(None)))
        return (fulls[phase], (direction,) + free + (half, pl.ds(row, rows), slice(None)))

    def accumulate(target, others):
        total = sum_ref[target].astype(F32)
        for ref, index in others:
            total += ref[index].astype(F32)
        return total

    parts = range(len(orders))
    for phase in range(phases):
        keys = [base + (part * phases + phase) * 4 for part in parts]
        for part in parts:
            axis = orders[part][phase]
            for direction, by in ((0, 1), (1, 3)):
                ref, index = landing(part, phase, direction, None)
                send(
                    sum_ref.at[view(part, phase, (at[axis] + 2) % 4, direction)],
                    ref.at[index],
                    keys[part] + direction,
                    step_along(at, axis, by),
                )
        for part in parts:
            axis = orders[part][phase]
            for direction, by in ((0, 1), (1, 3)):
                ref, index = landing(part, phase, direction, None)
                arrive(ref.at[index], keys[part] + direction)
                target = view(part, phase, (at[axis] + by) % 4, direction)
                sum_ref[target] = accumulate(target, [(ref, index)]).astype(BF)
            for direction, by in ((0, 1), (1, 3)):
                ref, index = landing(part, phase, direction, both)
                send(
                    sum_ref.at[view(part, phase, (at[axis] + by) % 4, both)],
                    ref.at[index],
                    keys[part] + 2 + direction,
                    step_along(at, axis, by),
                )
        for part in parts:
            axis = orders[part][phase]
            for direction in range(2):
                ref, index = landing(part, phase, direction, both)
                arrive(ref.at[index], keys[part] + 2 + direction)
            for half in range(2):
                target = view(part, phase, at[axis], half)
                total = accumulate(
                    target, [landing(part, phase, direction, half) for direction in range(2)]
                )
                if phase < phases - 1:
                    sum_ref[target] = total.astype(BF)
                else:
                    row, rows = part_rows[part]
                    finish(row, rows, half, total)


def owned_nodes(owner, dp_index, count):
    node = jnp.arange(owner.shape[0])
    owned = owner == dp_index
    rank = jnp.sum((owned[None, :] & (node[None, :] < node[:, None])).astype(jnp.int32), axis=1)
    chosen = owned[None, :] & (rank[None, :] == jnp.arange(count)[:, None])
    return jnp.sum(jnp.where(chosen, node[None, :], 0), axis=1), jnp.where(owned, rank, -1)


def slot_codes(slot_request, request_branch, branch_parent, root_place, branch_place):
    slots = slot_request.shape[0]
    slot = jnp.arange(slots)
    slot_branch = jnp.sum(
        jnp.where(slot_request[:, None] == slot[None, :], request_branch[None, :], 0), axis=1
    )
    rank = jnp.sum(
        ((slot_branch[:, None] == slot_branch[None, :]) & (slot[None, :] < slot[:, None])).astype(jnp.int32),
        axis=1,
    )
    branch = jnp.arange(branch_parent.shape[0])
    kid = jnp.sum(
        ((branch_parent[:, None] == branch_parent[None, :]) & (branch[None, :] < branch[:, None])).astype(
            jnp.int32
        ),
        axis=1,
    )
    parent_place = jnp.sum(
        jnp.where(branch_parent[:, None] == jnp.arange(root_place.shape[0])[None, :], root_place[None, :], 0),
        axis=1,
    )
    root_base = jnp.where(parent_place >= 0, parent_place * ROWS + kid * BR_CAP, -4096)
    branch_base = jnp.where(branch_place >= 0, branch_place * BR_CAP, -4096)
    mine = slot_branch[None, :, None] == branch[None, None, :]
    bases = jnp.sum(jnp.where(mine, jnp.stack([root_base, branch_base])[:, None, :], 0), axis=2)
    return jnp.maximum(bases + rank[None, :], -1)


def expert_phase(hidden, narrow, all_routes, norm_gain, router, expert_in, expert_out):
    dp = lax.axis_index("dp")
    names = jnp.arange(EXPERTS)
    hit = jnp.any(all_routes[:, :, :, None] == names, axis=2)
    before = jnp.tril(jnp.ones((ROWS, ROWS), F32), -1)
    rank = jnp.einsum(
        "rq,bqe->ebr", before.astype(BF), hit.astype(BF), preferred_element_type=F32
    ).astype(jnp.int32)
    rank = jnp.where(hit.transpose(2, 0, 1), rank, -1)
    mine = lax.dynamic_index_in_dim(rank, dp, 0, False)
    other = jnp.sum(all_routes, axis=2) - dp
    packed = mine[:, None, :] == jnp.arange(E_CAP)[None, :, None]
    other = jnp.sum(jnp.where(packed, other[:, None, :], 0), axis=2).reshape(-1, 1)
    core = dp % 2
    ours = lax.dynamic_index_in_dim(rank.reshape(EXPERTS, 4, 2, ROWS), core, 2, False)
    pair = jnp.stack(
        [
            lax.dynamic_index_in_dim(ours, dp, 0, False),
            lax.dynamic_index_in_dim(ours, dp + 1 - 2 * core, 0, False),
        ],
        axis=1,
    )
    buf = gather_rows(narrow)
    partial = run_experts(
        buf,
        mine,
        other,
        dp.reshape(1, 1).astype(jnp.int32),
        norm_gain[None, :],
        router,
        expert_in[0],
        expert_out[0],
    )
    return return_rows(partial.reshape(4, 2, 16, 2, E_CAP, 128), pair[..., None], hidden)


def shards(
    queries,
    new_kv,
    residual,
    out_weight,
    norm_gain,
    router,
    expert_in,
    expert_out,
    node_cache,
    leaf_cache,
    slot_request,
    request_branch,
    branch_parent,
    root_owner,
    branch_owner,
    root_pages,
    branch_pages,
    root_len,
    branch_len,
    leaf_len,
    routes,
):
    dp = lax.axis_index("dp")
    mp = lax.axis_index("mp")
    all_routes = lax.all_gather(routes, "dp", axis=0)
    local_roots, root_place = owned_nodes(root_owner, dp, ROOT_DEV)
    local_branches, branch_place = owned_nodes(branch_owner, dp, BR_DEV)
    codes = slot_codes(slot_request, request_branch, branch_parent, root_place, branch_place)
    all_queries = gather_queries(queries).reshape(8 * ROWS, 512)
    sums, stats = node_partials(
        local_roots,
        local_branches,
        (root_pages, branch_pages, root_len, branch_len),
        (mp % 2).reshape(1).astype(jnp.int32),
        all_queries,
        node_cache[:, :, 0],
        codes,
    )
    hidden, narrow = attend(
        sums.reshape(4, 2, ROWS, 512),
        stats.reshape(4, 2, ROWS, 128),
        lax.dynamic_slice_in_dim(queries, (mp // 2) * 512, 512, 1).astype(F32),
        lax.dynamic_slice_in_dim(queries, mp * 256, 256, 1),
        leaf_cache[:, :, 0],
        leaf_len[:, None],
        lax.dynamic_slice_in_dim(new_kv, (mp // 2) * 128, 128, 2),
        out_weight,
        residual,
    )
    return expert_phase(hidden, narrow, all_routes, norm_gain, router, expert_in, expert_out)


def solution(mesh):
    placed = (
        P("dp", None),
        P(None, "dp", None),
        P("dp", "mp"),
        P("mp", None),
        P(),
        P(),
        P("dp", None, "mp", None),
        P("dp", "mp", None),
        P(None, "dp", "mp", None, None),
        P(None, "dp", "mp", None, None),
        P(),
        P(),
        P(),
        P(),
        P(),
        P(),
        P(),
        P(),
        P(),
        P("dp"),
        P("dp", None),
    )
    return jax.shard_map(
        shards, mesh=mesh, in_specs=placed, out_specs=P("dp", "mp"), check_vma=False
    )
```

```python
import jax
import jax.numpy as jnp
from jax import lax
from jax.experimental import pallas as pl
from jax.experimental.pallas import tpu as pltpu
from jax.sharding import PartitionSpec as P

EXPERTS = 8
PAGE = 128
ROOT_DEV = 2
BR_DEV = 8
BR_CAP = 32
E_CAP = 64

MASKED_SCORE = -1e30
NORM_EPS = 1e-05

BF = jnp.bfloat16
F32 = jnp.float32
MESH = pl.DeviceIdType.MESH
ROWS = 128
PART_ROWS = ((0, 48), (48, 48), (96, 32))
AXES = ("x", "y", "z")
ORDERS = tuple(AXES[part:] + AXES[:part] for part in range(3))


def place():
    dp = lax.axis_index("dp")
    mp = lax.axis_index("mp")
    return {"x": dp // 2, "c": dp % 2, "y": mp // 4, "z": mp % 4}


def device_of(at, **moved):
    at = {**at, **moved}
    return (at["x"] * 2 + at["c"], at["y"] * 4 + at["z"])


def step_along(at, axis, by):
    return device_of(at, **{axis: (at[axis] + by) % 4})


def greet(peers):
    barrier = pltpu.get_barrier_semaphore()
    for peer in peers:
        pl.semaphore_signal(barrier, inc=1, device_id=peer, device_id_type=MESH)
    pl.semaphore_wait(barrier, len(peers))


def remote(src, dst, sems, key, device):
    return pltpu.make_async_remote_copy(
        src_ref=src,
        dst_ref=dst,
        send_sem=sems[0].at[key],
        recv_sem=sems[1].at[key],
        device_id=device,
        device_id_type=MESH,
    )


def all_peers(at):
    return [step_along(at, axis, by) for axis in AXES for by in (1, 2, 3)] + [
        device_of(at, c=1 - at["c"])
    ]


class Link:
    def __init__(self, at, sems):
        self.sems = sems
        self.sibling = device_of(at, c=1 - at["c"])
        self.started = []

    def send(self, src, dst, key, device):
        copy = remote(src, dst, self.sems, key, device)
        copy.start()
        self.started.append(copy)

    def arrive(self, ref, key):
        remote(ref, ref, self.sems, key, self.sibling).wait_recv()

    def finish(self):
        for copy in self.started:
            copy.wait_send()


def gather_all(at, link, own_ref, buf_ref, local_sem, base):
    both = slice(None)
    core = at["c"]

    def slab(part, phase, value, half, plane):
        index = {"x": at["x"], "y": at["y"], "z": at["z"]}
        for axis in ORDERS[part][:phase]:
            index[axis] = slice(None)
        index[ORDERS[part][phase]] = value
        row, rows = PART_ROWS[part]
        return buf_ref.at[index["x"], plane, index["y"], index["z"], half, pl.ds(row, rows), :]

    local = pltpu.make_async_copy(own_ref, buf_ref.at[at["x"], core, at["y"], at["z"]], local_sem)
    local.start()
    for phase in range(2):
        for part in range(3):
            axis = ORDERS[part][phase]
            ref = slab(part, phase, at[axis], both, core)
            src = ref
            if phase == 0:
                row, rows = PART_ROWS[part]
                src = own_ref.at[:, pl.ds(row, rows), :]
            for by in (2, 1, 3):
                link.send(src, ref, base + (part * 2 + phase) * 3 + by - 1, step_along(at, axis, by))
        if phase == 0:
            local.wait()
        for part in range(3):
            axis = ORDERS[part][phase]
            for by in (1, 3, 2):
                ref = slab(part, phase, (at[axis] - by) % 4, both, core)
                link.arrive(ref, base + (part * 2 + phase) * 3 + by - 1)
    base += 18
    for part in range(3):
        axis = ORDERS[part][2]
        key = base + part * 8
        ref = slab(part, 2, at[axis], both, core)
        link.send(ref, ref, key, step_along(at, axis, 1))
        link.send(ref, ref, key + 1, step_along(at, axis, 3))
        link.send(ref, ref, key + 4, link.sibling)
    for part in range(3):
        axis = ORDERS[part][2]
        key = base + part * 8
        for side, by in ((0, 3), (1, 1)):
            value = (at[axis] + by) % 4
            ref = slab(part, 2, value, both, core)
            link.arrive(ref, key + side)
            half = slab(part, 2, value, side, core)
            link.send(half, half, key + 2 + side, step_along(at, axis, 1 + 2 * side))
            link.send(ref, ref, key + 5 + side, link.sibling)
    for part in range(3):
        axis = ORDERS[part][2]
        key = base + part * 8
        far = (at[axis] + 2) % 4
        for side in range(2):
            link.arrive(slab(part, 2, far, side, core), key + 2 + side)
        ref = slab(part, 2, far, both, core)
        link.send(ref, ref, key + 7, link.sibling)

    def others():
        for part in range(3):
            v = at[ORDERS[part][2]]
            for i, by in enumerate((0, 3, 1, 2)):
                link.arrive(slab(part, 2, (v + by) % 4, both, 1 - core), base + part * 8 + 4 + i)

    return others


GATHER_KEYS = 18 + 24


def ring_reduce(at, link, sum_ref, dims, orders, part_rows, relay, lands, base, finish):
    phases = len(dims)
    both = slice(None)
    parts = range(len(orders))

    def view(part, phase, value, half):
        index = dict(at)
        for axis in orders[part][phase + 1 :]:
            index[axis] = slice(None)
        index[orders[part][phase]] = value
        row, rows = part_rows[part]
        return tuple(index[axis] for axis in dims) + (half, pl.ds(row, rows), slice(None))

    def spot(part, phase, slot, *half):
        row, rows = part_rows[part]
        return (slot,) + (slice(None),) * (phases - 1 - phase) + half + (pl.ds(row, rows), slice(None))

    def accumulate(target, others):
        total = sum_ref[target].astype(F32)
        for ref, index in others:
            total += ref[index].astype(F32)
        return total

    for phase in range(phases):
        keys = [base + (part * phases + phase) * 4 for part in parts]
        if phase < relay:
            halves, fulls = lands[phase]
            for part in parts:
                axis = orders[part][phase]
                for side, by in ((0, 1), (1, 3)):
                    link.send(
                        sum_ref.at[view(part, phase, (at[axis] + 2) % 4, side)],
                        halves.at[spot(part, phase, side)],
                        keys[part] + side,
                        step_along(at, axis, by),
                    )
            for part in parts:
                axis = orders[part][phase]
                for side, by in ((0, 1), (1, 3)):
                    index = spot(part, phase, side)
                    link.arrive(halves.at[index], keys[part] + side)
                    target = view(part, phase, (at[axis] + by) % 4, side)
                    sum_ref[target] = accumulate(target, [(halves, index)]).astype(BF)
                    link.send(
                        sum_ref.at[view(part, phase, (at[axis] + by) % 4, both)],
                        fulls.at[spot(part, phase, side, both)],
                        keys[part] + 2 + side,
                        step_along(at, axis, by),
                    )
            slots, first = 2, 2
        else:
            fulls = lands[phase]
            for part in parts:
                axis = orders[part][phase]
                for by in (2, 1, 3):
                    link.send(
                        sum_ref.at[view(part, phase, (at[axis] + by) % 4, both)],
                        fulls.at[spot(part, phase, by - 1, both)],
                        keys[part] + by - 1,
                        step_along(at, axis, by),
                    )
            slots, first = 3, 0
        for part in parts:
            axis = orders[part][phase]
            for slot in range(slots):
                link.arrive(fulls.at[spot(part, phase, slot, both)], keys[part] + first + slot)
            for half in range(2):
                target = view(part, phase, at[axis], half)
                total = accumulate(target, [(fulls, spot(part, phase, slot, half)) for slot in range(slots)])
                if phase < phases - 1:
                    sum_ref[target] = total.astype(BF)
                else:
                    finish(*part_rows[part], half, total)


def expert_kernel(
    own_ref, kept_ref, pick_ref, other_ref, spread_ref, gain_ref, router_ref, up_hbm, down_hbm,
    out_ref,
    buf_ref, rows_ref, gate_ref, up_ref, down_ref, act_ref, give_ref, theirs_ref, sum_ref,
    half0, full0, full1, full2,
    local_sem, up_sem, down_sem, send_sem, recv_sem,
):
    at = place()
    loads = [pltpu.make_async_copy(up_hbm, up_ref, up_sem), pltpu.make_async_copy(down_hbm, down_ref, down_sem)]
    for load in loads:
        load.start()
    greet(all_peers(at))
    link = Link(at, (send_sem, recv_sem))
    core = at["c"]
    mine = lax.axis_index("dp")
    others = gather_all(at, link, own_ref, buf_ref, local_sem, 0)

    def compact(plane):
        base = pl.multiple_of(plane * 256, 256)
        wanted = lax.broadcasted_iota(jnp.int32, (128, 256), 0)
        picks = [(wanted == pick_ref[plane, pair]).astype(BF) for pair in range(2)]

        def fill(y, squares):
            for z in range(4):
                pieces = []
                for pair in range(2):
                    whole = jnp.concatenate(
                        [
                            jnp.concatenate([buf_ref[2 * pair + k, plane, y, z, h] for h in range(2)], axis=1)
                            for k in range(2)
                        ],
                        axis=0,
                    )
                    pieces.append(jnp.dot(picks[pair], whole, preferred_element_type=F32))
                piece = jnp.concatenate(pieces, axis=0)
                cols = pl.ds(pl.multiple_of((y * 4 + z) * 256, 256), 256)
                rows_ref[pl.ds(base, 256), cols] = piece.astype(BF)
                piece = piece * piece
                squares += piece[:, :128] + piece[:, 128:]
            return squares

        squares = lax.fori_loop(0, 4, fill, jnp.zeros((256, 128), F32))
        scale = lax.rsqrt(jnp.sum(squares, axis=1, keepdims=True) / 4096.0 + NORM_EPS)

        def norm(y, _):
            for z in range(4):
                cols = pl.ds(pl.multiple_of((y * 4 + z) * 256, 256), 256)
                normed = rows_ref[pl.ds(base, 256), cols].astype(F32) * scale * gain_ref[y * 4 + z]
                rows_ref[pl.ds(base, 256), cols] = normed.astype(BF)
            return 0

        lax.fori_loop(0, 4, norm, 0)
        logits = jnp.dot(rows_ref[pl.ds(base, 256), :], router_ref[...], preferred_element_type=F32)
        lane = lax.broadcasted_iota(jnp.int32, logits.shape, 1)
        here = jnp.sum(jnp.where(lane == mine, logits, 0.0), axis=1, keepdims=True)
        there = jnp.sum(
            jnp.where(lane == other_ref[pl.ds(base, 256), 0:1], logits, 0.0), axis=1, keepdims=True
        )
        most = jnp.maximum(here, there)
        here = jnp.exp(here - most)
        there = jnp.exp(there - most)
        gate_ref[pl.ds(base, 256), :] = jnp.broadcast_to(here / (here + there), (256, 128))

    compact(core)
    others()
    compact(1 - core)
    for load in loads:
        load.wait()

    for j in range(2):
        span = slice(j * 256, (j + 1) * 256)
        gate, up = [
            lax.dot_general(rows_ref[...], up_ref[k, span, :], BY_ROW, preferred_element_type=F32)
            for k in range(2)
        ]
        act_ref[:, span] = (gate / (1.0 + jnp.exp(-gate)) * up).astype(BF)

    def project(plane, i):
        base = pl.multiple_of(plane * 256, 256)
        cols = pl.ds(pl.multiple_of(i * 256, 256), 256)
        product = jnp.dot(act_ref[pl.ds(base, 256), :], down_ref[:, cols], preferred_element_type=F32)
        return (product * gate_ref[pl.ds(base, 256), 0:1]).astype(BF)

    for group in range(4):

        def hand(k, _):
            i = group * 4 + k
            give_ref[i] = project(1 - core, i)
            return 0

        lax.fori_loop(0, 4, hand, 0)
        link.send(
            give_ref.at[pl.ds(group * 4, 4)], theirs_ref.at[pl.ds(group * 4, 4)], GATHER_KEYS + group, link.sibling
        )
    spreads = []
    for pair in range(2):
        lane = lax.broadcasted_iota(jnp.int32, (256, 128), 1)
        spreads.append(
            jnp.concatenate([(spread_ref[pair, :, k : k + 1] == lane).astype(BF) for k in range(2)], axis=1)
        )
    for group in range(4):
        link.arrive(theirs_ref.at[pl.ds(group * 4, 4)], GATHER_KEYS + group)

        def merge(k, _):
            i = group * 4 + k
            ours = project(core, i)
            for pair in range(2):
                rows = slice(pair * 128, (pair + 1) * 128)
                stacked = jnp.concatenate([ours[rows], theirs_ref[i, rows]], axis=0)
                spread = jnp.dot(spreads[pair], stacked, preferred_element_type=F32).astype(BF)
                for x in range(2):
                    for half in range(2):
                        sum_ref[2 * pair + x, group, k, half] = spread[
                            x * 128 : (x + 1) * 128, half * 128 : (half + 1) * 128
                        ]
            return 0

        lax.fori_loop(0, 4, merge, 0)

    def finish(row, rows, half, total):
        spot = (pl.ds(row, rows), pl.ds(half * 128, 128))
        out_ref[spot] = (kept_ref[spot] + total).astype(BF)

    ring_reduce(
        at, link, sum_ref, AXES, ORDERS, PART_ROWS, 1, ((half0, full0), full1, full2), GATHER_KEYS + 4, finish
    )
    link.finish()


def run_experts(own, kept, pick, other, spread, gain, router, expert_in, expert_out):
    keys = GATHER_KEYS + 4 + 36
    vmem, hbm = pl.BlockSpec(memory_space=pltpu.VMEM), pl.BlockSpec(memory_space=pl.ANY)
    return pl.pallas_call(
        expert_kernel,
        out_shape=jax.ShapeDtypeStruct((ROWS, 256), BF),
        in_specs=[vmem] * 7 + [hbm] * 2,
        out_specs=vmem,
        scratch_shapes=[
            pltpu.VMEM((4, 2, 4, 4, 2, ROWS, 128), BF),
            pltpu.VMEM((512, 4096), BF),
            pltpu.VMEM((512, 128), F32),
            pltpu.VMEM(expert_in.shape, BF),
            pltpu.VMEM(expert_out.shape, BF),
            pltpu.VMEM((512, 512), BF),
            pltpu.VMEM((16, 256, 256), BF),
            pltpu.VMEM((16, 256, 256), BF),
            pltpu.VMEM((4, 4, 4, 2, ROWS, 128), BF),
            pltpu.VMEM((2, 4, 4, ROWS, 128), BF),
            pltpu.VMEM((2, 4, 4, 2, ROWS, 128), BF),
            pltpu.VMEM((3, 4, 2, ROWS, 128), BF),
            pltpu.VMEM((3, 2, ROWS, 128), BF),
            pltpu.SemaphoreType.DMA,
            pltpu.SemaphoreType.DMA,
            pltpu.SemaphoreType.DMA,
            pltpu.SemaphoreType.DMA((keys,)),
            pltpu.SemaphoreType.DMA((keys,)),
        ],
        compiler_params=pltpu.CompilerParams(
            collective_id=1, has_side_effects=True, vmem_limit_bytes=60 * 2**20
        ),
        name="run_experts",
    )(own, kept, pick, other, spread, gain, router, expert_in, expert_out)


LOG2E = 1.4426950408889634


def query_kernel(queries_ref, routes_ref, all_ref, all_routes_ref, local_sem, route_sem, send_sem, recv_sem):
    at = place()
    link = Link(at, (send_sem, recv_sem))
    sibling = link.sibling
    right, left = step_along(at, "x", 1), step_along(at, "x", 3)
    x, core = at["x"], at["c"]
    peers = [(by, device_of(at, x=(x + by // 2) % 4, c=(core + by) % 2)) for by in range(1, 8)]
    greet([device for _, device in peers])
    kv_head = lax.axis_index("mp") // 2
    own = queries_ref.at[:, pl.ds(pl.multiple_of(kv_head * 512, 512), 512)]
    mine = all_ref.at[x, core]
    link.send(own, mine, 0, right)
    link.send(own, mine, 1, left)
    link.send(own, mine, 4, sibling)
    local = [
        pltpu.make_async_copy(own, mine, local_sem),
        pltpu.make_async_copy(routes_ref, all_routes_ref.at[x, core], route_sem),
    ]
    for copy in local:
        copy.start()
    for by, device in peers:
        link.send(routes_ref, all_routes_ref.at[x, core], 8 + by, device)
    low, high, far = (x + 3) % 4, (x + 1) % 4, (x + 2) % 4
    upper, lower = pl.ds(0, 64), pl.ds(64, 64)
    from_low, from_high = all_ref.at[low, core], all_ref.at[high, core]
    link.arrive(from_low, 0)
    first = all_ref.at[low, core, upper]
    link.send(first, first, 2, right)
    link.arrive(from_high, 1)
    second = all_ref.at[high, core, lower]
    link.send(second, second, 3, left)
    link.send(from_low, from_low, 5, sibling)
    link.send(from_high, from_high, 6, sibling)
    for key, rows in ((2, upper), (3, lower)):
        ref = all_ref.at[far, core, rows]
        link.arrive(ref, key)
        link.send(ref, ref, key + 5, sibling)
    for key, ref in (
        (4, all_ref.at[x, 1 - core]),
        (5, all_ref.at[low, 1 - core]),
        (6, all_ref.at[high, 1 - core]),
        (7, all_ref.at[far, 1 - core, upper]),
        (8, all_ref.at[far, 1 - core, lower]),
    ):
        link.arrive(ref, key)
    for by in range(1, 8):
        giver = all_routes_ref.at[(x + 4 - by // 2) % 4, (core + by) % 2]
        link.arrive(giver, 8 + by)
    for copy in local:
        copy.wait()
    link.finish()


def gather_queries(queries, routes):
    return pl.pallas_call(
        query_kernel,
        out_shape=(
            jax.ShapeDtypeStruct((4, 2, ROWS, 512), BF),
            jax.ShapeDtypeStruct((4, 2, 8, ROWS), jnp.int32),
        ),
        in_specs=[pl.BlockSpec(memory_space=pl.ANY)] * 2,
        out_specs=(pl.BlockSpec(memory_space=pl.ANY),) * 2,
        scratch_shapes=[
            pltpu.SemaphoreType.DMA,
            pltpu.SemaphoreType.DMA,
            pltpu.SemaphoreType.DMA((16,)),
            pltpu.SemaphoreType.DMA((16,)),
        ],
        compiler_params=pltpu.CompilerParams(collective_id=3, has_side_effects=True),
        name="gather_queries",
    )(queries, routes)


SCALE2 = LOG2E * 128 ** (-0.5)
BY_ROW = (((1,), (1,)), ((), ()))


def node_kernel(
    local_ref, branch_id_ref, root_pages_ref, branch_pages_ref, root_len_ref, branch_len_ref, part_ref,
    all_ref, pages_ref, code_row_ref, code_col_ref,
    sum_ref, stat_ref,
    query_ref, acc_ref, max_ref, total_ref, node_sum_ref, node_stat_ref,
):
    part = part_ref[0]
    lane = lax.broadcasted_iota(jnp.int32, (1, 128), 1)

    def pick(kind, base, count):
        wanted = lax.broadcasted_iota(jnp.int32, (count, 1024), 0) + base
        chosen = (wanted == code_row_ref[kind : kind + 1, :]).astype(BF)
        return jnp.dot(chosen, all_ref[...], preferred_element_type=F32).astype(BF)

    def put(row, rows):
        stats = jnp.zeros((rows, 128), F32)
        for h in range(4):
            span = pl.ds(h * rows, rows)
            node_sum_ref[pl.ds(row, rows), h * 128 : (h + 1) * 128] = acc_ref[span, :].astype(BF)
            stats = jnp.where(lane == h, max_ref[span, 0:1], stats)
            stats = jnp.where(lane == 4 + h, total_ref[span, 0:1], stats)
        node_stat_ref[pl.ds(row, rows), :] = stats

    chunk = 8
    for k in range(ROOT_DEV):
        root = local_ref[k]
        length = root_len_ref[root]
        picked = pick(0, k * 128, 128)
        for h in range(4):
            query_ref[h * 128 : (h + 1) * 128, :] = picked[:, h * 128 : (h + 1) * 128]
        acc_ref[...] = jnp.zeros_like(acc_ref)
        max_ref[...] = jnp.full_like(max_ref, MASKED_SCORE)
        total_ref[...] = jnp.zeros_like(total_ref)
        used = (length - part * 64 + PAGE - 1) // PAGE
        steps = (used + chunk - 1) // chunk

        def body(i, _):
            ids = [root_pages_ref[root, i * chunk + j] for j in range(chunk)]
            keys = jnp.concatenate([pages_ref[0, page] for page in ids], axis=0)
            values = jnp.concatenate([pages_ref[1, page] for page in ids], axis=0)
            spot = lax.broadcasted_iota(jnp.int32, (1, chunk * 64), 1)
            spot = (i * chunk + spot // 64) * PAGE + part * 64 + spot % 64
            usable = spot < length
            for h in range(4):
                span = pl.ds(h * 128, 128)
                scores = lax.dot_general(query_ref[span, :], keys, BY_ROW, preferred_element_type=F32)
                scores = jnp.where(usable, scores * SCALE2, MASKED_SCORE)
                old = max_ref[span, 0:1]
                new = jnp.maximum(old, jnp.max(scores, axis=1, keepdims=True))
                weights = jnp.where(usable, jnp.exp2(scores - new), 0.0)
                fade = jnp.exp2(old - new)
                total = total_ref[span, 0:1] * fade + jnp.sum(weights, axis=1, keepdims=True)
                acc_ref[span, :] = acc_ref[span, :] * fade + jnp.dot(
                    weights.astype(BF), values, preferred_element_type=F32
                )
                max_ref[span, :] = jnp.broadcast_to(new, (128, 128))
                total_ref[span, :] = jnp.broadcast_to(total, (128, 128))
            return 0

        lax.fori_loop(0, steps, body, 0)
        put(k * 128, 128)

    def branch_body(b, _):
        branch = branch_id_ref[b]
        length = branch_len_ref[branch]
        picked = pick(1, b * 32, 32)
        stacked = jnp.concatenate([picked[:, h * 128 : (h + 1) * 128] for h in range(4)], axis=0)
        ids = [branch_pages_ref[branch, j] for j in range(4)]
        keys = jnp.concatenate([pages_ref[0, page] for page in ids], axis=0)
        values = jnp.concatenate([pages_ref[1, page] for page in ids], axis=0)
        spot = lax.broadcasted_iota(jnp.int32, (1, 256), 1)
        spot = (spot // 64) * PAGE + part * 64 + spot % 64
        usable = spot < length
        scores = lax.dot_general(stacked, keys, BY_ROW, preferred_element_type=F32)
        scores = jnp.where(usable, scores * SCALE2, MASKED_SCORE)
        top = jnp.max(scores, axis=1, keepdims=True)
        weights = jnp.where(usable, jnp.exp2(scores - top), 0.0)
        total = jnp.sum(weights, axis=1, keepdims=True)
        acc = jnp.dot(weights.astype(BF), values, preferred_element_type=F32)
        row = pl.multiple_of(256 + b * 32, 32)
        stats = jnp.zeros((32, 128), F32)
        for h in range(4):
            node_sum_ref[pl.ds(row, 32), h * 128 : (h + 1) * 128] = acc[h * 32 : (h + 1) * 32].astype(BF)
            stats = jnp.where(lane == h, top[h * 32 : (h + 1) * 32], stats)
            stats = jnp.where(lane == 4 + h, total[h * 32 : (h + 1) * 32], stats)
        node_stat_ref[pl.ds(row, 32), :] = stats
        return 0

    lax.fori_loop(0, BR_DEV, branch_body, 0)

    def spread_body(block, _):
        parts = []
        wanted = lax.broadcasted_iota(jnp.int32, (ROWS, 256), 1)
        for kind in range(2):
            code = code_col_ref[block, :, kind : kind + 1]
            chosen = wanted == code
            rows = slice(kind * 256, kind * 256 + 256)
            sums = jnp.dot(chosen.astype(BF), node_sum_ref[rows, :], preferred_element_type=F32)
            stats = jnp.dot(
                chosen.astype(F32),
                node_stat_ref[rows, :],
                preferred_element_type=F32,
                precision=lax.Precision.HIGHEST,
            )
            stats = jnp.where((lane < 4) & (code < 0), MASKED_SCORE, stats)
            parts.append((sums, stats))
        merged, stats = merge_blocks(parts[0], parts[1], 4)
        sum_ref[block] = merged.astype(BF)
        stat_ref[block] = stats
        return 0

    lax.fori_loop(0, 8, spread_body, 0)


def merge_blocks(one, two, heads):
    sums_one, stats_one = one
    sums_two, stats_two = two
    lane = lax.broadcasted_iota(jnp.int32, (1, 128), 1)
    pieces = []
    stats = jnp.zeros_like(stats_one)
    for h in range(heads):
        span = slice(h * 128, (h + 1) * 128)
        top_one, top_two = stats_one[:, h : h + 1], stats_two[:, h : h + 1]
        top = jnp.maximum(top_one, top_two)
        factor_one, factor_two = jnp.exp2(top_one - top), jnp.exp2(top_two - top)
        pieces.append(
            sums_one[:, span].astype(F32) * factor_one + sums_two[:, span].astype(F32) * factor_two
        )
        total = stats_one[:, 4 + h : 5 + h] * factor_one + stats_two[:, 4 + h : 5 + h] * factor_two
        stats = jnp.where(lane == h, top, stats)
        stats = jnp.where(lane == 4 + h, total, stats)
    return jnp.concatenate(pieces, axis=1), stats


def node_partials(local_roots, local_branches, tables, part, all_queries, pages, codes):
    return pl.pallas_call(
        node_kernel,
        out_shape=(
            jax.ShapeDtypeStruct((8, ROWS, 512), BF),
            jax.ShapeDtypeStruct((8, ROWS, 128), F32),
        ),
        in_specs=[pl.BlockSpec(memory_space=pltpu.SMEM)] * 7 + [pl.BlockSpec(memory_space=pltpu.VMEM)] * 4,
        out_specs=(pl.BlockSpec(memory_space=pltpu.VMEM),) * 2,
        scratch_shapes=[
            pltpu.VMEM((512, 128), BF),
            pltpu.VMEM((512, 128), F32),
            pltpu.VMEM((512, 128), F32),
            pltpu.VMEM((512, 128), F32),
            pltpu.VMEM((512, 512), BF),
            pltpu.VMEM((512, 128), F32),
        ],
        compiler_params=pltpu.CompilerParams(vmem_limit_bytes=40 * 2**20),
        name="node_partials",
    )(local_roots, local_branches, *tables, part, all_queries, pages, codes, codes.T.reshape(8, ROWS, 2))


def attend_kernel(
    sum_ref, stat_ref, query_ref, own_query_ref, leaf_ref, leaf_len_ref, fresh_ref, weight_ref, residual_ref,
    hidden_ref, narrow_ref,
    their_sum, their_stat, run_sum, run_stat, land_sum, land_stat, last_sum, last_stat,
    leaf_sum, leaf_stat, side_sum, side_stat, give_sum,
    proj_ref, full1, full2, send_sem, recv_sem,
):
    at = place()
    link = Link(at, (send_sem, recv_sem))
    send, arrive, sibling = link.send, link.arrive, link.sibling
    beside = {**at, "z": at["z"] + 1 - 2 * (at["z"] % 2)}
    right, left = step_along(at, "x", 1), step_along(at, "x", 3)
    greet(all_peers(at))
    x, core = at["x"], at["c"]
    part = at["z"] % 2
    send(sum_ref.at[:, 1 - core], their_sum, 0, sibling)
    send(stat_ref.at[:, 1 - core], their_stat, 1, sibling)
    lane = lax.broadcasted_iota(jnp.int32, (1, 128), 1)

    def leaf_body(i, _):
        base = pl.multiple_of(i * 8, 8)
        span = pl.ds(base, 8)
        heads = [query_ref[span, h * 128 : (h + 1) * 128] for h in range(4)]
        stacked = jnp.concatenate(heads, axis=0)
        keys = leaf_ref[0, span].reshape(512, 128)
        values = leaf_ref[1, span].reshape(512, 128)
        scores = lax.dot_general(
            stacked.astype(BF), keys, BY_ROW, preferred_element_type=F32
        )
        row = lax.broadcasted_iota(jnp.int32, (32, 512), 0) % 8
        col = lax.broadcasted_iota(jnp.int32, (32, 512), 1)
        lengths = jnp.concatenate([leaf_len_ref[span, 0:1]] * 4, axis=0)
        usable = (row == col // 64) & (part * 64 + col % 64 < lengths)
        scores = jnp.where(usable, scores * SCALE2, MASKED_SCORE)
        top = jnp.max(scores, axis=1, keepdims=True)
        weights = jnp.where(usable, jnp.exp2(scores - top), 0.0)
        total = jnp.sum(weights, axis=1, keepdims=True)
        acc = jnp.dot(weights.astype(BF), values, preferred_element_type=F32)
        stats = jnp.zeros((8, 128), F32)
        for h in range(4):
            leaf_sum[span, h * 128 : (h + 1) * 128] = acc[h * 8 : (h + 1) * 8]
            stats = jnp.where(lane == h, top[h * 8 : (h + 1) * 8], stats)
            stats = jnp.where(lane == 4 + h, total[h * 8 : (h + 1) * 8], stats)
        leaf_stat[span, :] = stats
        return 0

    lax.fori_loop(0, 16, leaf_body, 0)
    arrive(their_sum, 0)
    arrive(their_stat, 1)

    def cross_body(i, _):
        value = lax.rem(x + 2 + i, 4)
        merged, stats = merge_blocks(
            (sum_ref[value, core], stat_ref[value, core]), (their_sum[value], their_stat[value]), 4
        )
        run_sum[value] = merged.astype(BF)
        run_stat[value] = stats
        return 0

    def cross_merge(by):
        cross_body(by - 2, 0)

    low, high, far = (x + 3) % 4, (x + 1) % 4, (x + 2) % 4
    upper, lower = pl.ds(0, 64), pl.ds(64, 64)
    cross_merge(2)
    for key, rows, device in ((2, upper, right), (4, lower, left)):
        send(run_sum.at[far, rows], land_sum.at[rows], key, device)
        send(run_stat.at[far, rows], land_stat.at[rows], key + 1, device)
    cross_merge(3)
    cross_merge(4)
    cross_merge(5)
    for key, rows, value, device, side in ((2, upper, high, right, 0), (4, lower, low, left, 1)):
        arrive(land_sum.at[rows], key)
        arrive(land_stat.at[rows], key + 1)
        merged, stats = merge_blocks(
            (run_sum[value, rows], run_stat[value, rows]), (land_sum[rows], land_stat[rows]), 4
        )
        run_sum[value, rows] = merged.astype(BF)
        run_stat[value, rows] = stats
        send(run_sum.at[value], last_sum.at[side], key + 4, device)
        send(run_stat.at[value], last_stat.at[side], key + 5, device)
    sums, stats = merge_blocks((run_sum[x], run_stat[x]), (leaf_sum[...], leaf_stat[...]), 4)
    for side, key in ((0, 6), (1, 8)):
        arrive(last_sum.at[side], key)
        arrive(last_stat.at[side], key + 1)
        sums, stats = merge_blocks((sums, stats), (last_sum[side], last_stat[side]), 4)
    first = part == 0
    give_sum[...] = jnp.where(first, sums[:, 256:], sums[:, :256]).astype(BF)
    leaf_stat[...] = stats
    send(give_sum, side_sum, 10, device_of(beside))
    send(leaf_stat, side_stat, 11, device_of(beside))
    kept = jnp.where(first, sums[:, :256], sums[:, 256:])
    fresh_key = fresh_ref[0].astype(F32)
    fresh_value = fresh_ref[1].astype(F32)
    own_scores = [
        jnp.sum(own_query_ref[:, h * 128 : (h + 1) * 128].astype(F32) * fresh_key, axis=1, keepdims=True)
        * SCALE2
        for h in range(2)
    ]
    arrive(side_sum, 10)
    arrive(side_stat, 11)
    theirs = side_stat[...]
    pieces = []
    for h in range(2):
        span = slice(h * 128, (h + 1) * 128)

        def column(from_stats, offset):
            return jnp.where(
                first,
                from_stats[:, offset + h : offset + h + 1],
                from_stats[:, offset + 2 + h : offset + 3 + h],
            )

        top_one, top_two = column(stats, 0), column(theirs, 0)
        top = jnp.maximum(jnp.maximum(top_one, top_two), own_scores[h])
        factor_one, factor_two = jnp.exp2(top_one - top), jnp.exp2(top_two - top)
        factor_own = jnp.exp2(own_scores[h] - top)
        weighted = (
            kept[:, span] * factor_one
            + side_sum[:, span].astype(F32) * factor_two
            + factor_own * fresh_value
        )
        total = column(stats, 4) * factor_one + column(theirs, 4) * factor_two + factor_own
        pieces.append((weighted / total).astype(BF))
    attended = jnp.concatenate(pieces, axis=1)
    for i in range(16):
        product = jnp.dot(
            attended, weight_ref[:, i * 256 : (i + 1) * 256], preferred_element_type=F32
        ).astype(BF)
        for half in range(2):
            proj_ref[i // 4, i % 4, half] = product[:, half * 128 : (half + 1) * 128]

    def finish(row, rows, half, total):
        cols = pl.ds(half * 128, 128)
        total += residual_ref[pl.ds(row, rows), cols].astype(F32)
        hidden_ref[pl.ds(row, rows), cols] = total
        narrow_ref[half, pl.ds(row, rows), :] = total.astype(BF)

    ring_reduce(
        at, link, proj_ref, ("y", "z"), (("y", "z"), ("z", "y")), ((0, 64), (64, 64)), 0,
        (full1, full2), 12, finish,
    )
    link.finish()


def attend(sums, stats, queries, own_queries, leaf, leaf_len, fresh, out_weight, residual):
    return pl.pallas_call(
        attend_kernel,
        out_shape=(
            jax.ShapeDtypeStruct((ROWS, 256), F32),
            jax.ShapeDtypeStruct((2, ROWS, 128), BF),
        ),
        in_specs=[pl.BlockSpec(memory_space=pltpu.VMEM)] * 9,
        out_specs=(pl.BlockSpec(memory_space=pltpu.VMEM),) * 2,
        scratch_shapes=[
            pltpu.VMEM((4, ROWS, 512), BF),
            pltpu.VMEM((4, ROWS, 128), F32),
            pltpu.VMEM((4, ROWS, 512), BF),
            pltpu.VMEM((4, ROWS, 128), F32),
            pltpu.VMEM((ROWS, 512), BF),
            pltpu.VMEM((ROWS, 128), F32),
            pltpu.VMEM((2, ROWS, 512), BF),
            pltpu.VMEM((2, ROWS, 128), F32),
            pltpu.VMEM((ROWS, 512), F32),
            pltpu.VMEM((ROWS, 128), F32),
            pltpu.VMEM((ROWS, 256), BF),
            pltpu.VMEM((ROWS, 128), F32),
            pltpu.VMEM((ROWS, 256), BF),
            pltpu.VMEM((4, 4, 2, ROWS, 128), BF),
            pltpu.VMEM((3, 4, 2, ROWS, 128), BF),
            pltpu.VMEM((3, 2, ROWS, 128), BF),
            pltpu.SemaphoreType.DMA((28,)),
            pltpu.SemaphoreType.DMA((28,)),
        ],
        compiler_params=pltpu.CompilerParams(
            collective_id=4, has_side_effects=True, vmem_limit_bytes=48 * 2**20
        ),
        name="attend",
    )(sums, stats, queries, own_queries, leaf, leaf_len, fresh, out_weight, residual)


def owned_nodes(owner, dp_index, count):
    node = jnp.arange(owner.shape[0])
    owned = owner == dp_index
    rank = jnp.sum((owned[None, :] & (node[None, :] < node[:, None])).astype(jnp.int32), axis=1)
    chosen = owned[None, :] & (rank[None, :] == jnp.arange(count)[:, None])
    return jnp.sum(jnp.where(chosen, node[None, :], 0), axis=1), jnp.where(owned, rank, -1)


def slot_codes(slot_request, request_branch, branch_parent, root_place, branch_place):
    slots = slot_request.shape[0]
    slot = jnp.arange(slots)
    slot_branch = jnp.sum(
        jnp.where(slot_request[:, None] == slot[None, :], request_branch[None, :], 0), axis=1
    )
    rank = jnp.sum(
        ((slot_branch[:, None] == slot_branch[None, :]) & (slot[None, :] < slot[:, None])).astype(jnp.int32),
        axis=1,
    )
    branch = jnp.arange(branch_parent.shape[0])
    kid = jnp.sum(
        ((branch_parent[:, None] == branch_parent[None, :]) & (branch[None, :] < branch[:, None])).astype(
            jnp.int32
        ),
        axis=1,
    )
    parent_place = jnp.sum(
        jnp.where(branch_parent[:, None] == jnp.arange(root_place.shape[0])[None, :], root_place[None, :], 0),
        axis=1,
    )
    root_base = jnp.where(parent_place >= 0, parent_place * ROWS + kid * BR_CAP, -4096)
    branch_base = jnp.where(branch_place >= 0, branch_place * BR_CAP, -4096)
    mine = slot_branch[None, :, None] == branch[None, None, :]
    bases = jnp.sum(jnp.where(mine, jnp.stack([root_base, branch_base])[:, None, :], 0), axis=2)
    return jnp.maximum(bases + rank[None, :], -1)


def expert_tables(all_routes):
    dp = lax.axis_index("dp")
    core = dp % 2
    names = jnp.arange(EXPERTS)
    hit = jnp.any(all_routes[:, :, :, None] == names, axis=2)
    before = jnp.tril(jnp.ones((ROWS, ROWS), F32), -1)
    rank = jnp.einsum(
        "rq,bqe->ebr", before.astype(BF), hit.astype(BF), preferred_element_type=F32
    ).astype(jnp.int32)
    rank = jnp.where(hit.transpose(2, 0, 1), rank, -1)
    mine = lax.dynamic_index_in_dim(rank, dp, 0, False)
    other = jnp.sum(all_routes, axis=2) - dp
    packed = mine[:, None, :] == jnp.arange(E_CAP)[None, :, None]
    other = jnp.sum(jnp.where(packed, other[:, None, :], 0), axis=2)
    other = other.reshape(4, 2, E_CAP).transpose(1, 0, 2).reshape(-1, 1)
    shift = (jnp.arange(4) % 2 * E_CAP)[:, None]

    def coded(ranks):
        return jnp.where(ranks >= 0, ranks + shift, -1)

    mine = mine.reshape(4, 2, ROWS)
    pick = jnp.stack([coded(mine[:, c]).reshape(2, 1, 256) for c in range(2)])
    ours = lax.dynamic_index_in_dim(rank.reshape(EXPERTS, 4, 2, ROWS), core, 2, False)
    spread = jnp.stack(
        [
            coded(lax.dynamic_index_in_dim(ours, dp, 0, False)).reshape(2, 256),
            coded(lax.dynamic_index_in_dim(ours, dp + 1 - 2 * core, 0, False)).reshape(2, 256),
        ],
        axis=2,
    )
    return pick, other, spread


def shards(
    queries,
    new_kv,
    residual,
    out_weight,
    norm_gain,
    router,
    expert_in,
    expert_out,
    node_cache,
    leaf_cache,
    slot_request,
    request_branch,
    branch_parent,
    root_owner,
    branch_owner,
    root_pages,
    branch_pages,
    root_len,
    branch_len,
    leaf_len,
    routes,
):
    dp = lax.axis_index("dp")
    mp = lax.axis_index("mp")
    local_roots, root_place = owned_nodes(root_owner, dp, ROOT_DEV)
    local_branches, branch_place = owned_nodes(branch_owner, dp, BR_DEV)
    codes = slot_codes(slot_request, request_branch, branch_parent, root_place, branch_place)
    all_queries, all_routes = gather_queries(queries, jnp.pad(routes.T, ((0, 6), (0, 0))))
    all_queries = all_queries.reshape(8 * ROWS, 512)
    pick, other, spread = expert_tables(all_routes.reshape(8, 8, ROWS)[:, :2].transpose(0, 2, 1))
    sums, stats = node_partials(
        local_roots,
        local_branches,
        (root_pages, branch_pages, root_len, branch_len),
        (mp % 2).reshape(1).astype(jnp.int32),
        all_queries,
        node_cache[:, :, 0],
        codes,
    )
    hidden, narrow = attend(
        sums.reshape(4, 2, ROWS, 512),
        stats.reshape(4, 2, ROWS, 128),
        lax.dynamic_slice_in_dim(queries, (mp // 2) * 512, 512, 1).astype(F32),
        lax.dynamic_slice_in_dim(queries, mp * 256, 256, 1),
        leaf_cache[:, :, 0],
        leaf_len[:, None],
        lax.dynamic_slice_in_dim(new_kv, (mp // 2) * 128, 128, 2),
        out_weight,
        residual,
    )
    return run_experts(
        narrow,
        hidden,
        pick,
        other,
        spread,
        norm_gain.reshape(16, 1, 256),
        router,
        expert_in[0],
        expert_out[0],
    )


def solution(mesh):
    placed = (
        P("dp", None),
        P(None, "dp", None),
        P("dp", "mp"),
        P("mp", None),
        P(),
        P(),
        P("dp", None, "mp", None),
        P("dp", "mp", None),
        P(None, "dp", "mp", None, None),
        P(None, "dp", "mp", None, None),
        P(),
        P(),
        P(),
        P(),
        P(),
        P(),
        P(),
        P(),
        P(),
        P("dp"),
        P("dp", None),
    )
    return jax.shard_map(
        shards, mesh=mesh, in_specs=placed, out_specs=P("dp", "mp"), check_vma=False
    )
```

```python
import jax
import jax.numpy as jnp
from jax import lax
from jax.experimental import pallas as pl
from jax.experimental.pallas import tpu as pltpu
from jax.sharding import PartitionSpec as P

EXPERTS = 8
PAGE = 128
ROOT_DEV = 2
BR_DEV = 8
BR_CAP = 32
E_CAP = 64

MASKED_SCORE = -1e30
NORM_EPS = 1e-05

BF = jnp.bfloat16
F32 = jnp.float32
MESH = pl.DeviceIdType.MESH
ROWS = 128
PART_ROWS = ((0, 48), (48, 48), (96, 32))
AXES = ("x", "y", "z")
ORDERS = tuple(AXES[part:] + AXES[:part] for part in range(3))


def place():
    dp = lax.axis_index("dp")
    mp = lax.axis_index("mp")
    return {"x": dp // 2, "c": dp % 2, "y": mp // 4, "z": mp % 4}


def device_of(at, **moved):
    at = {**at, **moved}
    return (at["x"] * 2 + at["c"], at["y"] * 4 + at["z"])


def step_along(at, axis, by):
    return device_of(at, **{axis: (at[axis] + by) % 4})


def greet(peers):
    barrier = pltpu.get_barrier_semaphore()
    for peer in peers:
        pl.semaphore_signal(barrier, inc=1, device_id=peer, device_id_type=MESH)
    pl.semaphore_wait(barrier, len(peers))


def remote(src, dst, sems, key, device):
    return pltpu.make_async_remote_copy(
        src_ref=src,
        dst_ref=dst,
        send_sem=sems[0].at[key],
        recv_sem=sems[1].at[key],
        device_id=device,
        device_id_type=MESH,
    )


def all_peers(at):
    return [step_along(at, axis, by) for axis in AXES for by in (1, 2, 3)] + [
        device_of(at, c=1 - at["c"])
    ]


class Link:
    def __init__(self, at, sems):
        self.sems = sems
        self.sibling = device_of(at, c=1 - at["c"])
        self.started = []

    def send(self, src, dst, key, device):
        copy = remote(src, dst, self.sems, key, device)
        copy.start()
        self.started.append(copy)

    def arrive(self, ref, key):
        remote(ref, ref, self.sems, key, self.sibling).wait_recv()

    def finish(self):
        for copy in self.started:
            copy.wait_send()


def gather_all(at, link, own_ref, buf_ref, local_sem, base, meanwhile):
    both = slice(None)
    core = at["c"]

    def slab(part, phase, value, half, plane):
        index = {"x": at["x"], "y": at["y"], "z": at["z"]}
        for axis in ORDERS[part][:phase]:
            index[axis] = slice(None)
        index[ORDERS[part][phase]] = value
        row, rows = PART_ROWS[part]
        return buf_ref.at[index["x"], plane, index["y"], index["z"], half, pl.ds(row, rows), :]

    local = pltpu.make_async_copy(own_ref, buf_ref.at[at["x"], core, at["y"], at["z"]], local_sem)
    local.start()
    for phase in range(2):
        for part in range(3):
            axis = ORDERS[part][phase]
            ref = slab(part, phase, at[axis], both, core)
            src = ref
            if phase == 0:
                row, rows = PART_ROWS[part]
                src = own_ref.at[:, pl.ds(row, rows), :]
            for by in (2, 1, 3):
                link.send(src, ref, base + (part * 2 + phase) * 3 + by - 1, step_along(at, axis, by))
        if phase == 0:
            local.wait()
        else:
            meanwhile()
        for part in range(3):
            axis = ORDERS[part][phase]
            for by in (1, 3, 2):
                ref = slab(part, phase, (at[axis] - by) % 4, both, core)
                link.arrive(ref, base + (part * 2 + phase) * 3 + by - 1)
    base += 18
    for part in range(3):
        axis = ORDERS[part][2]
        key = base + part * 8
        ref = slab(part, 2, at[axis], both, core)
        link.send(ref, ref, key, step_along(at, axis, 1))
        link.send(ref, ref, key + 1, step_along(at, axis, 3))
        link.send(ref, ref, key + 4, link.sibling)
    for part in range(3):
        axis = ORDERS[part][2]
        key = base + part * 8
        for side, by in ((0, 3), (1, 1)):
            value = (at[axis] + by) % 4
            ref = slab(part, 2, value, both, core)
            link.arrive(ref, key + side)
            half = slab(part, 2, value, side, core)
            link.send(half, half, key + 2 + side, step_along(at, axis, 1 + 2 * side))
            link.send(ref, ref, key + 5 + side, link.sibling)
    for part in range(3):
        axis = ORDERS[part][2]
        key = base + part * 8
        far = (at[axis] + 2) % 4
        for side in range(2):
            link.arrive(slab(part, 2, far, side, core), key + 2 + side)
        ref = slab(part, 2, far, both, core)
        link.send(ref, ref, key + 7, link.sibling)

    def others():
        for part in range(3):
            v = at[ORDERS[part][2]]
            for i, by in enumerate((0, 3, 1, 2)):
                link.arrive(slab(part, 2, (v + by) % 4, both, 1 - core), base + part * 8 + 4 + i)

    return others


GATHER_KEYS = 18 + 24


def ring_reduce(at, link, sum_ref, dims, orders, part_rows, relay, lands, base, finish):
    phases = len(dims)
    both = slice(None)
    parts = range(len(orders))

    def view(part, phase, value, half):
        index = dict(at)
        for axis in orders[part][phase + 1 :]:
            index[axis] = slice(None)
        index[orders[part][phase]] = value
        row, rows = part_rows[part]
        return tuple(index[axis] for axis in dims) + (half, pl.ds(row, rows), slice(None))

    def spot(part, phase, slot, *half):
        row, rows = part_rows[part]
        return (slot,) + (slice(None),) * (phases - 1 - phase) + half + (pl.ds(row, rows), slice(None))

    def accumulate(target, others):
        total = sum_ref[target].astype(F32)
        for ref, index in others:
            total += ref[index].astype(F32)
        return total

    for phase in range(phases):
        keys = [base + (part * phases + phase) * 4 for part in parts]
        if phase < relay:
            halves, fulls = lands[phase]
            for part in parts:
                axis = orders[part][phase]
                for side, by in ((0, 1), (1, 3)):
                    link.send(
                        sum_ref.at[view(part, phase, (at[axis] + 2) % 4, side)],
                        halves.at[spot(part, phase, side)],
                        keys[part] + side,
                        step_along(at, axis, by),
                    )
            for part in parts:
                axis = orders[part][phase]
                for side, by in ((0, 1), (1, 3)):
                    index = spot(part, phase, side)
                    link.arrive(halves.at[index], keys[part] + side)
                    target = view(part, phase, (at[axis] + by) % 4, side)
                    sum_ref[target] = accumulate(target, [(halves, index)]).astype(BF)
                    link.send(
                        sum_ref.at[view(part, phase, (at[axis] + by) % 4, both)],
                        fulls.at[spot(part, phase, side, both)],
                        keys[part] + 2 + side,
                        step_along(at, axis, by),
                    )
            slots, first = 2, 2
        else:
            fulls = lands[phase]
            for part in parts:
                axis = orders[part][phase]
                for by in (2, 1, 3):
                    link.send(
                        sum_ref.at[view(part, phase, (at[axis] + by) % 4, both)],
                        fulls.at[spot(part, phase, by - 1, both)],
                        keys[part] + by - 1,
                        step_along(at, axis, by),
                    )
            slots, first = 3, 0
        for part in parts:
            axis = orders[part][phase]
            for slot in range(slots):
                link.arrive(fulls.at[spot(part, phase, slot, both)], keys[part] + first + slot)
            for half in range(2):
                target = view(part, phase, at[axis], half)
                total = accumulate(target, [(fulls, spot(part, phase, slot, half)) for slot in range(slots)])
                if phase < phases - 1:
                    sum_ref[target] = total.astype(BF)
                else:
                    finish(*part_rows[part], half, total)


def expert_kernel(
    own_ref, kept_ref, routes_ref, gain_ref, router_ref, up_hbm, down_hbm,
    out_ref,
    buf_ref, code_ref, other_ref, rows_ref, gate_ref, up_ref, down_ref, act_ref, give_ref, theirs_ref, sum_ref,
    half0, full0, full1, full2,
    local_sem, up_sem, down_sem, send_sem, recv_sem,
):
    at = place()
    loads = [pltpu.make_async_copy(up_hbm, up_ref, up_sem), pltpu.make_async_copy(down_hbm, down_ref, down_sem)]
    for load in loads:
        load.start()
    greet(all_peers(at))
    link = Link(at, (send_sem, recv_sem))
    core = at["c"]
    mine = lax.axis_index("dp")
    row_index = lax.broadcasted_iota(jnp.int32, (ROWS, ROWS), 0)
    lane_index = lax.broadcasted_iota(jnp.int32, (ROWS, ROWS), 1)
    upright = []

    def tables():
        unit = (row_index == lane_index).astype(BF)
        later = (row_index < lane_index).astype(BF)
        earlier = (lane_index < row_index).astype(BF)
        first = jnp.concatenate([routes_ref[b // 2, b % 2, 0:1, :] for b in range(8)], axis=0)
        second = jnp.concatenate([routes_ref[b // 2, b % 2, 1:2, :] for b in range(8)], axis=0)
        shift = (lax.broadcasted_iota(jnp.int32, (8, ROWS), 0) // 2) % 2 * E_CAP
        hit = ((first == mine) | (second == mine)).astype(F32)
        rank = jnp.dot(hit.astype(BF), later, preferred_element_type=F32).astype(jnp.int32)
        code_ref[0:8, :] = jnp.where(hit > 0.5, rank + shift, -1)
        other_ref[...] = first + second - mine
        for expert in (mine, mine + 1 - 2 * core):
            hit = ((first == expert) | (second == expert)).astype(BF)
            there = lax.dot_general(unit, hit, BY_ROW, preferred_element_type=F32)
            rank = lax.dot_general(earlier, hit, BY_ROW, preferred_element_type=F32)
            codes = jnp.where(there > 0.5, rank, -1.0)
            upright.append(
                [jnp.where(core == 0, codes[:, 2 * b : 2 * b + 1], codes[:, 2 * b + 1 : 2 * b + 2]) for b in range(4)]
            )

    others = gather_all(at, link, own_ref, buf_ref, local_sem, 0, tables)

    def compact(plane):
        base = pl.multiple_of(plane * 256, 256)
        wanted = lax.broadcasted_iota(jnp.int32, (128, 256), 0)
        picks, answers = [], []
        for pair in range(2):
            blocks = [pl.ds(4 * pair + 2 * k + plane, 1) for k in range(2)]
            code = jnp.concatenate([code_ref[b, :] for b in blocks], axis=1)
            other = jnp.concatenate([other_ref[b, :] for b in blocks], axis=1)
            chosen = wanted == code
            picks.append(chosen.astype(BF))
            answers.append(jnp.sum(jnp.where(chosen, other, 0), axis=1, keepdims=True))
        answer = jnp.concatenate(answers, axis=0)

        def fill(y, squares):
            for z in range(4):
                pieces = []
                for pair in range(2):
                    whole = jnp.concatenate(
                        [
                            jnp.concatenate([buf_ref[2 * pair + k, plane, y, z, h] for h in range(2)], axis=1)
                            for k in range(2)
                        ],
                        axis=0,
                    )
                    pieces.append(jnp.dot(picks[pair], whole, preferred_element_type=F32))
                piece = jnp.concatenate(pieces, axis=0)
                cols = pl.ds(pl.multiple_of((y * 4 + z) * 256, 256), 256)
                rows_ref[pl.ds(base, 256), cols] = piece.astype(BF)
                piece = piece * piece
                squares += piece[:, :128] + piece[:, 128:]
            return squares

        squares = lax.fori_loop(0, 4, fill, jnp.zeros((256, 128), F32))
        scale = lax.rsqrt(jnp.sum(squares, axis=1, keepdims=True) / 4096.0 + NORM_EPS)

        def norm(y, _):
            for z in range(4):
                cols = pl.ds(pl.multiple_of((y * 4 + z) * 256, 256), 256)
                normed = rows_ref[pl.ds(base, 256), cols].astype(F32) * scale * gain_ref[y * 4 + z]
                rows_ref[pl.ds(base, 256), cols] = normed.astype(BF)
            return 0

        lax.fori_loop(0, 4, norm, 0)
        logits = jnp.dot(rows_ref[pl.ds(base, 256), :], router_ref[...], preferred_element_type=F32)
        lane = lax.broadcasted_iota(jnp.int32, logits.shape, 1)
        here = jnp.sum(jnp.where(lane == mine, logits, 0.0), axis=1, keepdims=True)
        there = jnp.sum(
            jnp.where(lane == answer, logits, 0.0), axis=1, keepdims=True
        )
        most = jnp.maximum(here, there)
        here = jnp.exp(here - most)
        there = jnp.exp(there - most)
        gate_ref[pl.ds(base, 256), :] = jnp.broadcast_to(here / (here + there), (256, 128))

    compact(core)
    others()
    compact(1 - core)
    for load in loads:
        load.wait()

    for j in range(2):
        span = slice(j * 256, (j + 1) * 256)
        gate, up = [
            lax.dot_general(rows_ref[...], up_ref[k, span, :], BY_ROW, preferred_element_type=F32)
            for k in range(2)
        ]
        act_ref[:, span] = (gate / (1.0 + jnp.exp(-gate)) * up).astype(BF)

    def project(plane, i):
        base = pl.multiple_of(plane * 256, 256)
        cols = pl.ds(pl.multiple_of(i * 256, 256), 256)
        product = jnp.dot(act_ref[pl.ds(base, 256), :], down_ref[:, cols], preferred_element_type=F32)
        return (product * gate_ref[pl.ds(base, 256), 0:1]).astype(BF)

    for group in range(4):

        def hand(k, _):
            i = group * 4 + k
            give_ref[i] = project(1 - core, i)
            return 0

        lax.fori_loop(0, 4, hand, 0)
        link.send(
            give_ref.at[pl.ds(group * 4, 4)], theirs_ref.at[pl.ds(group * 4, 4)], GATHER_KEYS + group, link.sibling
        )
    spreads = []
    for pair in range(2):
        corners = []
        for k in range(2):
            empty = jnp.zeros((ROWS, E_CAP), BF)
            lane = lax.broadcasted_iota(jnp.int32, (ROWS, E_CAP), 1).astype(F32)
            for codes in upright:
                hit = (codes[2 * pair + k] == lane).astype(BF)
                corners.append(jnp.concatenate([hit, empty] if k == 0 else [empty, hit], axis=1))
        spreads.append(
            jnp.concatenate(
                [jnp.concatenate(corners[0:2], axis=1), jnp.concatenate(corners[2:4], axis=1)], axis=0
            )
        )
    for group in range(4):
        link.arrive(theirs_ref.at[pl.ds(group * 4, 4)], GATHER_KEYS + group)

        def merge(k, _):
            i = group * 4 + k
            ours = project(core, i)
            for pair in range(2):
                rows = slice(pair * 128, (pair + 1) * 128)
                stacked = jnp.concatenate([ours[rows], theirs_ref[i, rows]], axis=0)
                spread = jnp.dot(spreads[pair], stacked, preferred_element_type=F32).astype(BF)
                for x in range(2):
                    for half in range(2):
                        sum_ref[2 * pair + x, group, k, half] = spread[
                            x * 128 : (x + 1) * 128, half * 128 : (half + 1) * 128
                        ]
            return 0

        lax.fori_loop(0, 4, merge, 0)

    def finish(row, rows, half, total):
        spot = (pl.ds(row, rows), pl.ds(half * 128, 128))
        out_ref[spot] = (kept_ref[spot] + total).astype(BF)

    ring_reduce(
        at, link, sum_ref, AXES, ORDERS, PART_ROWS, 1, ((half0, full0), full1, full2), GATHER_KEYS + 4, finish
    )
    link.finish()


def run_experts(own, kept, routes, gain, router, expert_in, expert_out):
    keys = GATHER_KEYS + 4 + 36
    vmem, hbm = pl.BlockSpec(memory_space=pltpu.VMEM), pl.BlockSpec(memory_space=pl.ANY)
    return pl.pallas_call(
        expert_kernel,
        out_shape=jax.ShapeDtypeStruct((ROWS, 256), BF),
        in_specs=[vmem] * 5 + [hbm] * 2,
        out_specs=vmem,
        scratch_shapes=[
            pltpu.VMEM((4, 2, 4, 4, 2, ROWS, 128), BF),
            pltpu.VMEM((8, ROWS), jnp.int32),
            pltpu.VMEM((8, ROWS), jnp.int32),
            pltpu.VMEM((512, 4096), BF),
            pltpu.VMEM((512, 128), F32),
            pltpu.VMEM(expert_in.shape, BF),
            pltpu.VMEM(expert_out.shape, BF),
            pltpu.VMEM((512, 512), BF),
            pltpu.VMEM((16, 256, 256), BF),
            pltpu.VMEM((16, 256, 256), BF),
            pltpu.VMEM((4, 4, 4, 2, ROWS, 128), BF),
            pltpu.VMEM((2, 4, 4, ROWS, 128), BF),
            pltpu.VMEM((2, 4, 4, 2, ROWS, 128), BF),
            pltpu.VMEM((3, 4, 2, ROWS, 128), BF),
            pltpu.VMEM((3, 2, ROWS, 128), BF),
            pltpu.SemaphoreType.DMA,
            pltpu.SemaphoreType.DMA,
            pltpu.SemaphoreType.DMA,
            pltpu.SemaphoreType.DMA((keys,)),
            pltpu.SemaphoreType.DMA((keys,)),
        ],
        compiler_params=pltpu.CompilerParams(
            collective_id=1, has_side_effects=True, vmem_limit_bytes=60 * 2**20
        ),
        name="run_experts",
    )(own, kept, routes, gain, router, expert_in, expert_out)


LOG2E = 1.4426950408889634


def query_kernel(queries_ref, routes_ref, all_ref, all_routes_ref, local_sem, route_sem, send_sem, recv_sem):
    at = place()
    link = Link(at, (send_sem, recv_sem))
    sibling = link.sibling
    right, left = step_along(at, "x", 1), step_along(at, "x", 3)
    x, core = at["x"], at["c"]
    peers = [(by, device_of(at, x=(x + by // 2) % 4, c=(core + by) % 2)) for by in range(1, 8)]
    greet([device for _, device in peers])
    kv_head = lax.axis_index("mp") // 2
    own = queries_ref.at[:, pl.ds(pl.multiple_of(kv_head * 512, 512), 512)]
    mine = all_ref.at[x, core]
    link.send(own, mine, 0, right)
    link.send(own, mine, 1, left)
    link.send(own, mine, 4, sibling)
    local = [
        pltpu.make_async_copy(own, mine, local_sem),
        pltpu.make_async_copy(routes_ref, all_routes_ref.at[x, core], route_sem),
    ]
    for copy in local:
        copy.start()
    for by, device in peers:
        link.send(routes_ref, all_routes_ref.at[x, core], 8 + by, device)
    low, high, far = (x + 3) % 4, (x + 1) % 4, (x + 2) % 4
    upper, lower = pl.ds(0, 64), pl.ds(64, 64)
    from_low, from_high = all_ref.at[low, core], all_ref.at[high, core]
    link.arrive(from_low, 0)
    first = all_ref.at[low, core, upper]
    link.send(first, first, 2, right)
    link.arrive(from_high, 1)
    second = all_ref.at[high, core, lower]
    link.send(second, second, 3, left)
    link.send(from_low, from_low, 5, sibling)
    link.send(from_high, from_high, 6, sibling)
    for key, rows in ((2, upper), (3, lower)):
        ref = all_ref.at[far, core, rows]
        link.arrive(ref, key)
        link.send(ref, ref, key + 5, sibling)
    for key, ref in (
        (4, all_ref.at[x, 1 - core]),
        (5, all_ref.at[low, 1 - core]),
        (6, all_ref.at[high, 1 - core]),
        (7, all_ref.at[far, 1 - core, upper]),
        (8, all_ref.at[far, 1 - core, lower]),
    ):
        link.arrive(ref, key)
    for by in range(1, 8):
        giver = all_routes_ref.at[(x + 4 - by // 2) % 4, (core + by) % 2]
        link.arrive(giver, 8 + by)
    for copy in local:
        copy.wait()
    link.finish()


def gather_queries(queries, routes):
    return pl.pallas_call(
        query_kernel,
        out_shape=(
            jax.ShapeDtypeStruct((4, 2, ROWS, 512), BF),
            jax.ShapeDtypeStruct((4, 2, 8, ROWS), jnp.int32),
        ),
        in_specs=[pl.BlockSpec(memory_space=pl.ANY)] * 2,
        out_specs=(pl.BlockSpec(memory_space=pl.ANY),) * 2,
        scratch_shapes=[
            pltpu.SemaphoreType.DMA,
            pltpu.SemaphoreType.DMA,
            pltpu.SemaphoreType.DMA((16,)),
            pltpu.SemaphoreType.DMA((16,)),
        ],
        compiler_params=pltpu.CompilerParams(collective_id=3, has_side_effects=True),
        name="gather_queries",
    )(queries, routes)


SCALE2 = LOG2E * 128 ** (-0.5)
BY_ROW = (((1,), (1,)), ((), ()))


def node_kernel(
    local_ref, branch_id_ref, root_pages_ref, branch_pages_ref, root_len_ref, branch_len_ref, part_ref,
    all_ref, pages_ref, code_row_ref, code_col_ref,
    sum_ref, stat_ref,
    query_ref, acc_ref, max_ref, total_ref, node_sum_ref, node_stat_ref,
):
    part = part_ref[0]
    lane = lax.broadcasted_iota(jnp.int32, (1, 128), 1)

    def pick(kind, base, count):
        wanted = lax.broadcasted_iota(jnp.int32, (count, 1024), 0) + base
        chosen = (wanted == code_row_ref[kind : kind + 1, :]).astype(BF)
        return jnp.dot(chosen, all_ref[...], preferred_element_type=F32).astype(BF)

    def put(row, rows):
        stats = jnp.zeros((rows, 128), F32)
        for h in range(4):
            span = pl.ds(h * rows, rows)
            node_sum_ref[pl.ds(row, rows), h * 128 : (h + 1) * 128] = acc_ref[span, :].astype(BF)
            stats = jnp.where(lane == h, max_ref[span, 0:1], stats)
            stats = jnp.where(lane == 4 + h, total_ref[span, 0:1], stats)
        node_stat_ref[pl.ds(row, rows), :] = stats

    chunk = 8
    for k in range(ROOT_DEV):
        root = local_ref[k]
        length = root_len_ref[root]
        picked = pick(0, k * 128, 128)
        for h in range(4):
            query_ref[h * 128 : (h + 1) * 128, :] = picked[:, h * 128 : (h + 1) * 128]
        acc_ref[...] = jnp.zeros_like(acc_ref)
        max_ref[...] = jnp.full_like(max_ref, MASKED_SCORE)
        total_ref[...] = jnp.zeros_like(total_ref)
        used = (length - part * 64 + PAGE - 1) // PAGE
        steps = (used + chunk - 1) // chunk

        def body(i, _):
            ids = [root_pages_ref[root, i * chunk + j] for j in range(chunk)]
            keys = jnp.concatenate([pages_ref[0, page] for page in ids], axis=0)
            values = jnp.concatenate([pages_ref[1, page] for page in ids], axis=0)
            spot = lax.broadcasted_iota(jnp.int32, (1, chunk * 64), 1)
            spot = (i * chunk + spot // 64) * PAGE + part * 64 + spot % 64
            usable = spot < length
            for h in range(4):
                span = pl.ds(h * 128, 128)
                scores = lax.dot_general(query_ref[span, :], keys, BY_ROW, preferred_element_type=F32)
                scores = jnp.where(usable, scores * SCALE2, MASKED_SCORE)
                old = max_ref[span, 0:1]
                new = jnp.maximum(old, jnp.max(scores, axis=1, keepdims=True))
                weights = jnp.where(usable, jnp.exp2(scores - new), 0.0)
                fade = jnp.exp2(old - new)
                total = total_ref[span, 0:1] * fade + jnp.sum(weights, axis=1, keepdims=True)
                acc_ref[span, :] = acc_ref[span, :] * fade + jnp.dot(
                    weights.astype(BF), values, preferred_element_type=F32
                )
                max_ref[span, :] = jnp.broadcast_to(new, (128, 128))
                total_ref[span, :] = jnp.broadcast_to(total, (128, 128))
            return 0

        lax.fori_loop(0, steps, body, 0)
        put(k * 128, 128)

    def branch_body(b, _):
        branch = branch_id_ref[b]
        length = branch_len_ref[branch]
        picked = pick(1, b * 32, 32)
        stacked = jnp.concatenate([picked[:, h * 128 : (h + 1) * 128] for h in range(4)], axis=0)
        ids = [branch_pages_ref[branch, j] for j in range(4)]
        keys = jnp.concatenate([pages_ref[0, page] for page in ids], axis=0)
        values = jnp.concatenate([pages_ref[1, page] for page in ids], axis=0)
        spot = lax.broadcasted_iota(jnp.int32, (1, 256), 1)
        spot = (spot // 64) * PAGE + part * 64 + spot % 64
        usable = spot < length
        scores = lax.dot_general(stacked, keys, BY_ROW, preferred_element_type=F32)
        scores = jnp.where(usable, scores * SCALE2, MASKED_SCORE)
        top = jnp.max(scores, axis=1, keepdims=True)
        weights = jnp.where(usable, jnp.exp2(scores - top), 0.0)
        total = jnp.sum(weights, axis=1, keepdims=True)
        acc = jnp.dot(weights.astype(BF), values, preferred_element_type=F32)
        row = pl.multiple_of(256 + b * 32, 32)
        stats = jnp.zeros((32, 128), F32)
        for h in range(4):
            node_sum_ref[pl.ds(row, 32), h * 128 : (h + 1) * 128] = acc[h * 32 : (h + 1) * 32].astype(BF)
            stats = jnp.where(lane == h, top[h * 32 : (h + 1) * 32], stats)
            stats = jnp.where(lane == 4 + h, total[h * 32 : (h + 1) * 32], stats)
        node_stat_ref[pl.ds(row, 32), :] = stats
        return 0

    lax.fori_loop(0, BR_DEV, branch_body, 0)

    def spread_body(block, _):
        parts = []
        wanted = lax.broadcasted_iota(jnp.int32, (ROWS, 256), 1)
        for kind in range(2):
            code = code_col_ref[block, :, kind : kind + 1]
            chosen = wanted == code
            rows = slice(kind * 256, kind * 256 + 256)
            sums = jnp.dot(chosen.astype(BF), node_sum_ref[rows, :], preferred_element_type=F32)
            stats = jnp.dot(
                chosen.astype(F32),
                node_stat_ref[rows, :],
                preferred_element_type=F32,
                precision=lax.Precision.HIGHEST,
            )
            stats = jnp.where((lane < 4) & (code < 0), MASKED_SCORE, stats)
            parts.append((sums, stats))
        merged, stats = merge_blocks(parts[0], parts[1], 4)
        sum_ref[block] = merged.astype(BF)
        stat_ref[block] = stats.T[0:8]
        return 0

    lax.fori_loop(0, 8, spread_body, 0)


def merge_blocks(one, two, heads):
    sums_one, stats_one = one
    sums_two, stats_two = two
    lane = lax.broadcasted_iota(jnp.int32, (1, 128), 1)
    pieces = []
    stats = jnp.zeros_like(stats_one)
    for h in range(heads):
        span = slice(h * 128, (h + 1) * 128)
        top_one, top_two = stats_one[:, h : h + 1], stats_two[:, h : h + 1]
        top = jnp.maximum(top_one, top_two)
        factor_one, factor_two = jnp.exp2(top_one - top), jnp.exp2(top_two - top)
        pieces.append(
            sums_one[:, span].astype(F32) * factor_one + sums_two[:, span].astype(F32) * factor_two
        )
        total = stats_one[:, 4 + h : 5 + h] * factor_one + stats_two[:, 4 + h : 5 + h] * factor_two
        stats = jnp.where(lane == h, top, stats)
        stats = jnp.where(lane == 4 + h, total, stats)
    return jnp.concatenate(pieces, axis=1), stats


def node_partials(local_roots, local_branches, tables, part, all_queries, pages, codes):
    return pl.pallas_call(
        node_kernel,
        out_shape=(
            jax.ShapeDtypeStruct((8, ROWS, 512), BF),
            jax.ShapeDtypeStruct((8, 8, ROWS), F32),
        ),
        in_specs=[pl.BlockSpec(memory_space=pltpu.SMEM)] * 7 + [pl.BlockSpec(memory_space=pltpu.VMEM)] * 4,
        out_specs=(pl.BlockSpec(memory_space=pltpu.VMEM),) * 2,
        scratch_shapes=[
            pltpu.VMEM((512, 128), BF),
            pltpu.VMEM((512, 128), F32),
            pltpu.VMEM((512, 128), F32),
            pltpu.VMEM((512, 128), F32),
            pltpu.VMEM((512, 512), BF),
            pltpu.VMEM((512, 128), F32),
        ],
        compiler_params=pltpu.CompilerParams(vmem_limit_bytes=40 * 2**20),
        name="node_partials",
    )(local_roots, local_branches, *tables, part, all_queries, pages, codes, codes.T.reshape(8, ROWS, 2))


def attend_kernel(
    sum_hbm, stat_hbm, query_hbm, leaf_hbm, leaf_len_ref, fresh_hbm, weight_hbm, residual_ref,
    hidden_ref, narrow_ref,
    own_sum, own_stat, their_sum, their_stat, run_sum, run_stat, land_sum, land_stat,
    query_ref, wide_query, own_query_ref, leaf_ref, length_ref, fresh_ref, weight_ref,
    leaf_sum, leaf_stat, give_stat, side_sum, side_stat, give_sum,
    proj_ref, full1, full2, load_sem, send_sem, recv_sem,
):
    at = place()
    link = Link(at, (send_sem, recv_sem))
    send, arrive, sibling = link.send, link.arrive, link.sibling
    beside = {**at, "z": at["z"] + 1 - 2 * (at["z"] % 2)}
    x, core = at["x"], at["c"]
    part = at["z"] % 2
    mp = lax.axis_index("mp")
    kv_head = mp // 2

    def columns(ref, width, index):
        return ref.at[:, pl.ds(pl.multiple_of(index * width, width), width)]

    loads = [
        pltpu.make_async_copy(src, dst, load_sem.at[i])
        for i, (src, dst) in enumerate(
            (
                (columns(query_hbm, 512, kv_head), query_ref),
                (leaf_hbm.at[:, :, 0], leaf_ref),
                (sum_hbm.at[:, core], own_sum),
                (stat_hbm.at[:, core], own_stat),
                (columns(query_hbm, 256, mp), own_query_ref),
                (columns(fresh_hbm.at[0], 128, kv_head), fresh_ref.at[0]),
                (columns(fresh_hbm.at[1], 128, kv_head), fresh_ref.at[1]),
                (weight_hbm, weight_ref),
            )
        )
    ]
    for load in loads:
        load.start()
    greet(all_peers(at))
    send(sum_hbm.at[:, 1 - core], their_sum, 0, sibling)
    send(stat_hbm.at[:, 1 - core], their_stat, 1, sibling)
    lane = lax.broadcasted_iota(jnp.int32, (1, 128), 1)
    unit = lax.broadcasted_iota(jnp.int32, (ROWS, ROWS), 0) == lax.broadcasted_iota(
        jnp.int32, (ROWS, ROWS), 1
    )
    lengths_row = jnp.broadcast_to(leaf_len_ref[...], (ROWS, ROWS))
    length_ref[...] = jnp.broadcast_to(
        jnp.sum(jnp.where(unit, lengths_row, 0), axis=1, keepdims=True), (ROWS, ROWS)
    )

    def upright(stats):
        return jnp.concatenate([stats, jnp.zeros((ROWS - 8, ROWS), F32)], axis=0).T

    loads[0].wait()
    loads[1].wait()
    wide_query[...] = query_ref[...].astype(F32)

    def leaf_group(base):
        span = pl.ds(base, 8)
        heads = [wide_query[span, h * 128 : (h + 1) * 128] for h in range(4)]
        stacked = jnp.concatenate(heads, axis=0)
        keys = leaf_ref[0, span].reshape(512, 128)
        values = leaf_ref[1, span].reshape(512, 128)
        scores = lax.dot_general(
            stacked.astype(BF), keys, BY_ROW, preferred_element_type=F32
        )
        row = lax.broadcasted_iota(jnp.int32, (32, 512), 0) % 8
        col = lax.broadcasted_iota(jnp.int32, (32, 512), 1)
        lengths = jnp.concatenate([length_ref[span, 0:1]] * 4, axis=0)
        usable = (row == col // 64) & (part * 64 + col % 64 < lengths)
        scores = jnp.where(usable, scores * SCALE2, MASKED_SCORE)
        top = jnp.max(scores, axis=1, keepdims=True)
        weights = jnp.where(usable, jnp.exp2(scores - top), 0.0)
        total = jnp.sum(weights, axis=1, keepdims=True)
        acc = jnp.dot(weights.astype(BF), values, preferred_element_type=F32)
        stats = jnp.zeros((8, 128), F32)
        for h in range(4):
            leaf_sum[span, h * 128 : (h + 1) * 128] = acc[h * 8 : (h + 1) * 8]
            stats = jnp.where(lane == h, top[h * 8 : (h + 1) * 8], stats)
            stats = jnp.where(lane == 4 + h, total[h * 8 : (h + 1) * 8], stats)
        leaf_stat[span, :] = stats

    def leaf_body(i, _):
        for k in range(4):
            leaf_group(pl.multiple_of(i * 32 + k * 8, 8))
        return 0

    lax.fori_loop(0, 4, leaf_body, 0)
    loads[2].wait()
    loads[3].wait()
    arrive(their_sum, 0)
    arrive(their_stat, 1)
    for by in (2, 1, 3):
        value = (x + by) % 4
        merged, stats = merge_blocks(
            (own_sum[value], upright(own_stat[value])), (their_sum[value], upright(their_stat[value])), 4
        )
        run_sum[by - 1] = merged.astype(BF)
        run_stat[by - 1] = stats.T[0:8]
        device = step_along(at, "x", by)
        send(run_sum.at[by - 1], land_sum.at[by - 1], 2 * by, device)
        send(run_stat.at[by - 1], land_stat.at[by - 1], 2 * by + 1, device)
    sums, stats = merge_blocks(
        (own_sum[x], upright(own_stat[x])), (their_sum[x], upright(their_stat[x])), 4
    )
    sums, stats = merge_blocks((sums, stats), (leaf_sum[...], leaf_stat[...]), 4)
    for load in loads[4:]:
        load.wait()
    fresh_key = fresh_ref[0].astype(F32)
    fresh_value = fresh_ref[1].astype(F32)
    own_scores = [
        jnp.sum(own_query_ref[:, h * 128 : (h + 1) * 128].astype(F32) * fresh_key, axis=1, keepdims=True)
        * SCALE2
        for h in range(2)
    ]
    for by in (1, 3, 2):
        arrive(land_sum.at[by - 1], 2 * by)
        arrive(land_stat.at[by - 1], 2 * by + 1)
        sums, stats = merge_blocks((sums, stats), (land_sum[by - 1], upright(land_stat[by - 1])), 4)
    first = part == 0
    give_sum[...] = jnp.where(first, sums[:, 256:], sums[:, :256]).astype(BF)
    give_stat[...] = stats.T[0:8]
    send(give_sum, side_sum, 10, device_of(beside))
    send(give_stat, side_stat, 11, device_of(beside))
    kept = jnp.where(first, sums[:, :256], sums[:, 256:])
    arrive(side_sum, 10)
    arrive(side_stat, 11)
    theirs = upright(side_stat[...])
    pieces = []
    for h in range(2):
        span = slice(h * 128, (h + 1) * 128)

        def column(from_stats, offset):
            return jnp.where(
                first,
                from_stats[:, offset + h : offset + h + 1],
                from_stats[:, offset + 2 + h : offset + 3 + h],
            )

        top_one, top_two = column(stats, 0), column(theirs, 0)
        top = jnp.maximum(jnp.maximum(top_one, top_two), own_scores[h])
        factor_one, factor_two = jnp.exp2(top_one - top), jnp.exp2(top_two - top)
        factor_own = jnp.exp2(own_scores[h] - top)
        weighted = (
            kept[:, span] * factor_one
            + side_sum[:, span].astype(F32) * factor_two
            + factor_own * fresh_value
        )
        total = column(stats, 4) * factor_one + column(theirs, 4) * factor_two + factor_own
        pieces.append((weighted / total).astype(BF))
    attended = jnp.concatenate(pieces, axis=1)
    for i in range(16):
        product = jnp.dot(
            attended, weight_ref[:, i * 256 : (i + 1) * 256], preferred_element_type=F32
        ).astype(BF)
        for half in range(2):
            proj_ref[i // 4, i % 4, half] = product[:, half * 128 : (half + 1) * 128]

    def finish(row, rows, half, total):
        cols = pl.ds(half * 128, 128)
        total += residual_ref[pl.ds(row, rows), cols].astype(F32)
        hidden_ref[pl.ds(row, rows), cols] = total
        narrow_ref[half, pl.ds(row, rows), :] = total.astype(BF)

    ring_reduce(
        at, link, proj_ref, ("y", "z"), (("y", "z"), ("z", "y")), ((0, 64), (64, 64)), 0,
        (full1, full2), 12, finish,
    )
    link.finish()


def attend(sums, stats, queries, leaf, leaf_len, fresh, out_weight, residual):
    vmem, hbm = pl.BlockSpec(memory_space=pltpu.VMEM), pl.BlockSpec(memory_space=pl.ANY)
    return pl.pallas_call(
        attend_kernel,
        out_shape=(
            jax.ShapeDtypeStruct((ROWS, 256), F32),
            jax.ShapeDtypeStruct((2, ROWS, 128), BF),
        ),
        in_specs=[hbm, hbm, hbm, hbm, vmem, hbm, hbm, vmem],
        out_specs=(vmem, vmem),
        scratch_shapes=[
            pltpu.VMEM((4, ROWS, 512), BF),
            pltpu.VMEM((4, 8, ROWS), F32),
            pltpu.VMEM((4, ROWS, 512), BF),
            pltpu.VMEM((4, 8, ROWS), F32),
            pltpu.VMEM((3, ROWS, 512), BF),
            pltpu.VMEM((3, 8, ROWS), F32),
            pltpu.VMEM((3, ROWS, 512), BF),
            pltpu.VMEM((3, 8, ROWS), F32),
            pltpu.VMEM((ROWS, 512), BF),
            pltpu.VMEM((ROWS, 512), F32),
            pltpu.VMEM((ROWS, 256), BF),
            pltpu.VMEM((2, ROWS, 64, 128), BF),
            pltpu.VMEM((ROWS, ROWS), jnp.int32),
            pltpu.VMEM((2, ROWS, 128), BF),
            pltpu.VMEM((256, 4096), BF),
            pltpu.VMEM((ROWS, 512), F32),
            pltpu.VMEM((ROWS, 128), F32),
            pltpu.VMEM((8, ROWS), F32),
            pltpu.VMEM((ROWS, 256), BF),
            pltpu.VMEM((8, ROWS), F32),
            pltpu.VMEM((ROWS, 256), BF),
            pltpu.VMEM((4, 4, 2, ROWS, 128), BF),
            pltpu.VMEM((3, 4, 2, ROWS, 128), BF),
            pltpu.VMEM((3, 2, ROWS, 128), BF),
            pltpu.SemaphoreType.DMA((8,)),
            pltpu.SemaphoreType.DMA((28,)),
            pltpu.SemaphoreType.DMA((28,)),
        ],
        compiler_params=pltpu.CompilerParams(
            collective_id=4, has_side_effects=True, vmem_limit_bytes=48 * 2**20
        ),
        name="attend",
    )(sums, stats, queries, leaf, leaf_len, fresh, out_weight, residual)


def owned_nodes(owner, dp_index, count):
    node = jnp.arange(owner.shape[0])
    owned = owner == dp_index
    rank = jnp.sum((owned[None, :] & (node[None, :] < node[:, None])).astype(jnp.int32), axis=1)
    chosen = owned[None, :] & (rank[None, :] == jnp.arange(count)[:, None])
    return jnp.sum(jnp.where(chosen, node[None, :], 0), axis=1), jnp.where(owned, rank, -1)


def slot_codes(slot_request, request_branch, branch_parent, root_place, branch_place):
    slots = slot_request.shape[0]
    slot = jnp.arange(slots)
    slot_branch = jnp.sum(
        jnp.where(slot_request[:, None] == slot[None, :], request_branch[None, :], 0), axis=1
    )
    rank = jnp.sum(
        ((slot_branch[:, None] == slot_branch[None, :]) & (slot[None, :] < slot[:, None])).astype(jnp.int32),
        axis=1,
    )
    branch = jnp.arange(branch_parent.shape[0])
    kid = jnp.sum(
        ((branch_parent[:, None] == branch_parent[None, :]) & (branch[None, :] < branch[:, None])).astype(
            jnp.int32
        ),
        axis=1,
    )
    parent_place = jnp.sum(
        jnp.where(branch_parent[:, None] == jnp.arange(root_place.shape[0])[None, :], root_place[None, :], 0),
        axis=1,
    )
    root_base = jnp.where(parent_place >= 0, parent_place * ROWS + kid * BR_CAP, -4096)
    branch_base = jnp.where(branch_place >= 0, branch_place * BR_CAP, -4096)
    mine = slot_branch[None, :, None] == branch[None, None, :]
    bases = jnp.sum(jnp.where(mine, jnp.stack([root_base, branch_base])[:, None, :], 0), axis=2)
    return jnp.maximum(bases + rank[None, :], -1)


def shards(
    queries,
    new_kv,
    residual,
    out_weight,
    norm_gain,
    router,
    expert_in,
    expert_out,
    node_cache,
    leaf_cache,
    slot_request,
    request_branch,
    branch_parent,
    root_owner,
    branch_owner,
    root_pages,
    branch_pages,
    root_len,
    branch_len,
    leaf_len,
    routes,
):
    dp = lax.axis_index("dp")
    mp = lax.axis_index("mp")
    local_roots, root_place = owned_nodes(root_owner, dp, ROOT_DEV)
    local_branches, branch_place = owned_nodes(branch_owner, dp, BR_DEV)
    codes = slot_codes(slot_request, request_branch, branch_parent, root_place, branch_place)
    all_queries, all_routes = gather_queries(queries, jnp.pad(routes.T, ((0, 6), (0, 0))))
    all_queries = all_queries.reshape(8 * ROWS, 512)
    sums, stats = node_partials(
        local_roots,
        local_branches,
        (root_pages, branch_pages, root_len, branch_len),
        (mp % 2).reshape(1).astype(jnp.int32),
        all_queries,
        node_cache[:, :, 0],
        codes,
    )
    hidden, narrow = attend(
        sums.reshape(4, 2, ROWS, 512),
        stats.reshape(4, 2, 8, ROWS),
        queries,
        leaf_cache,
        leaf_len[None, :],
        new_kv,
        out_weight,
        residual,
    )
    return run_experts(
        narrow, hidden, all_routes, norm_gain.reshape(16, 1, 256), router, expert_in[0], expert_out[0]
    )


def solution(mesh):
    placed = (
        P("dp", None),
        P(None, "dp", None),
        P("dp", "mp"),
        P("mp", None),
        P(),
        P(),
        P("dp", None, "mp", None),
        P("dp", "mp", None),
        P(None, "dp", "mp", None, None),
        P(None, "dp", "mp", None, None),
        P(),
        P(),
        P(),
        P(),
        P(),
        P(),
        P(),
        P(),
        P(),
        P("dp"),
        P("dp", None),
    )
    return jax.shard_map(
        shards, mesh=mesh, in_specs=placed, out_specs=P("dp", "mp"), check_vma=False
    )
```

```python
import jax
import jax.numpy as jnp
from jax import lax
from jax.experimental import pallas as pl
from jax.experimental.pallas import tpu as pltpu
from jax.sharding import PartitionSpec as P

EXPERTS = 8
PAGE = 128
ROOT_DEV = 2
BR_DEV = 8
BR_CAP = 32
E_CAP = 64

MASKED_SCORE = -1e30
NORM_EPS = 1e-05

BF = jnp.bfloat16
F32 = jnp.float32
MESH = pl.DeviceIdType.MESH
ROWS = 128
PART_ROWS = ((0, 48), (48, 48), (96, 32))
AXES = ("x", "y", "z")
ORDERS = tuple(AXES[part:] + AXES[:part] for part in range(3))


def place():
    dp = lax.axis_index("dp")
    mp = lax.axis_index("mp")
    return {"x": dp // 2, "c": dp % 2, "y": mp // 4, "z": mp % 4}


def device_of(at, **moved):
    at = {**at, **moved}
    return (at["x"] * 2 + at["c"], at["y"] * 4 + at["z"])


def step_along(at, axis, by):
    return device_of(at, **{axis: (at[axis] + by) % 4})


def greet(peers):
    barrier = pltpu.get_barrier_semaphore()
    for peer in peers:
        pl.semaphore_signal(barrier, inc=1, device_id=peer, device_id_type=MESH)
    pl.semaphore_wait(barrier, len(peers))


def remote(src, dst, sems, key, device):
    return pltpu.make_async_remote_copy(
        src_ref=src,
        dst_ref=dst,
        send_sem=sems[0].at[key],
        recv_sem=sems[1].at[key],
        device_id=device,
        device_id_type=MESH,
    )


def all_peers(at):
    return [step_along(at, axis, by) for axis in AXES for by in (1, 2, 3)] + [
        device_of(at, c=1 - at["c"])
    ]


class Link:
    def __init__(self, at, sems):
        self.sems = sems
        self.sibling = device_of(at, c=1 - at["c"])
        self.started = []

    def send(self, src, dst, key, device):
        copy = remote(src, dst, self.sems, key, device)
        copy.start()
        self.started.append(copy)

    def arrive(self, ref, key):
        remote(ref, ref, self.sems, key, self.sibling).wait_recv()

    def finish(self):
        for copy in self.started:
            copy.wait_send()


def gather_all(at, link, own_ref, buf_ref, local_sem, base, meanwhile):
    both = slice(None)
    core = at["c"]

    def slab(part, phase, value, half, plane):
        index = {"x": at["x"], "y": at["y"], "z": at["z"]}
        for axis in ORDERS[part][:phase]:
            index[axis] = slice(None)
        index[ORDERS[part][phase]] = value
        row, rows = PART_ROWS[part]
        return buf_ref.at[index["x"], plane, index["y"], index["z"], half, pl.ds(row, rows), :]

    local = pltpu.make_async_copy(own_ref, buf_ref.at[at["x"], core, at["y"], at["z"]], local_sem)
    local.start()
    for phase in range(2):
        for part in range(3):
            axis = ORDERS[part][phase]
            ref = slab(part, phase, at[axis], both, core)
            src = ref
            if phase == 0:
                row, rows = PART_ROWS[part]
                src = own_ref.at[:, pl.ds(row, rows), :]
            for by in (2, 1, 3):
                link.send(src, ref, base + (part * 2 + phase) * 3 + by - 1, step_along(at, axis, by))
        if phase == 0:
            local.wait()
        else:
            meanwhile()
        for part in range(3):
            axis = ORDERS[part][phase]
            for by in (1, 3, 2):
                ref = slab(part, phase, (at[axis] - by) % 4, both, core)
                link.arrive(ref, base + (part * 2 + phase) * 3 + by - 1)
    base += 18
    for part in range(3):
        axis = ORDERS[part][2]
        key = base + part * 8
        ref = slab(part, 2, at[axis], both, core)
        link.send(ref, ref, key, step_along(at, axis, 1))
        link.send(ref, ref, key + 1, step_along(at, axis, 3))
        link.send(ref, ref, key + 4, link.sibling)
    for part in range(3):
        axis = ORDERS[part][2]
        key = base + part * 8
        for side, by in ((0, 3), (1, 1)):
            value = (at[axis] + by) % 4
            ref = slab(part, 2, value, both, core)
            link.arrive(ref, key + side)
            half = slab(part, 2, value, side, core)
            link.send(half, half, key + 2 + side, step_along(at, axis, 1 + 2 * side))
            link.send(ref, ref, key + 5 + side, link.sibling)
    for part in range(3):
        axis = ORDERS[part][2]
        key = base + part * 8
        far = (at[axis] + 2) % 4
        for side in range(2):
            link.arrive(slab(part, 2, far, side, core), key + 2 + side)
        ref = slab(part, 2, far, both, core)
        link.send(ref, ref, key + 7, link.sibling)

    def others():
        for part in range(3):
            v = at[ORDERS[part][2]]
            for i, by in enumerate((0, 3, 1, 2)):
                link.arrive(slab(part, 2, (v + by) % 4, both, 1 - core), base + part * 8 + 4 + i)

    return others


GATHER_KEYS = 18 + 24


def ring_reduce(at, link, sum_ref, dims, orders, part_rows, relay, lands, base, finish):
    phases = len(dims)
    both = slice(None)
    parts = range(len(orders))

    def view(part, phase, value, half):
        index = dict(at)
        for axis in orders[part][phase + 1 :]:
            index[axis] = slice(None)
        index[orders[part][phase]] = value
        row, rows = part_rows[part]
        return tuple(index[axis] for axis in dims) + (half, pl.ds(row, rows), slice(None))

    def spot(part, phase, slot, *half):
        row, rows = part_rows[part]
        return (slot,) + (slice(None),) * (phases - 1 - phase) + half + (pl.ds(row, rows), slice(None))

    def accumulate(target, others):
        total = sum_ref[target].astype(F32)
        for ref, index in others:
            total += ref[index].astype(F32)
        return total

    for phase in range(phases):
        keys = [base + (part * phases + phase) * 4 for part in parts]
        if phase < relay:
            halves, fulls = lands[phase]
            for part in parts:
                axis = orders[part][phase]
                for side, by in ((0, 1), (1, 3)):
                    link.send(
                        sum_ref.at[view(part, phase, (at[axis] + 2) % 4, side)],
                        halves.at[spot(part, phase, side)],
                        keys[part] + side,
                        step_along(at, axis, by),
                    )
            for part in parts:
                axis = orders[part][phase]
                for side, by in ((0, 1), (1, 3)):
                    index = spot(part, phase, side)
                    link.arrive(halves.at[index], keys[part] + side)
                    target = view(part, phase, (at[axis] + by) % 4, side)
                    sum_ref[target] = accumulate(target, [(halves, index)]).astype(BF)
                    link.send(
                        sum_ref.at[view(part, phase, (at[axis] + by) % 4, both)],
                        fulls.at[spot(part, phase, side, both)],
                        keys[part] + 2 + side,
                        step_along(at, axis, by),
                    )
            slots, first = 2, 2
        else:
            fulls = lands[phase]
            for part in parts:
                axis = orders[part][phase]
                for by in (2, 1, 3):
                    link.send(
                        sum_ref.at[view(part, phase, (at[axis] + by) % 4, both)],
                        fulls.at[spot(part, phase, by - 1, both)],
                        keys[part] + by - 1,
                        step_along(at, axis, by),
                    )
            slots, first = 3, 0
        for part in parts:
            axis = orders[part][phase]
            for slot in range(slots):
                link.arrive(fulls.at[spot(part, phase, slot, both)], keys[part] + first + slot)
            for half in range(2):
                target = view(part, phase, at[axis], half)
                total = accumulate(target, [(fulls, spot(part, phase, slot, half)) for slot in range(slots)])
                if phase < phases - 1:
                    sum_ref[target] = total.astype(BF)
                else:
                    finish(*part_rows[part], half, total)


def expert_kernel(
    at, loads, tables_in,
    out_ref, kept_ref, own_ref,
    routes_ref, gain_ref, router_ref,
    buf_ref, code_ref, other_ref, rows_ref, gate_ref, up_ref, down_ref, act_ref, give_ref, theirs_ref, sum_ref,
    half0, full0, full1, full2,
    local_sem, send_sem, recv_sem,
):
    link = Link(at, (send_sem, recv_sem))
    core = at["c"]
    mine = lax.axis_index("dp")
    row_index = lax.broadcasted_iota(jnp.int32, (ROWS, ROWS), 0)
    lane_index = lax.broadcasted_iota(jnp.int32, (ROWS, ROWS), 1)
    upright = []

    def tables():
        for load in tables_in:
            load.wait()
        unit = (row_index == lane_index).astype(BF)
        later = (row_index < lane_index).astype(BF)
        earlier = (lane_index < row_index).astype(BF)
        first = jnp.concatenate([routes_ref[b // 2, b % 2, 0:1, :] for b in range(8)], axis=0)
        second = jnp.concatenate([routes_ref[b // 2, b % 2, 1:2, :] for b in range(8)], axis=0)
        shift = (lax.broadcasted_iota(jnp.int32, (8, ROWS), 0) // 2) % 2 * E_CAP
        hit = ((first == mine) | (second == mine)).astype(F32)
        rank = jnp.dot(hit.astype(BF), later, preferred_element_type=F32).astype(jnp.int32)
        code_ref[0:8, :] = jnp.where(hit > 0.5, rank + shift, -1)
        other_ref[...] = first + second - mine
        for expert in (mine, mine + 1 - 2 * core):
            hit = ((first == expert) | (second == expert)).astype(BF)
            there = lax.dot_general(unit, hit, BY_ROW, preferred_element_type=F32)
            rank = lax.dot_general(earlier, hit, BY_ROW, preferred_element_type=F32)
            codes = jnp.where(there > 0.5, rank, -1.0)
            upright.append(
                [jnp.where(core == 0, codes[:, 2 * b : 2 * b + 1], codes[:, 2 * b + 1 : 2 * b + 2]) for b in range(4)]
            )

    others = gather_all(at, link, own_ref, buf_ref, local_sem, 0, tables)

    def compact(plane):
        base = pl.multiple_of(plane * 256, 256)
        wanted = lax.broadcasted_iota(jnp.int32, (128, 256), 0)
        picks, answers = [], []
        for pair in range(2):
            blocks = [pl.ds(4 * pair + 2 * k + plane, 1) for k in range(2)]
            code = jnp.concatenate([code_ref[b, :] for b in blocks], axis=1)
            other = jnp.concatenate([other_ref[b, :] for b in blocks], axis=1)
            chosen = wanted == code
            picks.append(chosen.astype(BF))
            answers.append(jnp.sum(jnp.where(chosen, other, 0), axis=1, keepdims=True))
        answer = jnp.concatenate(answers, axis=0)

        def fill(y, squares):
            for z in range(4):
                pieces = []
                for pair in range(2):
                    whole = jnp.concatenate(
                        [
                            jnp.concatenate([buf_ref[2 * pair + k, plane, y, z, h] for h in range(2)], axis=1)
                            for k in range(2)
                        ],
                        axis=0,
                    )
                    pieces.append(jnp.dot(picks[pair], whole, preferred_element_type=F32))
                piece = jnp.concatenate(pieces, axis=0)
                cols = pl.ds(pl.multiple_of((y * 4 + z) * 256, 256), 256)
                rows_ref[pl.ds(base, 256), cols] = piece.astype(BF)
                piece = piece * piece
                squares += piece[:, :128] + piece[:, 128:]
            return squares

        squares = lax.fori_loop(0, 4, fill, jnp.zeros((256, 128), F32))
        scale = lax.rsqrt(jnp.sum(squares, axis=1, keepdims=True) / 4096.0 + NORM_EPS)

        def norm(y, _):
            for z in range(4):
                cols = pl.ds(pl.multiple_of((y * 4 + z) * 256, 256), 256)
                normed = rows_ref[pl.ds(base, 256), cols].astype(F32) * scale * gain_ref[y * 4 + z]
                rows_ref[pl.ds(base, 256), cols] = normed.astype(BF)
            return 0

        lax.fori_loop(0, 4, norm, 0)
        logits = lax.dot_general(
            rows_ref[pl.ds(base, 256), :], router_ref[...], BY_ROW, preferred_element_type=F32
        )
        lane = lax.broadcasted_iota(jnp.int32, logits.shape, 1)
        here = jnp.sum(jnp.where(lane == mine, logits, 0.0), axis=1, keepdims=True)
        there = jnp.sum(
            jnp.where(lane == answer, logits, 0.0), axis=1, keepdims=True
        )
        most = jnp.maximum(here, there)
        here = jnp.exp(here - most)
        there = jnp.exp(there - most)
        gate_ref[pl.ds(base, 256), :] = jnp.broadcast_to(here / (here + there), (256, 128))

    compact(core)
    others()
    compact(1 - core)
    for load in loads:
        load.wait()

    for j in range(2):
        span = slice(j * 256, (j + 1) * 256)
        gate, up = [
            lax.dot_general(rows_ref[...], up_ref[k, span, :], BY_ROW, preferred_element_type=F32)
            for k in range(2)
        ]
        act_ref[:, span] = (gate / (1.0 + jnp.exp(-gate)) * up).astype(BF)

    def project(plane, i):
        base = pl.multiple_of(plane * 256, 256)
        cols = pl.ds(pl.multiple_of(i * 256, 256), 256)
        product = jnp.dot(act_ref[pl.ds(base, 256), :], down_ref[:, cols], preferred_element_type=F32)
        return (product * gate_ref[pl.ds(base, 256), 0:1]).astype(BF)

    for group in range(4):

        def hand(k, _):
            i = group * 4 + k
            give_ref[i] = project(1 - core, i)
            return 0

        lax.fori_loop(0, 4, hand, 0)
        link.send(
            give_ref.at[pl.ds(group * 4, 4)], theirs_ref.at[pl.ds(group * 4, 4)], GATHER_KEYS + group, link.sibling
        )
    spreads = []
    for pair in range(2):
        corners = []
        for k in range(2):
            empty = jnp.zeros((ROWS, E_CAP), BF)
            lane = lax.broadcasted_iota(jnp.int32, (ROWS, E_CAP), 1).astype(F32)
            for codes in upright:
                hit = (codes[2 * pair + k] == lane).astype(BF)
                corners.append(jnp.concatenate([hit, empty] if k == 0 else [empty, hit], axis=1))
        spreads.append(
            jnp.concatenate(
                [jnp.concatenate(corners[0:2], axis=1), jnp.concatenate(corners[2:4], axis=1)], axis=0
            )
        )
    for group in range(4):
        link.arrive(theirs_ref.at[pl.ds(group * 4, 4)], GATHER_KEYS + group)

        def merge(k, _):
            i = group * 4 + k
            ours = project(core, i)
            for pair in range(2):
                rows = slice(pair * 128, (pair + 1) * 128)
                stacked = jnp.concatenate([ours[rows], theirs_ref[i, rows]], axis=0)
                spread = jnp.dot(spreads[pair], stacked, preferred_element_type=F32).astype(BF)
                for x in range(2):
                    for half in range(2):
                        sum_ref[2 * pair + x, group, k, half] = spread[
                            x * 128 : (x + 1) * 128, half * 128 : (half + 1) * 128
                        ]
            return 0

        lax.fori_loop(0, 4, merge, 0)

    def finish(row, rows, half, total):
        spot = (pl.ds(row, rows), pl.ds(half * 128, 128))
        out_ref[spot] = (kept_ref[spot] + total).astype(BF)

    ring_reduce(
        at, link, sum_ref, AXES, ORDERS, PART_ROWS, 1, ((half0, full0), full1, full2), GATHER_KEYS + 4, finish
    )
    link.finish()


LOG2E = 1.4426950408889634


def member_codes(request_ref, request_branch_ref, parent_ref, root_owner_ref, branch_owner_ref, code_ref, dp):
    def grid(shape, dim):
        return lax.broadcasted_iota(jnp.int32, shape, dim)

    def wide(ref):
        return jnp.broadcast_to(ref[...], (8, ref.shape[1]))

    def stand(matrix, row):
        return lax.dot_general(matrix.astype(BF), row.astype(BF), BY_ROW, preferred_element_type=F32)[:, 0:1]

    roots, branches, slots = root_owner_ref.shape[1], parent_ref.shape[1], request_ref.shape[1]
    square = (branches, branches)
    unit = grid(square, 0) == grid(square, 1)
    earlier = grid(square, 1) < grid(square, 0)
    owned = (wide(branch_owner_ref) == dp).astype(F32)
    branch_owned, branch_place = stand(unit, owned), stand(earlier, owned)
    parent = stand(unit, wide(parent_ref).astype(F32)).astype(jnp.int32)
    kid = jnp.sum(jnp.where((parent == parent_ref[...]) & earlier, 1.0, 0.0), axis=1, keepdims=True)
    root_owned = (wide(root_owner_ref) == dp).astype(F32)
    before = grid((roots, roots), 0) < grid((roots, roots), 1)
    root_place = jnp.dot(root_owned.astype(BF), before.astype(BF), preferred_element_type=F32)
    chosen = parent == grid((branches, roots), 1)
    parent_place = jnp.sum(jnp.where(chosen, root_place[0:1], 0.0), axis=1, keepdims=True)
    parent_owned = jnp.sum(jnp.where(chosen, root_owned[0:1], 0.0), axis=1, keepdims=True)
    root_base = jnp.where(parent_owned > 0.5, parent_place * ROWS + kid * BR_CAP, -4096.0)
    branch_base = jnp.where(branch_owned > 0.5, branch_place * BR_CAP, -4096.0)
    branch_row = wide(request_branch_ref).astype(F32).astype(BF)
    later = (grid((ROWS, ROWS), 0) < grid((ROWS, ROWS), 1)).astype(BF)
    count = jnp.zeros((branches, 1), F32)
    for block in range(slots // ROWS):
        span = slice(block * ROWS, (block + 1) * ROWS)
        asked = (grid((slots, ROWS), 0) == request_ref[0:1, span]).astype(BF)
        branch = jnp.dot(branch_row, asked, preferred_element_type=F32).astype(jnp.int32)[0:1]
        member = grid((branches, ROWS), 0) == branch
        rank = jnp.dot(member.astype(BF), later, preferred_element_type=F32) + count
        count += jnp.sum(jnp.where(member, 1.0, 0.0), axis=1, keepdims=True)
        for kind, base in enumerate((root_base, branch_base)):
            code = jnp.sum(jnp.where(member, base + rank, 0.0), axis=0, keepdims=True)
            code_ref[kind : kind + 1, span] = jnp.maximum(code, -1.0).astype(jnp.int32)


def query_kernel(
    queries_ref, routes_ref, request_ref, request_branch_ref, parent_ref, root_owner_ref, branch_owner_ref,
    all_ref, all_routes_ref, code_ref, local_sem, route_sem, send_sem, recv_sem,
):
    at = place()
    link = Link(at, (send_sem, recv_sem))
    sibling = link.sibling
    right, left = step_along(at, "x", 1), step_along(at, "x", 3)
    x, core = at["x"], at["c"]
    peers = [(by, device_of(at, x=(x + by // 2) % 4, c=(core + by) % 2)) for by in range(1, 8)]
    greet([device for _, device in peers])
    kv_head = lax.axis_index("mp") // 2
    own = queries_ref.at[:, pl.ds(pl.multiple_of(kv_head * 512, 512), 512)]
    mine = all_ref.at[x, core]
    link.send(own, mine, 0, right)
    link.send(own, mine, 1, left)
    link.send(own, mine, 4, sibling)
    local = [
        pltpu.make_async_copy(own, mine, local_sem),
        pltpu.make_async_copy(routes_ref, all_routes_ref.at[x, core], route_sem),
    ]
    for copy in local:
        copy.start()
    for by, device in peers:
        link.send(routes_ref, all_routes_ref.at[x, core], 8 + by, device)
    code_ref[...] = jnp.full_like(code_ref, -1)
    member_codes(
        request_ref, request_branch_ref, parent_ref, root_owner_ref, branch_owner_ref, code_ref, lax.axis_index("dp")
    )
    low, high, far = (x + 3) % 4, (x + 1) % 4, (x + 2) % 4
    upper, lower = pl.ds(0, 64), pl.ds(64, 64)
    from_low, from_high = all_ref.at[low, core], all_ref.at[high, core]
    link.arrive(from_low, 0)
    first = all_ref.at[low, core, upper]
    link.send(first, first, 2, right)
    link.arrive(from_high, 1)
    second = all_ref.at[high, core, lower]
    link.send(second, second, 3, left)
    link.send(from_low, from_low, 5, sibling)
    link.send(from_high, from_high, 6, sibling)
    for key, rows in ((2, upper), (3, lower)):
        ref = all_ref.at[far, core, rows]
        link.arrive(ref, key)
        link.send(ref, ref, key + 5, sibling)
    for key, ref in (
        (4, all_ref.at[x, 1 - core]),
        (5, all_ref.at[low, 1 - core]),
        (6, all_ref.at[high, 1 - core]),
        (7, all_ref.at[far, 1 - core, upper]),
        (8, all_ref.at[far, 1 - core, lower]),
    ):
        link.arrive(ref, key)
    for by in range(1, 8):
        giver = all_routes_ref.at[(x + 4 - by // 2) % 4, (core + by) % 2]
        link.arrive(giver, 8 + by)
    for copy in local:
        copy.wait()
    link.finish()


def gather_queries(queries, routes, *tables):
    return pl.pallas_call(
        query_kernel,
        out_shape=(
            jax.ShapeDtypeStruct((4, 2, ROWS, 512), BF),
            jax.ShapeDtypeStruct((4, 2, 2, ROWS), jnp.int32),
            jax.ShapeDtypeStruct((8, 1024), jnp.int32),
        ),
        in_specs=[pl.BlockSpec(memory_space=pl.ANY)] * 2 + [pl.BlockSpec(memory_space=pltpu.VMEM)] * 5,
        out_specs=(pl.BlockSpec(memory_space=pl.ANY),) * 2 + (pl.BlockSpec(memory_space=pltpu.VMEM),),
        scratch_shapes=[
            pltpu.SemaphoreType.DMA,
            pltpu.SemaphoreType.DMA,
            pltpu.SemaphoreType.DMA((16,)),
            pltpu.SemaphoreType.DMA((16,)),
        ],
        compiler_params=pltpu.CompilerParams(collective_id=3, has_side_effects=True),
        name="gather_queries",
    )(queries, routes, *(table[None, :] for table in tables))


HEAD_STEPS = 2
SCALE2 = LOG2E * 128 ** (-0.5)
BY_ROW = (((1,), (1,)), ((), ()))


def node_kernel(
    root_owner_ref, branch_owner_ref, root_pages_ref, branch_pages_ref, root_len_ref, branch_len_ref,
    all_hbm, pages_hbm, code_row_ref,
    sum_ref, stat_ref,
    query_ref, acc_ref, max_ref, total_ref, node_sum_ref, node_stat_ref, all_ref, pages_ref,
    root_id_ref, branch_id_ref, load_sem,
):
    loads = [
        pltpu.make_async_copy(all_hbm, all_ref, load_sem.at[0]),
        pltpu.make_async_copy(pages_hbm, pages_ref, load_sem.at[1]),
    ]
    for load in loads:
        load.start()
    dp = lax.axis_index("dp")
    part = lax.axis_index("mp") % 2
    lane = lax.broadcasted_iota(jnp.int32, (1, 128), 1)
    for owner_ref, id_ref in ((root_owner_ref, root_id_ref), (branch_owner_ref, branch_id_ref)):

        def scan(i, found):
            owned = owner_ref[i] == dp

            @pl.when(owned)
            def _():
                id_ref[found] = i

            return found + owned.astype(jnp.int32)

        lax.fori_loop(0, owner_ref.shape[0], scan, 0)
    loads[0].wait()
    loads[1].wait()

    def pick(kind, base, count):
        wanted = lax.broadcasted_iota(jnp.int32, (count, 1024), 0) + base
        chosen = (wanted == code_row_ref[kind : kind + 1, :]).astype(BF)
        return jnp.dot(chosen, all_ref[...], preferred_element_type=F32).astype(BF)

    def put(row, rows):
        stats = jnp.zeros((rows, 128), F32)
        for h in range(4):
            span = pl.ds(h * rows, rows)
            node_sum_ref[pl.ds(row, rows), h * 128 : (h + 1) * 128] = acc_ref[span, :].astype(BF)
            stats = jnp.where(lane == h, max_ref[span, 0:1], stats)
            stats = jnp.where(lane == 4 + h, total_ref[span, 0:1], stats)
        node_stat_ref[pl.ds(row, rows), :] = stats

    chunk = 8
    for k in range(ROOT_DEV):
        root = root_id_ref[k]
        length = root_len_ref[root]
        picked = pick(0, k * 128, 128)
        for h in range(4):
            query_ref[h * 128 : (h + 1) * 128, :] = picked[:, h * 128 : (h + 1) * 128]
        acc_ref[...] = jnp.zeros_like(acc_ref)
        max_ref[...] = jnp.full_like(max_ref, MASKED_SCORE)
        total_ref[...] = jnp.zeros_like(total_ref)
        used = (length - part * 64 + PAGE - 1) // PAGE
        steps = (used + chunk - 1) // chunk

        def body(i, _):
            ids = [root_pages_ref[root, i * chunk + j] for j in range(chunk)]
            keys = jnp.concatenate([pages_ref[0, page] for page in ids], axis=0)
            values = jnp.concatenate([pages_ref[1, page] for page in ids], axis=0)
            spot = lax.broadcasted_iota(jnp.int32, (1, chunk * 64), 1)
            spot = (i * chunk + spot // 64) * PAGE + part * 64 + spot % 64
            usable = spot < length
            for h in range(HEAD_STEPS):
                span = pl.ds(h * (512 // HEAD_STEPS), 512 // HEAD_STEPS)
                scores = lax.dot_general(query_ref[span, :], keys, BY_ROW, preferred_element_type=F32)
                scores = jnp.where(usable, scores * SCALE2, MASKED_SCORE)
                old = max_ref[span, :]
                new = jnp.maximum(old, jnp.max(scores, axis=1, keepdims=True))
                weights = jnp.exp2(scores - new[:, 0:1])
                fade = jnp.exp2(old - new)
                total_ref[span, :] = total_ref[span, :] * fade + jnp.sum(weights, axis=1, keepdims=True)
                acc_ref[span, :] = acc_ref[span, :] * fade + jnp.dot(
                    weights.astype(BF), values, preferred_element_type=F32
                )
                max_ref[span, :] = new
            return 0

        lax.fori_loop(0, steps, body, 0)
        put(k * 128, 128)

    def branch_body(b, _):
        branch = branch_id_ref[b]
        length = branch_len_ref[branch]
        picked = pick(1, b * 32, 32)
        stacked = jnp.concatenate([picked[:, h * 128 : (h + 1) * 128] for h in range(4)], axis=0)
        ids = [branch_pages_ref[j, branch] for j in range(4)]
        keys = jnp.concatenate([pages_ref[0, page] for page in ids], axis=0)
        values = jnp.concatenate([pages_ref[1, page] for page in ids], axis=0)
        spot = lax.broadcasted_iota(jnp.int32, (1, 256), 1)
        spot = (spot // 64) * PAGE + part * 64 + spot % 64
        usable = spot < length
        scores = lax.dot_general(stacked, keys, BY_ROW, preferred_element_type=F32)
        scores = jnp.where(usable, scores * SCALE2, MASKED_SCORE)
        top = jnp.max(scores, axis=1, keepdims=True)
        weights = jnp.where(usable, jnp.exp2(scores - top), 0.0)
        total = jnp.sum(weights, axis=1, keepdims=True)
        acc = jnp.dot(weights.astype(BF), values, preferred_element_type=F32)
        row = pl.multiple_of(256 + b * 32, 32)
        stats = jnp.zeros((32, 128), F32)
        for h in range(4):
            node_sum_ref[pl.ds(row, 32), h * 128 : (h + 1) * 128] = acc[h * 32 : (h + 1) * 32].astype(BF)
            stats = jnp.where(lane == h, top[h * 32 : (h + 1) * 32], stats)
            stats = jnp.where(lane == 4 + h, total[h * 32 : (h + 1) * 32], stats)
        node_stat_ref[pl.ds(row, 32), :] = stats
        return 0

    lax.fori_loop(0, BR_DEV, branch_body, 0)

    unit = lax.broadcasted_iota(jnp.int32, (ROWS, ROWS), 0) == lax.broadcasted_iota(jnp.int32, (ROWS, ROWS), 1)
    unit = unit.astype(BF)

    def spread_body(block, _):
        parts = []
        wanted = lax.broadcasted_iota(jnp.int32, (ROWS, 256), 1)
        row = code_row_ref[:, pl.ds(pl.multiple_of(block * ROWS, ROWS), ROWS)].astype(F32).astype(BF)
        codes = lax.dot_general(unit, row, BY_ROW, preferred_element_type=F32).astype(jnp.int32)
        for kind in range(2):
            code = codes[:, kind : kind + 1]
            chosen = wanted == code
            rows = slice(kind * 256, kind * 256 + 256)
            sums = jnp.dot(chosen.astype(BF), node_sum_ref[rows, :], preferred_element_type=F32)
            stats = jnp.dot(
                chosen.astype(F32),
                node_stat_ref[rows, :],
                preferred_element_type=F32,
                precision=lax.Precision.HIGHEST,
            )
            stats = jnp.where((lane < 4) & (code < 0), MASKED_SCORE, stats)
            parts.append((sums, stats))
        merged, stats = merge_blocks(parts[0], parts[1], 4)
        sum_ref[block] = merged.astype(BF)
        stat_ref[block] = stats.T[0:8]
        return 0

    lax.fori_loop(0, 8, spread_body, 0)


def merge_blocks(one, two, heads):
    sums_one, stats_one = one
    sums_two, stats_two = two
    lane = lax.broadcasted_iota(jnp.int32, (1, 128), 1)
    pieces = []
    stats = jnp.zeros_like(stats_one)
    for h in range(heads):
        span = slice(h * 128, (h + 1) * 128)
        top_one, top_two = stats_one[:, h : h + 1], stats_two[:, h : h + 1]
        top = jnp.maximum(top_one, top_two)
        factor_one, factor_two = jnp.exp2(top_one - top), jnp.exp2(top_two - top)
        pieces.append(
            sums_one[:, span].astype(F32) * factor_one + sums_two[:, span].astype(F32) * factor_two
        )
        total = stats_one[:, 4 + h : 5 + h] * factor_one + stats_two[:, 4 + h : 5 + h] * factor_two
        stats = jnp.where(lane == h, top, stats)
        stats = jnp.where(lane == 4 + h, total, stats)
    return jnp.concatenate(pieces, axis=1), stats


def node_partials(tables, all_queries, pages, codes):
    vmem, hbm = pl.BlockSpec(memory_space=pltpu.VMEM), pl.BlockSpec(memory_space=pl.ANY)
    return pl.pallas_call(
        node_kernel,
        out_shape=(
            jax.ShapeDtypeStruct((8, ROWS, 512), BF),
            jax.ShapeDtypeStruct((8, 8, ROWS), F32),
        ),
        in_specs=[pl.BlockSpec(memory_space=pltpu.SMEM)] * 6 + [hbm, hbm, vmem],
        out_specs=(vmem, vmem),
        scratch_shapes=[
            pltpu.VMEM((512, 128), BF),
            pltpu.VMEM((512, 128), F32),
            pltpu.VMEM((512, 128), F32),
            pltpu.VMEM((512, 128), F32),
            pltpu.VMEM((512, 512), BF),
            pltpu.VMEM((512, 128), F32),
            pltpu.VMEM(all_queries.shape, BF),
            pltpu.VMEM(pages.shape, BF),
            pltpu.SMEM((ROOT_DEV,), jnp.int32),
            pltpu.SMEM((BR_DEV,), jnp.int32),
            pltpu.SemaphoreType.DMA((2,)),
        ],
        compiler_params=pltpu.CompilerParams(vmem_limit_bytes=62 * 2**20),
        name="node_partials",
    )(*tables, all_queries, pages, codes)


def attend_kernel(
    at, begin,
    sum_hbm, stat_hbm, query_hbm, leaf_hbm, leaf_len_ref, fresh_hbm, weight_hbm, residual_ref,
    hidden_ref, narrow_ref,
    own_sum, own_stat, their_sum, their_stat, run_sum, run_stat, land_sum, land_stat,
    query_ref, wide_query, own_query_ref, leaf_ref, length_ref, fresh_ref, weight_ref,
    leaf_sum, leaf_stat, give_stat, side_sum, side_stat, give_sum,
    proj_ref, full1, full2, load_sem, send_sem, recv_sem,
):
    link = Link(at, (send_sem, recv_sem))
    send, arrive, sibling = link.send, link.arrive, link.sibling
    beside = {**at, "z": at["z"] + 1 - 2 * (at["z"] % 2)}
    x, core = at["x"], at["c"]
    part = at["z"] % 2
    mp = lax.axis_index("mp")
    kv_head = mp // 2

    def columns(ref, width, index):
        return ref.at[:, pl.ds(pl.multiple_of(index * width, width), width)]

    loads = [
        pltpu.make_async_copy(src, dst, load_sem.at[i])
        for i, (src, dst) in enumerate(
            (
                (columns(query_hbm, 512, kv_head), query_ref),
                (leaf_hbm.at[:, :, 0], leaf_ref),
                (sum_hbm.at[:, core], own_sum),
                (stat_hbm.at[:, core], own_stat),
                (columns(query_hbm, 256, mp), own_query_ref),
                (columns(fresh_hbm.at[0], 128, kv_head), fresh_ref.at[0]),
                (columns(fresh_hbm.at[1], 128, kv_head), fresh_ref.at[1]),
                (weight_hbm, weight_ref),
            )
        )
    ]
    for load in loads:
        load.start()
    greet(all_peers(at))
    send(sum_hbm.at[:, 1 - core], their_sum, 0, sibling)
    send(stat_hbm.at[:, 1 - core], their_stat, 1, sibling)
    lane = lax.broadcasted_iota(jnp.int32, (1, 128), 1)
    unit = lax.broadcasted_iota(jnp.int32, (ROWS, ROWS), 0) == lax.broadcasted_iota(
        jnp.int32, (ROWS, ROWS), 1
    )
    lengths_row = jnp.broadcast_to(leaf_len_ref[...], (ROWS, ROWS))
    length_ref[...] = jnp.broadcast_to(
        jnp.sum(jnp.where(unit, lengths_row, 0), axis=1, keepdims=True), (ROWS, ROWS)
    )

    def upright(stats):
        return jnp.concatenate([stats, jnp.zeros((ROWS - 8, ROWS), F32)], axis=0).T

    loads[0].wait()
    loads[1].wait()
    begin()
    wide_query[...] = query_ref[...].astype(F32)

    def leaf_group(base):
        span = pl.ds(base, 8)
        heads = [wide_query[span, h * 128 : (h + 1) * 128] for h in range(4)]
        stacked = jnp.concatenate(heads, axis=0)
        keys = leaf_ref[0, span].reshape(512, 128)
        values = leaf_ref[1, span].reshape(512, 128)
        scores = lax.dot_general(
            stacked.astype(BF), keys, BY_ROW, preferred_element_type=F32
        )
        row = lax.broadcasted_iota(jnp.int32, (32, 512), 0) % 8
        col = lax.broadcasted_iota(jnp.int32, (32, 512), 1)
        lengths = jnp.concatenate([length_ref[span, 0:1]] * 4, axis=0)
        usable = (row == col // 64) & (part * 64 + col % 64 < lengths)
        scores = jnp.where(usable, scores * SCALE2, MASKED_SCORE)
        top = jnp.max(scores, axis=1, keepdims=True)
        weights = jnp.where(usable, jnp.exp2(scores - top), 0.0)
        total = jnp.sum(weights, axis=1, keepdims=True)
        acc = jnp.dot(weights.astype(BF), values, preferred_element_type=F32)
        stats = jnp.zeros((8, 128), F32)
        for h in range(4):
            leaf_sum[span, h * 128 : (h + 1) * 128] = acc[h * 8 : (h + 1) * 8]
            stats = jnp.where(lane == h, top[h * 8 : (h + 1) * 8], stats)
            stats = jnp.where(lane == 4 + h, total[h * 8 : (h + 1) * 8], stats)
        leaf_stat[span, :] = stats

    def leaf_body(i, _):
        for k in range(4):
            leaf_group(pl.multiple_of(i * 32 + k * 8, 8))
        return 0

    lax.fori_loop(0, 4, leaf_body, 0)
    loads[2].wait()
    loads[3].wait()
    arrive(their_sum, 0)
    arrive(their_stat, 1)
    for by in (2, 1, 3):
        value = (x + by) % 4
        merged, stats = merge_blocks(
            (own_sum[value], upright(own_stat[value])), (their_sum[value], upright(their_stat[value])), 4
        )
        run_sum[by - 1] = merged.astype(BF)
        run_stat[by - 1] = stats.T[0:8]
        device = step_along(at, "x", by)
        send(run_sum.at[by - 1], land_sum.at[by - 1], 2 * by, device)
        send(run_stat.at[by - 1], land_stat.at[by - 1], 2 * by + 1, device)
    sums, stats = merge_blocks(
        (own_sum[x], upright(own_stat[x])), (their_sum[x], upright(their_stat[x])), 4
    )
    sums, stats = merge_blocks((sums, stats), (leaf_sum[...], leaf_stat[...]), 4)
    for load in loads[4:]:
        load.wait()
    fresh_key = fresh_ref[0].astype(F32)
    fresh_value = fresh_ref[1].astype(F32)
    own_scores = [
        jnp.sum(own_query_ref[:, h * 128 : (h + 1) * 128].astype(F32) * fresh_key, axis=1, keepdims=True)
        * SCALE2
        for h in range(2)
    ]
    for by in (1, 3, 2):
        arrive(land_sum.at[by - 1], 2 * by)
        arrive(land_stat.at[by - 1], 2 * by + 1)
        sums, stats = merge_blocks((sums, stats), (land_sum[by - 1], upright(land_stat[by - 1])), 4)
    first = part == 0
    give_sum[...] = jnp.where(first, sums[:, 256:], sums[:, :256]).astype(BF)
    give_stat[...] = stats.T[0:8]
    send(give_sum, side_sum, 10, device_of(beside))
    send(give_stat, side_stat, 11, device_of(beside))
    kept = jnp.where(first, sums[:, :256], sums[:, 256:])
    arrive(side_sum, 10)
    arrive(side_stat, 11)
    theirs = upright(side_stat[...])
    pieces = []
    for h in range(2):
        span = slice(h * 128, (h + 1) * 128)

        def column(from_stats, offset):
            return jnp.where(
                first,
                from_stats[:, offset + h : offset + h + 1],
                from_stats[:, offset + 2 + h : offset + 3 + h],
            )

        top_one, top_two = column(stats, 0), column(theirs, 0)
        top = jnp.maximum(jnp.maximum(top_one, top_two), own_scores[h])
        factor_one, factor_two = jnp.exp2(top_one - top), jnp.exp2(top_two - top)
        factor_own = jnp.exp2(own_scores[h] - top)
        weighted = (
            kept[:, span] * factor_one
            + side_sum[:, span].astype(F32) * factor_two
            + factor_own * fresh_value
        )
        total = column(stats, 4) * factor_one + column(theirs, 4) * factor_two + factor_own
        pieces.append((weighted / total).astype(BF))
    attended = jnp.concatenate(pieces, axis=1)
    for i in range(16):
        product = jnp.dot(
            attended, weight_ref[:, i * 256 : (i + 1) * 256], preferred_element_type=F32
        ).astype(BF)
        for half in range(2):
            proj_ref[i // 4, i % 4, half] = product[:, half * 128 : (half + 1) * 128]

    def finish(row, rows, half, total):
        cols = pl.ds(half * 128, 128)
        total += residual_ref[pl.ds(row, rows), cols].astype(F32)
        hidden_ref[pl.ds(row, rows), cols] = total
        narrow_ref[half, pl.ds(row, rows), :] = total.astype(BF)

    ring_reduce(
        at, link, proj_ref, ("y", "z"), (("y", "z"), ("z", "y")), ((0, 64), (64, 64)), 0,
        (full1, full2), 12, finish,
    )
    link.finish()


def layer_kernel(*refs):
    ins, out_ref = refs[:13], refs[13]
    attend_refs = refs[14 : 14 + ATTEND_SCRATCH]
    hidden_ref, narrow_ref, tables_sem, weight_sem = refs[14 + ATTEND_SCRATCH : 18 + ATTEND_SCRATCH]
    expert_refs = refs[18 + ATTEND_SCRATCH :]
    at = place()
    tables = [
        pltpu.make_async_copy(ins[8 + i], expert_refs[i], tables_sem.at[i]) for i in range(3)
    ]
    loads = [
        pltpu.make_async_copy(ins[11 + i], expert_refs[EXPERT_WEIGHTS + i], weight_sem.at[i]) for i in range(2)
    ]

    def begin():
        for load in tables + loads:
            load.start()

    attend_kernel(at, begin, *ins[:8], hidden_ref, narrow_ref, *attend_refs)
    expert_kernel(at, loads, tables, out_ref, hidden_ref, narrow_ref, *expert_refs)


ATTEND_SCRATCH = 27
EXPERT_WEIGHTS = 8


def attend_and_route(
    sums, stats, queries, leaf, leaf_len, fresh, out_weight, residual, routes, gain, router, expert_in, expert_out
):
    keys = GATHER_KEYS + 4 + 36
    vmem, hbm = pl.BlockSpec(memory_space=pltpu.VMEM), pl.BlockSpec(memory_space=pl.ANY)
    return pl.pallas_call(
        layer_kernel,
        out_shape=jax.ShapeDtypeStruct((ROWS, 256), BF),
        in_specs=[hbm, hbm, hbm, hbm, vmem, hbm, hbm, vmem] + [hbm] * 5,
        out_specs=vmem,
        scratch_shapes=[
            pltpu.VMEM((4, ROWS, 512), BF),
            pltpu.VMEM((4, 8, ROWS), F32),
            pltpu.VMEM((4, ROWS, 512), BF),
            pltpu.VMEM((4, 8, ROWS), F32),
            pltpu.VMEM((3, ROWS, 512), BF),
            pltpu.VMEM((3, 8, ROWS), F32),
            pltpu.VMEM((3, ROWS, 512), BF),
            pltpu.VMEM((3, 8, ROWS), F32),
            pltpu.VMEM((ROWS, 512), BF),
            pltpu.VMEM((ROWS, 512), F32),
            pltpu.VMEM((ROWS, 256), BF),
            pltpu.VMEM((2, ROWS, 64, 128), BF),
            pltpu.VMEM((ROWS, ROWS), jnp.int32),
            pltpu.VMEM((2, ROWS, 128), BF),
            pltpu.VMEM((256, 4096), BF),
            pltpu.VMEM((ROWS, 512), F32),
            pltpu.VMEM((ROWS, 128), F32),
            pltpu.VMEM((8, ROWS), F32),
            pltpu.VMEM((ROWS, 256), BF),
            pltpu.VMEM((8, ROWS), F32),
            pltpu.VMEM((ROWS, 256), BF),
            pltpu.VMEM((4, 4, 2, ROWS, 128), BF),
            pltpu.VMEM((3, 4, 2, ROWS, 128), BF),
            pltpu.VMEM((3, 2, ROWS, 128), BF),
            pltpu.SemaphoreType.DMA((8,)),
            pltpu.SemaphoreType.DMA((28,)),
            pltpu.SemaphoreType.DMA((28,)),
            pltpu.VMEM((ROWS, 256), F32),
            pltpu.VMEM((2, ROWS, 128), BF),
            pltpu.SemaphoreType.DMA((3,)),
            pltpu.SemaphoreType.DMA((2,)),
            pltpu.VMEM(routes.shape, jnp.int32),
            pltpu.VMEM(gain.shape, F32),
            pltpu.VMEM(router.shape, BF),
            pltpu.VMEM((4, 2, 4, 4, 2, ROWS, 128), BF),
            pltpu.VMEM((8, ROWS), jnp.int32),
            pltpu.VMEM((8, ROWS), jnp.int32),
            pltpu.VMEM((512, 4096), BF),
            pltpu.VMEM((512, 128), F32),
            pltpu.VMEM(expert_in.shape, BF),
            pltpu.VMEM(expert_out.shape, BF),
            pltpu.VMEM((512, 512), BF),
            pltpu.VMEM((16, 256, 256), BF),
            pltpu.VMEM((16, 256, 256), BF),
            pltpu.VMEM((4, 4, 4, 2, ROWS, 128), BF),
            pltpu.VMEM((2, 4, 4, ROWS, 128), BF),
            pltpu.VMEM((2, 4, 4, 2, ROWS, 128), BF),
            pltpu.VMEM((3, 4, 2, ROWS, 128), BF),
            pltpu.VMEM((3, 2, ROWS, 128), BF),
            pltpu.SemaphoreType.DMA,
            pltpu.SemaphoreType.DMA((keys,)),
            pltpu.SemaphoreType.DMA((keys,)),
        ],
        compiler_params=pltpu.CompilerParams(
            collective_id=1, has_side_effects=True, vmem_limit_bytes=62 * 2**20
        ),
        name="attend_and_route",
    )(sums, stats, queries, leaf, leaf_len, fresh, out_weight, residual, routes, gain, router, expert_in, expert_out)


def shards(
    queries,
    new_kv,
    residual,
    out_weight,
    norm_gain,
    router,
    expert_in,
    expert_out,
    node_cache,
    leaf_cache,
    slot_request,
    request_branch,
    branch_parent,
    root_owner,
    branch_owner,
    root_pages,
    branch_pages,
    root_len,
    branch_len,
    leaf_len,
    routes,
):
    all_queries, all_routes, codes = gather_queries(
        queries,
        routes.T,
        slot_request,
        request_branch,
        branch_parent,
        root_owner,
        branch_owner,
    )
    sums, stats = node_partials(
        (root_owner, branch_owner, root_pages, branch_pages.T, root_len, branch_len),
        all_queries.reshape(8 * ROWS, 512),
        node_cache[:, :, 0],
        codes,
    )
    return attend_and_route(
        sums.reshape(4, 2, ROWS, 512),
        stats.reshape(4, 2, 8, ROWS),
        queries,
        leaf_cache,
        leaf_len[None, :],
        new_kv,
        out_weight,
        residual,
        all_routes,
        norm_gain.reshape(16, 1, 256),
        router.T,
        expert_in[0],
        expert_out[0],
    )


def solution(mesh):
    placed = (
        P("dp", None),
        P(None, "dp", None),
        P("dp", "mp"),
        P("mp", None),
        P(),
        P(),
        P("dp", None, "mp", None),
        P("dp", "mp", None),
        P(None, "dp", "mp", None, None),
        P(None, "dp", "mp", None, None),
        P(),
        P(),
        P(),
        P(),
        P(),
        P(),
        P(),
        P(),
        P(),
        P("dp"),
        P("dp", None),
    )
    return jax.shard_map(
        shards, mesh=mesh, in_specs=placed, out_specs=P("dp", "mp"), check_vma=False
    )
```

```python
import jax
import jax.numpy as jnp
from jax import lax
from jax.experimental import pallas as pl
from jax.experimental.pallas import tpu as pltpu
from jax.sharding import PartitionSpec as P

EXPERTS = 8
PAGE = 128
ROOT_DEV = 2
BR_DEV = 8
BR_CAP = 32
E_CAP = 64

MASKED_SCORE = -1e30
NORM_EPS = 1e-05

BF = jnp.bfloat16
F32 = jnp.float32
MESH = pl.DeviceIdType.MESH
ROWS = 128
PART_ROWS = ((0, 48), (48, 48), (96, 32))
AXES = ("x", "y", "z")
ORDERS = tuple(AXES[part:] + AXES[:part] for part in range(3))


def place():
    dp = lax.axis_index("dp")
    mp = lax.axis_index("mp")
    return {"x": dp // 2, "c": dp % 2, "y": mp // 4, "z": mp % 4}


def device_of(at, **moved):
    at = {**at, **moved}
    return (at["x"] * 2 + at["c"], at["y"] * 4 + at["z"])


def step_along(at, axis, by):
    return device_of(at, **{axis: (at[axis] + by) % 4})


def greet(peers):
    barrier = pltpu.get_barrier_semaphore()
    for peer in peers:
        pl.semaphore_signal(barrier, inc=1, device_id=peer, device_id_type=MESH)
    pl.semaphore_wait(barrier, len(peers))


def remote(src, dst, sems, key, device):
    return pltpu.make_async_remote_copy(
        src_ref=src,
        dst_ref=dst,
        send_sem=sems[0].at[key],
        recv_sem=sems[1].at[key],
        device_id=device,
        device_id_type=MESH,
    )


def all_peers(at):
    return [step_along(at, axis, by) for axis in AXES for by in (1, 2, 3)] + [
        device_of(at, c=1 - at["c"])
    ]


class Link:
    def __init__(self, at, sems):
        self.sems = sems
        self.sibling = device_of(at, c=1 - at["c"])
        self.started = []

    def send(self, src, dst, key, device):
        copy = remote(src, dst, self.sems, key, device)
        copy.start()
        self.started.append(copy)

    def arrive(self, ref, key):
        remote(ref, ref, self.sems, key, self.sibling).wait_recv()

    def finish(self):
        for copy in self.started:
            copy.wait_send()


def gather_all(at, link, own_ref, buf_ref, local_sem, base, meanwhile):
    both = slice(None)
    core = at["c"]

    def slab(part, phase, value, half, plane):
        index = {"x": at["x"], "y": at["y"], "z": at["z"]}
        for axis in ORDERS[part][:phase]:
            index[axis] = slice(None)
        index[ORDERS[part][phase]] = value
        row, rows = PART_ROWS[part]
        return buf_ref.at[index["x"], plane, index["y"], index["z"], half, pl.ds(row, rows), :]

    local = pltpu.make_async_copy(own_ref, buf_ref.at[at["x"], core, at["y"], at["z"]], local_sem)
    local.start()
    for phase in range(2):
        for part in range(3):
            axis = ORDERS[part][phase]
            ref = slab(part, phase, at[axis], both, core)
            src = ref
            if phase == 0:
                row, rows = PART_ROWS[part]
                src = own_ref.at[:, pl.ds(row, rows), :]
            for by in (2, 1, 3):
                link.send(src, ref, base + (part * 2 + phase) * 3 + by - 1, step_along(at, axis, by))
        if phase == 0:
            local.wait()
        else:
            meanwhile()
        for part in range(3):
            axis = ORDERS[part][phase]
            for by in (1, 3, 2):
                ref = slab(part, phase, (at[axis] - by) % 4, both, core)
                link.arrive(ref, base + (part * 2 + phase) * 3 + by - 1)
    base += 18
    for part in range(3):
        axis = ORDERS[part][2]
        key = base + part * 8
        ref = slab(part, 2, at[axis], both, core)
        link.send(ref, ref, key, step_along(at, axis, 1))
        link.send(ref, ref, key + 1, step_along(at, axis, 3))
        link.send(ref, ref, key + 4, link.sibling)
    for part in range(3):
        axis = ORDERS[part][2]
        key = base + part * 8
        for side, by in ((0, 3), (1, 1)):
            value = (at[axis] + by) % 4
            ref = slab(part, 2, value, both, core)
            link.arrive(ref, key + side)
            half = slab(part, 2, value, side, core)
            link.send(half, half, key + 2 + side, step_along(at, axis, 1 + 2 * side))
            link.send(ref, ref, key + 5 + side, link.sibling)
    for part in range(3):
        axis = ORDERS[part][2]
        key = base + part * 8
        far = (at[axis] + 2) % 4
        for side in range(2):
            link.arrive(slab(part, 2, far, side, core), key + 2 + side)
        ref = slab(part, 2, far, both, core)
        link.send(ref, ref, key + 7, link.sibling)

    def others():
        for part in range(3):
            v = at[ORDERS[part][2]]
            for i, by in enumerate((0, 3, 1, 2)):
                link.arrive(slab(part, 2, (v + by) % 4, both, 1 - core), base + part * 8 + 4 + i)

    return others


GATHER_KEYS = 18 + 24


def ring_reduce(at, link, sum_ref, dims, orders, part_rows, relay, lands, base, finish):
    phases = len(dims)
    both = slice(None)
    parts = range(len(orders))

    def view(part, phase, value, half):
        index = dict(at)
        for axis in orders[part][phase + 1 :]:
            index[axis] = slice(None)
        index[orders[part][phase]] = value
        row, rows = part_rows[part]
        return tuple(index[axis] for axis in dims) + (half, pl.ds(row, rows), slice(None))

    def spot(part, phase, slot, *half):
        row, rows = part_rows[part]
        return (slot,) + (slice(None),) * (phases - 1 - phase) + half + (pl.ds(row, rows), slice(None))

    def accumulate(target, others):
        total = sum_ref[target].astype(F32)
        for ref, index in others:
            total += ref[index].astype(F32)
        return total

    for phase in range(phases):
        keys = [base + (part * phases + phase) * 4 for part in parts]
        if phase < relay:
            halves, fulls = lands[phase]
            for part in parts:
                axis = orders[part][phase]
                for side, by in ((0, 1), (1, 3)):
                    link.send(
                        sum_ref.at[view(part, phase, (at[axis] + 2) % 4, side)],
                        halves.at[spot(part, phase, side)],
                        keys[part] + side,
                        step_along(at, axis, by),
                    )
            for part in parts:
                axis = orders[part][phase]
                for side, by in ((0, 1), (1, 3)):
                    index = spot(part, phase, side)
                    link.arrive(halves.at[index], keys[part] + side)
                    target = view(part, phase, (at[axis] + by) % 4, side)
                    sum_ref[target] = accumulate(target, [(halves, index)]).astype(BF)
                    link.send(
                        sum_ref.at[view(part, phase, (at[axis] + by) % 4, both)],
                        fulls.at[spot(part, phase, side, both)],
                        keys[part] + 2 + side,
                        step_along(at, axis, by),
                    )
            slots, first = 2, 2
        else:
            fulls = lands[phase]
            for part in parts:
                axis = orders[part][phase]
                for by in (2, 1, 3):
                    link.send(
                        sum_ref.at[view(part, phase, (at[axis] + by) % 4, both)],
                        fulls.at[spot(part, phase, by - 1, both)],
                        keys[part] + by - 1,
                        step_along(at, axis, by),
                    )
            slots, first = 3, 0
        for part in parts:
            axis = orders[part][phase]
            for slot in range(slots):
                link.arrive(fulls.at[spot(part, phase, slot, both)], keys[part] + first + slot)
            for half in range(2):
                target = view(part, phase, at[axis], half)
                total = accumulate(target, [(fulls, spot(part, phase, slot, half)) for slot in range(slots)])
                if phase < phases - 1:
                    sum_ref[target] = total.astype(BF)
                else:
                    finish(*part_rows[part], half, total)


def expert_kernel(
    at, loads, tables_in,
    out_ref, kept_ref, own_ref,
    routes_ref, gain_ref, router_ref,
    buf_ref, code_ref, other_ref, rows_ref, gate_ref, up_ref, down_ref, act_ref, give_ref, theirs_ref, sum_ref,
    half0, full0, full1, full2,
    local_sem, send_sem, recv_sem,
):
    link = Link(at, (send_sem, recv_sem))
    core = at["c"]
    mine = lax.axis_index("dp")
    row_index = lax.broadcasted_iota(jnp.int32, (ROWS, ROWS), 0)
    lane_index = lax.broadcasted_iota(jnp.int32, (ROWS, ROWS), 1)
    upright = []

    def tables():
        for load in tables_in:
            load.wait()
        unit = (row_index == lane_index).astype(BF)
        later = (row_index < lane_index).astype(BF)
        earlier = (lane_index < row_index).astype(BF)
        first = jnp.concatenate([routes_ref[b // 2, b % 2, 0:1, :] for b in range(8)], axis=0)
        second = jnp.concatenate([routes_ref[b // 2, b % 2, 1:2, :] for b in range(8)], axis=0)
        shift = (lax.broadcasted_iota(jnp.int32, (8, ROWS), 0) // 2) % 2 * E_CAP
        hit = ((first == mine) | (second == mine)).astype(F32)
        rank = jnp.dot(hit.astype(BF), later, preferred_element_type=F32).astype(jnp.int32)
        code_ref[0:8, :] = jnp.where(hit > 0.5, rank + shift, -1)
        other_ref[...] = first + second - mine
        for expert in (mine, mine + 1 - 2 * core):
            hit = ((first == expert) | (second == expert)).astype(BF)
            there = lax.dot_general(unit, hit, BY_ROW, preferred_element_type=F32)
            rank = lax.dot_general(earlier, hit, BY_ROW, preferred_element_type=F32)
            codes = jnp.where(there > 0.5, rank, -1.0)
            upright.append(
                [jnp.where(core == 0, codes[:, 2 * b : 2 * b + 1], codes[:, 2 * b + 1 : 2 * b + 2]) for b in range(4)]
            )

    others = gather_all(at, link, own_ref, buf_ref, local_sem, 0, tables)

    def compact(plane):
        base = pl.multiple_of(plane * 256, 256)
        wanted = lax.broadcasted_iota(jnp.int32, (128, 256), 0)
        picks, answers = [], []
        for pair in range(2):
            blocks = [pl.ds(4 * pair + 2 * k + plane, 1) for k in range(2)]
            code = jnp.concatenate([code_ref[b, :] for b in blocks], axis=1)
            other = jnp.concatenate([other_ref[b, :] for b in blocks], axis=1)
            chosen = wanted == code
            picks.append(chosen.astype(BF))
            answers.append(jnp.sum(jnp.where(chosen, other, 0), axis=1, keepdims=True))
        answer = jnp.concatenate(answers, axis=0)

        def fill(y, squares):
            for z in range(4):
                pieces = []
                for pair in range(2):
                    whole = jnp.concatenate(
                        [
                            jnp.concatenate([buf_ref[2 * pair + k, plane, y, z, h] for h in range(2)], axis=1)
                            for k in range(2)
                        ],
                        axis=0,
                    )
                    pieces.append(jnp.dot(picks[pair], whole, preferred_element_type=F32))
                piece = jnp.concatenate(pieces, axis=0)
                cols = pl.ds(pl.multiple_of((y * 4 + z) * 256, 256), 256)
                rows_ref[pl.ds(base, 256), cols] = piece.astype(BF)
                piece = piece * piece
                squares += piece[:, :128] + piece[:, 128:]
            return squares

        squares = lax.fori_loop(0, 4, fill, jnp.zeros((256, 128), F32))
        scale = lax.rsqrt(jnp.sum(squares, axis=1, keepdims=True) / 4096.0 + NORM_EPS)

        def norm(y, _):
            for z in range(4):
                cols = pl.ds(pl.multiple_of((y * 4 + z) * 256, 256), 256)
                normed = rows_ref[pl.ds(base, 256), cols].astype(F32) * scale * gain_ref[y * 4 + z]
                rows_ref[pl.ds(base, 256), cols] = normed.astype(BF)
            return 0

        lax.fori_loop(0, 4, norm, 0)
        logits = lax.dot_general(
            rows_ref[pl.ds(base, 256), :], router_ref[...], BY_ROW, preferred_element_type=F32
        )
        lane = lax.broadcasted_iota(jnp.int32, logits.shape, 1)
        here = jnp.sum(jnp.where(lane == mine, logits, 0.0), axis=1, keepdims=True)
        there = jnp.sum(
            jnp.where(lane == answer, logits, 0.0), axis=1, keepdims=True
        )
        most = jnp.maximum(here, there)
        here = jnp.exp(here - most)
        there = jnp.exp(there - most)
        gate_ref[pl.ds(base, 256), :] = jnp.broadcast_to(here / (here + there), (256, 128))

    def activate(plane):
        base = pl.multiple_of(plane * 256, 256)
        for j in range(2):
            span = slice(j * 256, (j + 1) * 256)
            gate, up = [
                lax.dot_general(
                    rows_ref[pl.ds(base, 256), :], up_ref[k, span, :], BY_ROW, preferred_element_type=F32
                )
                for k in range(2)
            ]
            act_ref[pl.ds(base, 256), span] = (gate / (1.0 + jnp.exp(-gate)) * up).astype(BF)

    compact(core)
    for load in loads:
        load.wait()
    activate(core)
    others()
    compact(1 - core)
    activate(1 - core)

    def project(plane, i):
        base = pl.multiple_of(plane * 256, 256)
        cols = pl.ds(pl.multiple_of(i * 256, 256), 256)
        product = jnp.dot(act_ref[pl.ds(base, 256), :], down_ref[:, cols], preferred_element_type=F32)
        return (product * gate_ref[pl.ds(base, 256), 0:1]).astype(BF)

    for group in range(4):

        def hand(k, _):
            i = group * 4 + k
            give_ref[i] = project(1 - core, i)
            return 0

        lax.fori_loop(0, 4, hand, 0)
        link.send(
            give_ref.at[pl.ds(group * 4, 4)], theirs_ref.at[pl.ds(group * 4, 4)], GATHER_KEYS + group, link.sibling
        )
    spreads = []
    for pair in range(2):
        corners = []
        for k in range(2):
            empty = jnp.zeros((ROWS, E_CAP), BF)
            lane = lax.broadcasted_iota(jnp.int32, (ROWS, E_CAP), 1).astype(F32)
            for codes in upright:
                hit = (codes[2 * pair + k] == lane).astype(BF)
                corners.append(jnp.concatenate([hit, empty] if k == 0 else [empty, hit], axis=1))
        spreads.append(
            jnp.concatenate(
                [jnp.concatenate(corners[0:2], axis=1), jnp.concatenate(corners[2:4], axis=1)], axis=0
            )
        )
    for group in range(4):
        link.arrive(theirs_ref.at[pl.ds(group * 4, 4)], GATHER_KEYS + group)

        def merge(k, _):
            i = group * 4 + k
            ours = project(core, i)
            for pair in range(2):
                rows = slice(pair * 128, (pair + 1) * 128)
                stacked = jnp.concatenate([ours[rows], theirs_ref[i, rows]], axis=0)
                spread = jnp.dot(spreads[pair], stacked, preferred_element_type=F32).astype(BF)
                for x in range(2):
                    for half in range(2):
                        sum_ref[2 * pair + x, group, k, half] = spread[
                            x * 128 : (x + 1) * 128, half * 128 : (half + 1) * 128
                        ]
            return 0

        lax.fori_loop(0, 4, merge, 0)

    def finish(row, rows, half, total):
        spot = (pl.ds(row, rows), pl.ds(half * 128, 128))
        out_ref[spot] = (kept_ref[spot] + total).astype(BF)

    ring_reduce(
        at, link, sum_ref, AXES, ORDERS, PART_ROWS, 1, ((half0, full0), full1, full2), GATHER_KEYS + 4, finish
    )
    link.finish()


LOG2E = 1.4426950408889634


def member_codes(request_ref, request_branch_ref, parent_ref, root_owner_ref, branch_owner_ref, code_ref, dp):
    def grid(shape, dim):
        return lax.broadcasted_iota(jnp.int32, shape, dim)

    def wide(ref):
        return jnp.broadcast_to(ref[...], (8, ref.shape[1]))

    def stand(matrix, row):
        return lax.dot_general(matrix.astype(BF), row.astype(BF), BY_ROW, preferred_element_type=F32)[:, 0:1]

    roots, branches, slots = root_owner_ref.shape[1], parent_ref.shape[1], request_ref.shape[1]
    square = (branches, branches)
    unit = grid(square, 0) == grid(square, 1)
    earlier = grid(square, 1) < grid(square, 0)
    owned = (wide(branch_owner_ref) == dp).astype(F32)
    branch_owned, branch_place = stand(unit, owned), stand(earlier, owned)
    parent = stand(unit, wide(parent_ref).astype(F32)).astype(jnp.int32)
    kid = jnp.sum(jnp.where((parent == parent_ref[...]) & earlier, 1.0, 0.0), axis=1, keepdims=True)
    root_owned = (wide(root_owner_ref) == dp).astype(F32)
    before = grid((roots, roots), 0) < grid((roots, roots), 1)
    root_place = jnp.dot(root_owned.astype(BF), before.astype(BF), preferred_element_type=F32)
    chosen = parent == grid((branches, roots), 1)
    parent_place = jnp.sum(jnp.where(chosen, root_place[0:1], 0.0), axis=1, keepdims=True)
    parent_owned = jnp.sum(jnp.where(chosen, root_owned[0:1], 0.0), axis=1, keepdims=True)
    root_base = jnp.where(parent_owned > 0.5, parent_place * ROWS + kid * BR_CAP, -4096.0)
    branch_base = jnp.where(branch_owned > 0.5, branch_place * BR_CAP, -4096.0)
    branch_row = wide(request_branch_ref).astype(F32).astype(BF)
    later = (grid((ROWS, ROWS), 0) < grid((ROWS, ROWS), 1)).astype(BF)
    count = jnp.zeros((branches, 1), F32)
    for block in range(slots // ROWS):
        span = slice(block * ROWS, (block + 1) * ROWS)
        asked = (grid((slots, ROWS), 0) == request_ref[0:1, span]).astype(BF)
        branch = jnp.dot(branch_row, asked, preferred_element_type=F32).astype(jnp.int32)[0:1]
        member = grid((branches, ROWS), 0) == branch
        rank = jnp.dot(member.astype(BF), later, preferred_element_type=F32) + count
        count += jnp.sum(jnp.where(member, 1.0, 0.0), axis=1, keepdims=True)
        for kind, base in enumerate((root_base, branch_base)):
            code = jnp.sum(jnp.where(member, base + rank, 0.0), axis=0, keepdims=True)
            code_ref[kind : kind + 1, span] = jnp.maximum(code, -1.0).astype(jnp.int32)


def query_kernel(
    queries_ref, routes_ref, request_ref, request_branch_ref, parent_ref, root_owner_ref, branch_owner_ref,
    all_ref, all_routes_ref, code_ref, local_sem, route_sem, send_sem, recv_sem,
):
    at = place()
    link = Link(at, (send_sem, recv_sem))
    sibling = link.sibling
    right, left = step_along(at, "x", 1), step_along(at, "x", 3)
    x, core = at["x"], at["c"]
    peers = [(by, device_of(at, x=(x + by // 2) % 4, c=(core + by) % 2)) for by in range(1, 8)]
    greet([device for _, device in peers])
    kv_head = lax.axis_index("mp") // 2
    own = queries_ref.at[:, pl.ds(pl.multiple_of(kv_head * 512, 512), 512)]
    mine = all_ref.at[x, core]
    link.send(own, mine, 0, right)
    link.send(own, mine, 1, left)
    link.send(own, mine, 4, sibling)
    local = [
        pltpu.make_async_copy(own, mine, local_sem),
        pltpu.make_async_copy(routes_ref, all_routes_ref.at[x, core], route_sem),
    ]
    for copy in local:
        copy.start()
    for by, device in peers:
        link.send(routes_ref, all_routes_ref.at[x, core], 8 + by, device)
    code_ref[...] = jnp.full_like(code_ref, -1)
    member_codes(
        request_ref, request_branch_ref, parent_ref, root_owner_ref, branch_owner_ref, code_ref, lax.axis_index("dp")
    )
    low, high, far = (x + 3) % 4, (x + 1) % 4, (x + 2) % 4
    upper, lower = pl.ds(0, 64), pl.ds(64, 64)
    from_low, from_high = all_ref.at[low, core], all_ref.at[high, core]
    link.arrive(from_low, 0)
    first = all_ref.at[low, core, upper]
    link.send(first, first, 2, right)
    link.arrive(from_high, 1)
    second = all_ref.at[high, core, lower]
    link.send(second, second, 3, left)
    link.send(from_low, from_low, 5, sibling)
    link.send(from_high, from_high, 6, sibling)
    for key, rows in ((2, upper), (3, lower)):
        ref = all_ref.at[far, core, rows]
        link.arrive(ref, key)
        link.send(ref, ref, key + 5, sibling)
    for key, ref in (
        (4, all_ref.at[x, 1 - core]),
        (5, all_ref.at[low, 1 - core]),
        (6, all_ref.at[high, 1 - core]),
        (7, all_ref.at[far, 1 - core, upper]),
        (8, all_ref.at[far, 1 - core, lower]),
    ):
        link.arrive(ref, key)
    for by in range(1, 8):
        giver = all_routes_ref.at[(x + 4 - by // 2) % 4, (core + by) % 2]
        link.arrive(giver, 8 + by)
    for copy in local:
        copy.wait()
    link.finish()


def gather_queries(queries, routes, *tables):
    return pl.pallas_call(
        query_kernel,
        out_shape=(
            jax.ShapeDtypeStruct((4, 2, ROWS, 512), BF),
            jax.ShapeDtypeStruct((4, 2, 2, ROWS), jnp.int32),
            jax.ShapeDtypeStruct((8, 1024), jnp.int32),
        ),
        in_specs=[pl.BlockSpec(memory_space=pl.ANY)] * 2 + [pl.BlockSpec(memory_space=pltpu.VMEM)] * 5,
        out_specs=(pl.BlockSpec(memory_space=pl.ANY),) * 2 + (pl.BlockSpec(memory_space=pltpu.VMEM),),
        scratch_shapes=[
            pltpu.SemaphoreType.DMA,
            pltpu.SemaphoreType.DMA,
            pltpu.SemaphoreType.DMA((16,)),
            pltpu.SemaphoreType.DMA((16,)),
        ],
        compiler_params=pltpu.CompilerParams(collective_id=3, has_side_effects=True),
        name="gather_queries",
    )(queries, routes, *(table[None, :] for table in tables))


HEAD_STEPS = 1
SCALE2 = LOG2E * 128 ** (-0.5)
BY_ROW = (((1,), (1,)), ((), ()))


def node_kernel(
    root_owner_ref, branch_owner_ref, root_pages_ref, branch_pages_ref, root_len_ref, branch_len_ref,
    all_hbm, pages_hbm, code_row_ref,
    sum_ref, stat_ref,
    query_ref, acc_ref, max_ref, total_ref, node_sum_ref, node_stat_ref, picked_ref, all_ref, pages_ref,
    root_id_ref, branch_id_ref, load_sem,
):
    loads = [
        pltpu.make_async_copy(all_hbm, all_ref, load_sem.at[0]),
        pltpu.make_async_copy(pages_hbm, pages_ref, load_sem.at[1]),
    ]
    for load in loads:
        load.start()
    dp = lax.axis_index("dp")
    part = lax.axis_index("mp") % 2
    lane = lax.broadcasted_iota(jnp.int32, (1, 128), 1)
    for owner_ref, id_ref in ((root_owner_ref, root_id_ref), (branch_owner_ref, branch_id_ref)):

        def scan(i, found):
            owned = owner_ref[i] == dp

            @pl.when(owned)
            def _():
                id_ref[found] = i

            return found + owned.astype(jnp.int32)

        lax.fori_loop(0, owner_ref.shape[0], scan, 0)
    loads[0].wait()
    loads[1].wait()

    for kind in range(2):
        wanted = lax.broadcasted_iota(jnp.int32, (256, 1024), 0)
        chosen = (wanted == code_row_ref[kind : kind + 1, :]).astype(BF)
        picked_ref[kind * 256 : kind * 256 + 256, :] = jnp.dot(
            chosen, all_ref[...], preferred_element_type=F32
        ).astype(BF)

    def keep_stats(row, rows, stats):
        for i in range(3):
            piece = stats.astype(BF)
            node_stat_ref[i, pl.ds(row, rows), :] = piece
            stats = stats - piece.astype(F32)

    def put(row, rows):
        stats = jnp.zeros((rows, 128), F32)
        for h in range(4):
            span = pl.ds(h * rows, rows)
            node_sum_ref[pl.ds(row, rows), h * 128 : (h + 1) * 128] = acc_ref[span, :].astype(BF)
            stats = jnp.where(lane == h, max_ref[span, 0:1], stats)
            stats = jnp.where(lane == 4 + h, total_ref[span, 0:1], stats)
        keep_stats(row, rows, stats)

    chunk = 8
    for k in range(ROOT_DEV):
        root = root_id_ref[k]
        length = root_len_ref[root]
        for h in range(4):
            query_ref[h * 128 : (h + 1) * 128, :] = picked_ref[k * 128 : (k + 1) * 128, h * 128 : (h + 1) * 128]
        acc_ref[...] = jnp.zeros_like(acc_ref)
        max_ref[...] = jnp.full_like(max_ref, MASKED_SCORE)
        total_ref[...] = jnp.zeros_like(total_ref)
        used = (length - part * 64 + PAGE - 1) // PAGE
        steps = (used + chunk - 1) // chunk

        def body(i, _):
            ids = [root_pages_ref[root, i * chunk + j] for j in range(chunk)]
            keys = jnp.concatenate([pages_ref[0, page] for page in ids], axis=0)
            values = jnp.concatenate([pages_ref[1, page] for page in ids], axis=0)
            spot = lax.broadcasted_iota(jnp.int32, (1, chunk * 64), 1)
            spot = (i * chunk + spot // 64) * PAGE + part * 64 + spot % 64
            usable = spot < length
            for h in range(HEAD_STEPS):
                span = pl.ds(h * (512 // HEAD_STEPS), 512 // HEAD_STEPS)
                scores = lax.dot_general(query_ref[span, :], keys, BY_ROW, preferred_element_type=F32)
                scores = jnp.where(usable, scores * SCALE2, MASKED_SCORE)
                old = max_ref[span, :]
                new = jnp.maximum(old, jnp.max(scores, axis=1, keepdims=True))
                weights = jnp.exp2(scores - new[:, 0:1])
                fade = jnp.exp2(old - new)
                total_ref[span, :] = total_ref[span, :] * fade + jnp.sum(weights, axis=1, keepdims=True)
                acc_ref[span, :] = acc_ref[span, :] * fade + jnp.dot(
                    weights.astype(BF), values, preferred_element_type=F32
                )
                max_ref[span, :] = new
            return 0

        lax.fori_loop(0, steps, body, 0)
        put(k * 128, 128)

    def branch_work(b):
        branch = branch_id_ref[b]
        length = branch_len_ref[branch]
        row = pl.multiple_of(256 + b * 32, 32)
        picked = picked_ref[pl.ds(row, 32), :]
        stacked = jnp.concatenate([picked[:, h * 128 : (h + 1) * 128] for h in range(4)], axis=0)
        ids = [branch_pages_ref[j, branch] for j in range(4)]
        keys = jnp.concatenate([pages_ref[0, page] for page in ids], axis=0)
        values = jnp.concatenate([pages_ref[1, page] for page in ids], axis=0)
        spot = lax.broadcasted_iota(jnp.int32, (1, 256), 1)
        spot = (spot // 64) * PAGE + part * 64 + spot % 64
        usable = spot < length
        scores = lax.dot_general(stacked, keys, BY_ROW, preferred_element_type=F32)
        scores = jnp.where(usable, scores * SCALE2, MASKED_SCORE)
        top = jnp.max(scores, axis=1, keepdims=True)
        weights = jnp.where(usable, jnp.exp2(scores - top), 0.0)
        total = jnp.sum(weights, axis=1, keepdims=True)
        acc = jnp.dot(weights.astype(BF), values, preferred_element_type=F32)
        stats = jnp.zeros((32, 128), F32)
        for h in range(4):
            node_sum_ref[pl.ds(row, 32), h * 128 : (h + 1) * 128] = acc[h * 32 : (h + 1) * 32].astype(BF)
            stats = jnp.where(lane == h, top[h * 32 : (h + 1) * 32], stats)
            stats = jnp.where(lane == 4 + h, total[h * 32 : (h + 1) * 32], stats)
        keep_stats(row, 32, stats)

    def branch_body(i, _):
        for k in range(4):
            branch_work(i * 4 + k)
        return 0

    lax.fori_loop(0, BR_DEV // 4, branch_body, 0)

    unit = lax.broadcasted_iota(jnp.int32, (ROWS, ROWS), 0) == lax.broadcasted_iota(jnp.int32, (ROWS, ROWS), 1)
    unit = unit.astype(BF)

    def spread_work(block):
        parts = []
        wanted = lax.broadcasted_iota(jnp.int32, (ROWS, 256), 1)
        row = code_row_ref[:, pl.ds(pl.multiple_of(block * ROWS, ROWS), ROWS)].astype(F32).astype(BF)
        codes = lax.dot_general(unit, row, BY_ROW, preferred_element_type=F32).astype(jnp.int32)
        for kind in range(2):
            code = codes[:, kind : kind + 1]
            chosen = wanted == code
            rows = slice(kind * 256, kind * 256 + 256)
            sums = jnp.dot(chosen.astype(BF), node_sum_ref[rows, :], preferred_element_type=F32)
            stats = sum(
                jnp.dot(chosen.astype(BF), node_stat_ref[i, rows, :], preferred_element_type=F32)
                for i in (2, 1, 0)
            )
            stats = jnp.where((lane < 4) & (code < 0), MASKED_SCORE, stats)
            parts.append((sums, stats))
        merged, stats = merge_blocks(parts[0], parts[1], 4)
        sum_ref[block] = merged.astype(BF)
        stat_ref[block] = stats.T[0:8]

    def spread_body(i, _):
        for k in range(2):
            spread_work(i * 2 + k)
        return 0

    lax.fori_loop(0, 4, spread_body, 0)


def merge_blocks(one, two, heads):
    sums_one, stats_one = one
    sums_two, stats_two = two
    lane = lax.broadcasted_iota(jnp.int32, (1, 128), 1)
    top = jnp.maximum(stats_one, stats_two)
    factor_one, factor_two = jnp.exp2(stats_one - top), jnp.exp2(stats_two - top)
    total = stats_one * pltpu.roll(factor_one, 4, 1) + stats_two * pltpu.roll(factor_two, 4, 1)
    stats = jnp.where(lane < 4, top, jnp.where(lane < 8, total, 0.0))
    pieces = []
    for h in range(heads):
        span = slice(h * 128, (h + 1) * 128)
        pieces.append(
            sums_one[:, span].astype(F32) * factor_one[:, h : h + 1]
            + sums_two[:, span].astype(F32) * factor_two[:, h : h + 1]
        )
    return jnp.concatenate(pieces, axis=1), stats


def node_partials(tables, all_queries, pages, codes):
    vmem, hbm = pl.BlockSpec(memory_space=pltpu.VMEM), pl.BlockSpec(memory_space=pl.ANY)
    return pl.pallas_call(
        node_kernel,
        out_shape=(
            jax.ShapeDtypeStruct((8, ROWS, 512), BF),
            jax.ShapeDtypeStruct((8, 8, ROWS), F32),
        ),
        in_specs=[pl.BlockSpec(memory_space=pltpu.SMEM)] * 6 + [hbm, hbm, vmem],
        out_specs=(vmem, vmem),
        scratch_shapes=[
            pltpu.VMEM((512, 128), BF),
            pltpu.VMEM((512, 128), F32),
            pltpu.VMEM((512, 128), F32),
            pltpu.VMEM((512, 128), F32),
            pltpu.VMEM((512, 512), BF),
            pltpu.VMEM((3, 512, 128), BF),
            pltpu.VMEM((512, 512), BF),
            pltpu.VMEM(all_queries.shape, BF),
            pltpu.VMEM(pages.shape, BF),
            pltpu.SMEM((ROOT_DEV,), jnp.int32),
            pltpu.SMEM((BR_DEV,), jnp.int32),
            pltpu.SemaphoreType.DMA((2,)),
        ],
        compiler_params=pltpu.CompilerParams(vmem_limit_bytes=62 * 2**20),
        name="node_partials",
    )(*tables, all_queries, pages, codes)


def attend_kernel(
    at, begin,
    sum_hbm, stat_hbm, query_hbm, leaf_hbm, leaf_len_ref, fresh_hbm, weight_hbm, residual_ref,
    hidden_ref, narrow_ref,
    own_sum, own_stat, their_sum, their_stat, run_sum, run_stat, land_sum, land_stat,
    query_ref, wide_query, own_query_ref, leaf_ref, length_ref, fresh_ref, weight_ref,
    leaf_sum, leaf_stat, give_stat, side_sum, side_stat, give_sum,
    proj_ref, full1, full2, load_sem, send_sem, recv_sem,
):
    link = Link(at, (send_sem, recv_sem))
    send, arrive, sibling = link.send, link.arrive, link.sibling
    beside = {**at, "z": at["z"] + 1 - 2 * (at["z"] % 2)}
    x, core = at["x"], at["c"]
    part = at["z"] % 2
    mp = lax.axis_index("mp")
    kv_head = mp // 2

    def columns(ref, width, index):
        return ref.at[:, pl.ds(pl.multiple_of(index * width, width), width)]

    loads = [
        pltpu.make_async_copy(src, dst, load_sem.at[i])
        for i, (src, dst) in enumerate(
            (
                (columns(query_hbm, 512, kv_head), query_ref),
                (leaf_hbm.at[:, :, 0], leaf_ref),
                (sum_hbm.at[:, core], own_sum),
                (stat_hbm.at[:, core], own_stat),
                (columns(query_hbm, 256, mp), own_query_ref),
                (columns(fresh_hbm.at[0], 128, kv_head), fresh_ref.at[0]),
                (columns(fresh_hbm.at[1], 128, kv_head), fresh_ref.at[1]),
                (weight_hbm, weight_ref),
            )
        )
    ]
    for load in loads:
        load.start()
    greet(all_peers(at))
    send(sum_hbm.at[:, 1 - core], their_sum, 0, sibling)
    send(stat_hbm.at[:, 1 - core], their_stat, 1, sibling)
    lane = lax.broadcasted_iota(jnp.int32, (1, 128), 1)
    unit = lax.broadcasted_iota(jnp.int32, (ROWS, ROWS), 0) == lax.broadcasted_iota(
        jnp.int32, (ROWS, ROWS), 1
    )
    lengths_row = jnp.broadcast_to(leaf_len_ref[...], (ROWS, ROWS))
    length_ref[...] = jnp.broadcast_to(
        jnp.sum(jnp.where(unit, lengths_row, 0), axis=1, keepdims=True), (ROWS, ROWS)
    )

    def upright(stats):
        return jnp.concatenate([stats, jnp.zeros((ROWS - 8, ROWS), F32)], axis=0).T

    loads[0].wait()
    loads[1].wait()
    begin()
    wide_query[...] = query_ref[...].astype(F32)

    def leaf_group(base):
        span = pl.ds(base, 8)
        heads = [wide_query[span, h * 128 : (h + 1) * 128] for h in range(4)]
        stacked = jnp.concatenate(heads, axis=0)
        keys = leaf_ref[0, span].reshape(512, 128)
        values = leaf_ref[1, span].reshape(512, 128)
        scores = lax.dot_general(
            stacked.astype(BF), keys, BY_ROW, preferred_element_type=F32
        )
        row = lax.broadcasted_iota(jnp.int32, (32, 512), 0) % 8
        col = lax.broadcasted_iota(jnp.int32, (32, 512), 1)
        lengths = jnp.concatenate([length_ref[span, 0:1]] * 4, axis=0)
        usable = (row == col // 64) & (part * 64 + col % 64 < lengths)
        scores = jnp.where(usable, scores * SCALE2, MASKED_SCORE)
        top = jnp.max(scores, axis=1, keepdims=True)
        weights = jnp.where(usable, jnp.exp2(scores - top), 0.0)
        total = jnp.sum(weights, axis=1, keepdims=True)
        acc = jnp.dot(weights.astype(BF), values, preferred_element_type=F32)
        stats = jnp.zeros((8, 128), F32)
        for h in range(4):
            leaf_sum[span, h * 128 : (h + 1) * 128] = acc[h * 8 : (h + 1) * 8]
            stats = jnp.where(lane == h, top[h * 8 : (h + 1) * 8], stats)
            stats = jnp.where(lane == 4 + h, total[h * 8 : (h + 1) * 8], stats)
        leaf_stat[span, :] = stats

    def leaf_body(i, _):
        for k in range(4):
            leaf_group(pl.multiple_of(i * 32 + k * 8, 8))
        return 0

    lax.fori_loop(0, 4, leaf_body, 0)
    loads[2].wait()
    loads[3].wait()
    arrive(their_sum, 0)
    arrive(their_stat, 1)
    for by in (2, 1, 3):
        value = (x + by) % 4
        merged, stats = merge_blocks(
            (own_sum[value], upright(own_stat[value])), (their_sum[value], upright(their_stat[value])), 4
        )
        run_sum[by - 1] = merged.astype(BF)
        run_stat[by - 1] = stats.T[0:8]
        device = step_along(at, "x", by)
        send(run_sum.at[by - 1], land_sum.at[by - 1], 2 * by, device)
        send(run_stat.at[by - 1], land_stat.at[by - 1], 2 * by + 1, device)
    sums, stats = merge_blocks(
        (own_sum[x], upright(own_stat[x])), (their_sum[x], upright(their_stat[x])), 4
    )
    sums, stats = merge_blocks((sums, stats), (leaf_sum[...], leaf_stat[...]), 4)
    for load in loads[4:]:
        load.wait()
    fresh_key = fresh_ref[0].astype(F32)
    fresh_value = fresh_ref[1].astype(F32)
    own_scores = [
        jnp.sum(own_query_ref[:, h * 128 : (h + 1) * 128].astype(F32) * fresh_key, axis=1, keepdims=True)
        * SCALE2
        for h in range(2)
    ]
    for by in (1, 3, 2):
        arrive(land_sum.at[by - 1], 2 * by)
        arrive(land_stat.at[by - 1], 2 * by + 1)
        sums, stats = merge_blocks((sums, stats), (land_sum[by - 1], upright(land_stat[by - 1])), 4)
    first = part == 0
    give_sum[...] = jnp.where(first, sums[:, 256:], sums[:, :256]).astype(BF)
    give_stat[...] = stats.T[0:8]
    send(give_sum, side_sum, 10, device_of(beside))
    send(give_stat, side_stat, 11, device_of(beside))
    kept = jnp.where(first, sums[:, :256], sums[:, 256:])
    arrive(side_sum, 10)
    arrive(side_stat, 11)
    theirs = upright(side_stat[...])
    pieces = []
    for h in range(2):
        span = slice(h * 128, (h + 1) * 128)

        def column(from_stats, offset):
            return jnp.where(
                first,
                from_stats[:, offset + h : offset + h + 1],
                from_stats[:, offset + 2 + h : offset + 3 + h],
            )

        top_one, top_two = column(stats, 0), column(theirs, 0)
        top = jnp.maximum(jnp.maximum(top_one, top_two), own_scores[h])
        factor_one, factor_two = jnp.exp2(top_one - top), jnp.exp2(top_two - top)
        factor_own = jnp.exp2(own_scores[h] - top)
        weighted = (
            kept[:, span] * factor_one
            + side_sum[:, span].astype(F32) * factor_two
            + factor_own * fresh_value
        )
        total = column(stats, 4) * factor_one + column(theirs, 4) * factor_two + factor_own
        pieces.append((weighted / total).astype(BF))
    attended = jnp.concatenate(pieces, axis=1)
    for i in range(16):
        product = jnp.dot(
            attended, weight_ref[:, i * 256 : (i + 1) * 256], preferred_element_type=F32
        ).astype(BF)
        for half in range(2):
            proj_ref[i // 4, i % 4, half] = product[:, half * 128 : (half + 1) * 128]

    def finish(row, rows, half, total):
        cols = pl.ds(half * 128, 128)
        total += residual_ref[pl.ds(row, rows), cols].astype(F32)
        hidden_ref[pl.ds(row, rows), cols] = total
        narrow_ref[half, pl.ds(row, rows), :] = total.astype(BF)

    ring_reduce(
        at, link, proj_ref, ("y", "z"), (("y", "z"), ("z", "y")), ((0, 64), (64, 64)), 0,
        (full1, full2), 12, finish,
    )
    link.finish()


def layer_kernel(*refs):
    ins, out_ref = refs[:13], refs[13]
    attend_refs = refs[14 : 14 + ATTEND_SCRATCH]
    hidden_ref, narrow_ref, tables_sem, weight_sem = refs[14 + ATTEND_SCRATCH : 18 + ATTEND_SCRATCH]
    expert_refs = refs[18 + ATTEND_SCRATCH :]
    at = place()
    tables = [
        pltpu.make_async_copy(ins[8 + i], expert_refs[i], tables_sem.at[i]) for i in range(3)
    ]
    loads = [
        pltpu.make_async_copy(ins[11 + i], expert_refs[EXPERT_WEIGHTS + i], weight_sem.at[i]) for i in range(2)
    ]

    def begin():
        for load in tables + loads:
            load.start()

    attend_kernel(at, begin, *ins[:8], hidden_ref, narrow_ref, *attend_refs)
    expert_kernel(at, loads, tables, out_ref, hidden_ref, narrow_ref, *expert_refs)


ATTEND_SCRATCH = 27
EXPERT_WEIGHTS = 8


def attend_and_route(
    sums, stats, queries, leaf, leaf_len, fresh, out_weight, residual, routes, gain, router, expert_in, expert_out
):
    keys = GATHER_KEYS + 4 + 36
    vmem, hbm = pl.BlockSpec(memory_space=pltpu.VMEM), pl.BlockSpec(memory_space=pl.ANY)
    return pl.pallas_call(
        layer_kernel,
        out_shape=jax.ShapeDtypeStruct((ROWS, 256), BF),
        in_specs=[hbm, hbm, hbm, hbm, vmem, hbm, hbm, vmem] + [hbm] * 5,
        out_specs=vmem,
        scratch_shapes=[
            pltpu.VMEM((4, ROWS, 512), BF),
            pltpu.VMEM((4, 8, ROWS), F32),
            pltpu.VMEM((4, ROWS, 512), BF),
            pltpu.VMEM((4, 8, ROWS), F32),
            pltpu.VMEM((3, ROWS, 512), BF),
            pltpu.VMEM((3, 8, ROWS), F32),
            pltpu.VMEM((3, ROWS, 512), BF),
            pltpu.VMEM((3, 8, ROWS), F32),
            pltpu.VMEM((ROWS, 512), BF),
            pltpu.VMEM((ROWS, 512), F32),
            pltpu.VMEM((ROWS, 256), BF),
            pltpu.VMEM((2, ROWS, 64, 128), BF),
            pltpu.VMEM((ROWS, ROWS), jnp.int32),
            pltpu.VMEM((2, ROWS, 128), BF),
            pltpu.VMEM((256, 4096), BF),
            pltpu.VMEM((ROWS, 512), F32),
            pltpu.VMEM((ROWS, 128), F32),
            pltpu.VMEM((8, ROWS), F32),
            pltpu.VMEM((ROWS, 256), BF),
            pltpu.VMEM((8, ROWS), F32),
            pltpu.VMEM((ROWS, 256), BF),
            pltpu.VMEM((4, 4, 2, ROWS, 128), BF),
            pltpu.VMEM((3, 4, 2, ROWS, 128), BF),
            pltpu.VMEM((3, 2, ROWS, 128), BF),
            pltpu.SemaphoreType.DMA((8,)),
            pltpu.SemaphoreType.DMA((28,)),
            pltpu.SemaphoreType.DMA((28,)),
            pltpu.VMEM((ROWS, 256), F32),
            pltpu.VMEM((2, ROWS, 128), BF),
            pltpu.SemaphoreType.DMA((3,)),
            pltpu.SemaphoreType.DMA((2,)),
            pltpu.VMEM(routes.shape, jnp.int32),
            pltpu.VMEM(gain.shape, F32),
            pltpu.VMEM(router.shape, BF),
            pltpu.VMEM((4, 2, 4, 4, 2, ROWS, 128), BF),
            pltpu.VMEM((8, ROWS), jnp.int32),
            pltpu.VMEM((8, ROWS), jnp.int32),
            pltpu.VMEM((512, 4096), BF),
            pltpu.VMEM((512, 128), F32),
            pltpu.VMEM(expert_in.shape, BF),
            pltpu.VMEM(expert_out.shape, BF),
            pltpu.VMEM((512, 512), BF),
            pltpu.VMEM((16, 256, 256), BF),
            pltpu.VMEM((16, 256, 256), BF),
            pltpu.VMEM((4, 4, 4, 2, ROWS, 128), BF),
            pltpu.VMEM((2, 4, 4, ROWS, 128), BF),
            pltpu.VMEM((2, 4, 4, 2, ROWS, 128), BF),
            pltpu.VMEM((3, 4, 2, ROWS, 128), BF),
            pltpu.VMEM((3, 2, ROWS, 128), BF),
            pltpu.SemaphoreType.DMA,
            pltpu.SemaphoreType.DMA((keys,)),
            pltpu.SemaphoreType.DMA((keys,)),
        ],
        compiler_params=pltpu.CompilerParams(
            collective_id=1, has_side_effects=True, vmem_limit_bytes=62 * 2**20
        ),
        name="attend_and_route",
    )(sums, stats, queries, leaf, leaf_len, fresh, out_weight, residual, routes, gain, router, expert_in, expert_out)


def shards(
    queries,
    new_kv,
    residual,
    out_weight,
    norm_gain,
    router,
    expert_in,
    expert_out,
    node_cache,
    leaf_cache,
    slot_request,
    request_branch,
    branch_parent,
    root_owner,
    branch_owner,
    root_pages,
    branch_pages,
    root_len,
    branch_len,
    leaf_len,
    routes,
):
    all_queries, all_routes, codes = gather_queries(
        queries,
        routes.T,
        slot_request,
        request_branch,
        branch_parent,
        root_owner,
        branch_owner,
    )
    sums, stats = node_partials(
        (root_owner, branch_owner, root_pages, branch_pages.T, root_len, branch_len),
        all_queries.reshape(8 * ROWS, 512),
        node_cache[:, :, 0],
        codes,
    )
    return attend_and_route(
        sums.reshape(4, 2, ROWS, 512),
        stats.reshape(4, 2, 8, ROWS),
        queries,
        leaf_cache,
        leaf_len[None, :],
        new_kv,
        out_weight,
        residual,
        all_routes,
        norm_gain.reshape(16, 1, 256),
        router.T,
        expert_in[0],
        expert_out[0],
    )


def solution(mesh):
    placed = (
        P("dp", None),
        P(None, "dp", None),
        P("dp", "mp"),
        P("mp", None),
        P(),
        P(),
        P("dp", None, "mp", None),
        P("dp", "mp", None),
        P(None, "dp", "mp", None, None),
        P(None, "dp", "mp", None, None),
        P(),
        P(),
        P(),
        P(),
        P(),
        P(),
        P(),
        P(),
        P(),
        P("dp"),
        P("dp", None),
    )
    return jax.shard_map(
        shards, mesh=mesh, in_specs=placed, out_specs=P("dp", "mp"), check_vma=False
    )
```

```python
import jax
import jax.numpy as jnp
from jax import lax
from jax.experimental import pallas as pl
from jax.experimental.pallas import tpu as pltpu
from jax.sharding import PartitionSpec as P

EXPERTS = 8
PAGE = 128
ROOT_DEV = 2
BR_DEV = 8
BR_CAP = 32
E_CAP = 64

MASKED_SCORE = -1e30
NORM_EPS = 1e-05

BF = jnp.bfloat16
F32 = jnp.float32
MESH = pl.DeviceIdType.MESH
ROWS = 128
PART_ROWS = ((0, 48), (48, 48), (96, 32))
AXES = ("x", "y", "z")
ORDERS = tuple(AXES[part:] + AXES[:part] for part in range(3))


def place():
    dp = lax.axis_index("dp")
    mp = lax.axis_index("mp")
    return {"x": dp // 2, "c": dp % 2, "y": mp // 4, "z": mp % 4}


def device_of(at, **moved):
    at = {**at, **moved}
    return (at["x"] * 2 + at["c"], at["y"] * 4 + at["z"])


def step_along(at, axis, by):
    return device_of(at, **{axis: (at[axis] + by) % 4})


def greet(peers):
    barrier = pltpu.get_barrier_semaphore()
    for peer in peers:
        pl.semaphore_signal(barrier, inc=1, device_id=peer, device_id_type=MESH)
    pl.semaphore_wait(barrier, len(peers))


def remote(src, dst, sems, key, device):
    return pltpu.make_async_remote_copy(
        src_ref=src,
        dst_ref=dst,
        send_sem=sems[0].at[key],
        recv_sem=sems[1].at[key],
        device_id=device,
        device_id_type=MESH,
    )


def all_peers(at):
    return [step_along(at, axis, by) for axis in AXES for by in (1, 2, 3)] + [
        device_of(at, c=1 - at["c"])
    ]


class Link:
    def __init__(self, at, sems):
        self.sems = sems
        self.sibling = device_of(at, c=1 - at["c"])
        self.started = []

    def send(self, src, dst, key, device):
        copy = remote(src, dst, self.sems, key, device)
        copy.start()
        self.started.append(copy)

    def arrive(self, ref, key):
        remote(ref, ref, self.sems, key, self.sibling).wait_recv()

    def finish(self):
        for copy in self.started:
            copy.wait_send()


def gather_all(at, link, own_ref, buf_ref, local_sem, base, meanwhile):
    both = slice(None)
    core = at["c"]

    def slab(part, phase, value, half, plane):
        index = {"x": at["x"], "y": at["y"], "z": at["z"]}
        for axis in ORDERS[part][:phase]:
            index[axis] = slice(None)
        index[ORDERS[part][phase]] = value
        row, rows = PART_ROWS[part]
        return buf_ref.at[index["x"], plane, index["y"], index["z"], half, pl.ds(row, rows), :]

    local = pltpu.make_async_copy(own_ref, buf_ref.at[at["x"], core, at["y"], at["z"]], local_sem)
    local.start()
    for phase in range(2):
        for part in range(3):
            axis = ORDERS[part][phase]
            ref = slab(part, phase, at[axis], both, core)
            src = ref
            if phase == 0:
                row, rows = PART_ROWS[part]
                src = own_ref.at[:, pl.ds(row, rows), :]
            for by in (2, 1, 3):
                link.send(src, ref, base + (part * 2 + phase) * 3 + by - 1, step_along(at, axis, by))
        if phase == 0:
            local.wait()
        else:
            meanwhile()
        for part in range(3):
            axis = ORDERS[part][phase]
            for by in (1, 3, 2):
                ref = slab(part, phase, (at[axis] - by) % 4, both, core)
                link.arrive(ref, base + (part * 2 + phase) * 3 + by - 1)
    base += 18
    for part in range(3):
        axis = ORDERS[part][2]
        key = base + part * 8
        ref = slab(part, 2, at[axis], both, core)
        link.send(ref, ref, key, step_along(at, axis, 1))
        link.send(ref, ref, key + 1, step_along(at, axis, 3))
        link.send(ref, ref, key + 4, link.sibling)
    for part in range(3):
        axis = ORDERS[part][2]
        key = base + part * 8
        for side, by in ((0, 3), (1, 1)):
            value = (at[axis] + by) % 4
            ref = slab(part, 2, value, both, core)
            link.arrive(ref, key + side)
            half = slab(part, 2, value, side, core)
            link.send(half, half, key + 2 + side, step_along(at, axis, 1 + 2 * side))
            link.send(ref, ref, key + 5 + side, link.sibling)
    for part in range(3):
        axis = ORDERS[part][2]
        key = base + part * 8
        far = (at[axis] + 2) % 4
        for side in range(2):
            link.arrive(slab(part, 2, far, side, core), key + 2 + side)
        ref = slab(part, 2, far, both, core)
        link.send(ref, ref, key + 7, link.sibling)

    def others():
        for part in range(3):
            v = at[ORDERS[part][2]]
            for i, by in enumerate((0, 3, 1, 2)):
                link.arrive(slab(part, 2, (v + by) % 4, both, 1 - core), base + part * 8 + 4 + i)

    return others


GATHER_KEYS = 18 + 24


def ring_reduce(at, link, sum_ref, dims, orders, part_rows, relay, lands, base, finish):
    phases = len(dims)
    both = slice(None)
    parts = range(len(orders))

    def view(part, phase, value, half):
        index = dict(at)
        for axis in orders[part][phase + 1 :]:
            index[axis] = slice(None)
        index[orders[part][phase]] = value
        row, rows = part_rows[part]
        return tuple(index[axis] for axis in dims) + (half, pl.ds(row, rows), slice(None))

    def spot(part, phase, slot, *half):
        row, rows = part_rows[part]
        return (slot,) + (slice(None),) * (phases - 1 - phase) + half + (pl.ds(row, rows), slice(None))

    def accumulate(target, others):
        total = sum_ref[target].astype(F32)
        for ref, index in others:
            total += ref[index].astype(F32)
        return total

    for phase in range(phases):
        keys = [base + (part * phases + phase) * 4 for part in parts]
        if phase < relay:
            halves, fulls = lands[phase]
            for part in parts:
                axis = orders[part][phase]
                for side, by in ((0, 1), (1, 3)):
                    link.send(
                        sum_ref.at[view(part, phase, (at[axis] + 2) % 4, side)],
                        halves.at[spot(part, phase, side)],
                        keys[part] + side,
                        step_along(at, axis, by),
                    )
            for part in parts:
                axis = orders[part][phase]
                for side, by in ((0, 1), (1, 3)):
                    index = spot(part, phase, side)
                    link.arrive(halves.at[index], keys[part] + side)
                    target = view(part, phase, (at[axis] + by) % 4, side)
                    sum_ref[target] = accumulate(target, [(halves, index)]).astype(BF)
                    link.send(
                        sum_ref.at[view(part, phase, (at[axis] + by) % 4, both)],
                        fulls.at[spot(part, phase, side, both)],
                        keys[part] + 2 + side,
                        step_along(at, axis, by),
                    )
            slots, first = 2, 2
        else:
            fulls = lands[phase]
            for part in parts:
                axis = orders[part][phase]
                for by in (2, 1, 3):
                    link.send(
                        sum_ref.at[view(part, phase, (at[axis] + by) % 4, both)],
                        fulls.at[spot(part, phase, by - 1, both)],
                        keys[part] + by - 1,
                        step_along(at, axis, by),
                    )
            slots, first = 3, 0
        for part in parts:
            axis = orders[part][phase]
            for slot in range(slots):
                link.arrive(fulls.at[spot(part, phase, slot, both)], keys[part] + first + slot)
            for half in range(2):
                target = view(part, phase, at[axis], half)
                total = accumulate(target, [(fulls, spot(part, phase, slot, half)) for slot in range(slots)])
                if phase < phases - 1:
                    sum_ref[target] = total.astype(BF)
                else:
                    finish(*part_rows[part], half, total)


def expert_kernel(
    at, loads, tables_in,
    out_ref, kept_ref, own_ref,
    routes_ref, gain_ref, router_ref,
    buf_ref, code_ref, other_ref, rows_ref, gate_ref, up_ref, down_ref, act_ref, give_ref, theirs_ref, sum_ref,
    half0, full0, full1, full2,
    local_sem, send_sem, recv_sem,
):
    link = Link(at, (send_sem, recv_sem))
    core = at["c"]
    mine = lax.axis_index("dp")
    row_index = lax.broadcasted_iota(jnp.int32, (ROWS, ROWS), 0)
    lane_index = lax.broadcasted_iota(jnp.int32, (ROWS, ROWS), 1)
    upright = []

    def tables():
        for load in tables_in:
            load.wait()
        unit = (row_index == lane_index).astype(BF)
        later = (row_index < lane_index).astype(BF)
        earlier = (lane_index < row_index).astype(BF)
        first = jnp.concatenate([routes_ref[b // 2, b % 2, 0:1, :] for b in range(8)], axis=0)
        second = jnp.concatenate([routes_ref[b // 2, b % 2, 1:2, :] for b in range(8)], axis=0)
        shift = (lax.broadcasted_iota(jnp.int32, (8, ROWS), 0) // 2) % 2 * E_CAP
        hit = ((first == mine) | (second == mine)).astype(F32)
        rank = jnp.dot(hit.astype(BF), later, preferred_element_type=F32).astype(jnp.int32)
        code_ref[0:8, :] = jnp.where(hit > 0.5, rank + shift, -1)
        other_ref[...] = first + second - mine
        for expert in (mine, mine + 1 - 2 * core):
            hit = ((first == expert) | (second == expert)).astype(BF)
            there = lax.dot_general(unit, hit, BY_ROW, preferred_element_type=F32)
            rank = lax.dot_general(earlier, hit, BY_ROW, preferred_element_type=F32)
            codes = jnp.where(there > 0.5, rank, -1.0)
            upright.append(
                [jnp.where(core == 0, codes[:, 2 * b : 2 * b + 1], codes[:, 2 * b + 1 : 2 * b + 2]) for b in range(4)]
            )

    others = gather_all(at, link, own_ref, buf_ref, local_sem, 0, tables)

    def compact(plane):
        base = pl.multiple_of(plane * 256, 256)
        wanted = lax.broadcasted_iota(jnp.int32, (128, 256), 0)
        picks, answers = [], []
        for pair in range(2):
            blocks = [pl.ds(4 * pair + 2 * k + plane, 1) for k in range(2)]
            code = jnp.concatenate([code_ref[b, :] for b in blocks], axis=1)
            other = jnp.concatenate([other_ref[b, :] for b in blocks], axis=1)
            chosen = wanted == code
            picks.append(chosen.astype(BF))
            answers.append(jnp.sum(jnp.where(chosen, other, 0), axis=1, keepdims=True))
        answer = jnp.concatenate(answers, axis=0)

        def fill(y, squares):
            for z in range(4):
                pieces = []
                for pair in range(2):
                    whole = jnp.concatenate(
                        [
                            jnp.concatenate([buf_ref[2 * pair + k, plane, y, z, h] for h in range(2)], axis=1)
                            for k in range(2)
                        ],
                        axis=0,
                    )
                    pieces.append(jnp.dot(picks[pair], whole, preferred_element_type=F32))
                piece = jnp.concatenate(pieces, axis=0)
                cols = pl.ds(pl.multiple_of((y * 4 + z) * 256, 256), 256)
                rows_ref[pl.ds(base, 256), cols] = piece.astype(BF)
                piece = piece * piece
                squares += piece[:, :128] + piece[:, 128:]
            return squares

        squares = lax.fori_loop(0, 4, fill, jnp.zeros((256, 128), F32))
        scale = lax.rsqrt(jnp.sum(squares, axis=1, keepdims=True) / 4096.0 + NORM_EPS)

        def norm(y, _):
            for z in range(4):
                cols = pl.ds(pl.multiple_of((y * 4 + z) * 256, 256), 256)
                normed = rows_ref[pl.ds(base, 256), cols].astype(F32) * scale * gain_ref[y * 4 + z]
                rows_ref[pl.ds(base, 256), cols] = normed.astype(BF)
            return 0

        lax.fori_loop(0, 4, norm, 0)
        logits = lax.dot_general(
            rows_ref[pl.ds(base, 256), :], router_ref[...], BY_ROW, preferred_element_type=F32
        )
        lane = lax.broadcasted_iota(jnp.int32, logits.shape, 1)
        here = jnp.sum(jnp.where(lane == mine, logits, 0.0), axis=1, keepdims=True)
        there = jnp.sum(
            jnp.where(lane == answer, logits, 0.0), axis=1, keepdims=True
        )
        most = jnp.maximum(here, there)
        here = jnp.exp(here - most)
        there = jnp.exp(there - most)
        gate_ref[pl.ds(base, 256), :] = jnp.broadcast_to(here / (here + there), (256, 128))

    def activate(plane):
        base = pl.multiple_of(plane * 256, 256)
        for j in range(2):
            span = slice(j * 256, (j + 1) * 256)
            gate, up = [
                lax.dot_general(
                    rows_ref[pl.ds(base, 256), :], up_ref[k, span, :], BY_ROW, preferred_element_type=F32
                )
                for k in range(2)
            ]
            act_ref[pl.ds(base, 256), span] = (gate / (1.0 + jnp.exp(-gate)) * up).astype(BF)

    compact(core)
    for load in loads:
        load.wait()
    activate(core)
    others()
    compact(1 - core)
    activate(1 - core)

    def project(plane, i):
        base = pl.multiple_of(plane * 256, 256)
        cols = pl.ds(pl.multiple_of(i * 256, 256), 256)
        product = jnp.dot(act_ref[pl.ds(base, 256), :], down_ref[:, cols], preferred_element_type=F32)
        return (product * gate_ref[pl.ds(base, 256), 0:1]).astype(BF)

    for group in range(4):

        def hand(k, _):
            i = group * 4 + k
            give_ref[i] = project(1 - core, i)
            return 0

        lax.fori_loop(0, 4, hand, 0)
        link.send(
            give_ref.at[pl.ds(group * 4, 4)], theirs_ref.at[pl.ds(group * 4, 4)], GATHER_KEYS + group, link.sibling
        )
    spreads = []
    for pair in range(2):
        corners = []
        for k in range(2):
            empty = jnp.zeros((ROWS, E_CAP), BF)
            lane = lax.broadcasted_iota(jnp.int32, (ROWS, E_CAP), 1).astype(F32)
            for codes in upright:
                hit = (codes[2 * pair + k] == lane).astype(BF)
                corners.append(jnp.concatenate([hit, empty] if k == 0 else [empty, hit], axis=1))
        spreads.append(
            jnp.concatenate(
                [jnp.concatenate(corners[0:2], axis=1), jnp.concatenate(corners[2:4], axis=1)], axis=0
            )
        )
    for group in range(4):
        link.arrive(theirs_ref.at[pl.ds(group * 4, 4)], GATHER_KEYS + group)

        def merge(k, _):
            i = group * 4 + k
            ours = project(core, i)
            for pair in range(2):
                rows = slice(pair * 128, (pair + 1) * 128)
                stacked = jnp.concatenate([ours[rows], theirs_ref[i, rows]], axis=0)
                spread = jnp.dot(spreads[pair], stacked, preferred_element_type=F32).astype(BF)
                for x in range(2):
                    for half in range(2):
                        sum_ref[2 * pair + x, group, k, half] = spread[
                            x * 128 : (x + 1) * 128, half * 128 : (half + 1) * 128
                        ]
            return 0

        lax.fori_loop(0, 4, merge, 0)

    def finish(row, rows, half, total):
        spot = (pl.ds(row, rows), pl.ds(half * 128, 128))
        out_ref[spot] = (kept_ref[spot] + total).astype(BF)

    ring_reduce(
        at, link, sum_ref, AXES, ORDERS, PART_ROWS, 1, ((half0, full0), full1, full2), GATHER_KEYS + 4, finish
    )
    link.finish()


LOG2E = 1.4426950408889634


def member_codes(request_ref, request_branch_ref, parent_ref, root_owner_ref, branch_owner_ref, code_ref, dp):
    def grid(shape, dim):
        return lax.broadcasted_iota(jnp.int32, shape, dim)

    def wide(ref):
        return jnp.broadcast_to(ref[...], (8, ref.shape[1]))

    def stand(matrix, row):
        return lax.dot_general(matrix.astype(BF), row.astype(BF), BY_ROW, preferred_element_type=F32)[:, 0:1]

    roots, branches, slots = root_owner_ref.shape[1], parent_ref.shape[1], request_ref.shape[1]
    square = (branches, branches)
    unit = grid(square, 0) == grid(square, 1)
    earlier = grid(square, 1) < grid(square, 0)
    owned = (wide(branch_owner_ref) == dp).astype(F32)
    branch_owned, branch_place = stand(unit, owned), stand(earlier, owned)
    parent = stand(unit, wide(parent_ref).astype(F32)).astype(jnp.int32)
    kid = jnp.sum(jnp.where((parent == parent_ref[...]) & earlier, 1.0, 0.0), axis=1, keepdims=True)
    root_owned = (wide(root_owner_ref) == dp).astype(F32)
    before = grid((roots, roots), 0) < grid((roots, roots), 1)
    root_place = jnp.dot(root_owned.astype(BF), before.astype(BF), preferred_element_type=F32)
    chosen = parent == grid((branches, roots), 1)
    parent_place = jnp.sum(jnp.where(chosen, root_place[0:1], 0.0), axis=1, keepdims=True)
    parent_owned = jnp.sum(jnp.where(chosen, root_owned[0:1], 0.0), axis=1, keepdims=True)
    root_base = jnp.where(parent_owned > 0.5, parent_place * ROWS + kid * BR_CAP, -4096.0)
    branch_base = jnp.where(branch_owned > 0.5, branch_place * BR_CAP, -4096.0)
    branch_row = wide(request_branch_ref).astype(F32).astype(BF)
    later = (grid((ROWS, ROWS), 0) < grid((ROWS, ROWS), 1)).astype(BF)
    count = jnp.zeros((branches, 1), F32)
    for block in range(slots // ROWS):
        span = slice(block * ROWS, (block + 1) * ROWS)
        asked = (grid((slots, ROWS), 0) == request_ref[0:1, span]).astype(BF)
        branch = jnp.dot(branch_row, asked, preferred_element_type=F32).astype(jnp.int32)[0:1]
        member = grid((branches, ROWS), 0) == branch
        rank = jnp.dot(member.astype(BF), later, preferred_element_type=F32) + count
        count += jnp.sum(jnp.where(member, 1.0, 0.0), axis=1, keepdims=True)
        for kind, base in enumerate((root_base, branch_base)):
            code = jnp.sum(jnp.where(member, base + rank, 0.0), axis=0, keepdims=True)
            code_ref[kind : kind + 1, span] = jnp.maximum(code, -1.0).astype(jnp.int32)


def query_kernel(
    queries_ref, routes_ref, request_ref, request_branch_ref, parent_ref, root_owner_ref, branch_owner_ref,
    all_ref, all_routes_ref, code_ref, local_sem, route_sem, send_sem, recv_sem,
):
    at = place()
    link = Link(at, (send_sem, recv_sem))
    sibling = link.sibling
    right, left = step_along(at, "x", 1), step_along(at, "x", 3)
    x, core = at["x"], at["c"]
    peers = [(by, device_of(at, x=(x + by // 2) % 4, c=(core + by) % 2)) for by in range(1, 8)]
    greet([device for _, device in peers])
    kv_head = lax.axis_index("mp") // 2
    own = queries_ref.at[:, pl.ds(pl.multiple_of(kv_head * 512, 512), 512)]
    mine = all_ref.at[x, core]
    link.send(own, mine, 0, right)
    link.send(own, mine, 1, left)
    link.send(own, mine, 4, sibling)
    local = [
        pltpu.make_async_copy(own, mine, local_sem),
        pltpu.make_async_copy(routes_ref, all_routes_ref.at[x, core], route_sem),
    ]
    for copy in local:
        copy.start()
    for by, device in peers:
        link.send(routes_ref, all_routes_ref.at[x, core], 8 + by, device)
    low, high, far = (x + 3) % 4, (x + 1) % 4, (x + 2) % 4
    upper, lower = pl.ds(0, 64), pl.ds(64, 64)
    from_low, from_high = all_ref.at[low, core], all_ref.at[high, core]
    link.arrive(from_low, 0)
    first = all_ref.at[low, core, upper]
    link.send(first, first, 2, right)
    link.arrive(from_high, 1)
    second = all_ref.at[high, core, lower]
    link.send(second, second, 3, left)
    link.send(from_low, from_low, 5, sibling)
    link.send(from_high, from_high, 6, sibling)
    code_ref[...] = jnp.full_like(code_ref, -1)
    member_codes(
        request_ref, request_branch_ref, parent_ref, root_owner_ref, branch_owner_ref, code_ref, lax.axis_index("dp")
    )
    for key, rows in ((2, upper), (3, lower)):
        ref = all_ref.at[far, core, rows]
        link.arrive(ref, key)
        link.send(ref, ref, key + 5, sibling)
    for key, ref in (
        (4, all_ref.at[x, 1 - core]),
        (5, all_ref.at[low, 1 - core]),
        (6, all_ref.at[high, 1 - core]),
        (7, all_ref.at[far, 1 - core, upper]),
        (8, all_ref.at[far, 1 - core, lower]),
    ):
        link.arrive(ref, key)
    for by in range(1, 8):
        giver = all_routes_ref.at[(x + 4 - by // 2) % 4, (core + by) % 2]
        link.arrive(giver, 8 + by)
    for copy in local:
        copy.wait()
    link.finish()


def gather_queries(queries, routes, *tables):
    return pl.pallas_call(
        query_kernel,
        out_shape=(
            jax.ShapeDtypeStruct((4, 2, ROWS, 512), BF),
            jax.ShapeDtypeStruct((4, 2, 2, ROWS), jnp.int32),
            jax.ShapeDtypeStruct((8, 1024), jnp.int32),
        ),
        in_specs=[pl.BlockSpec(memory_space=pl.ANY)] * 2 + [pl.BlockSpec(memory_space=pltpu.VMEM)] * 5,
        out_specs=(pl.BlockSpec(memory_space=pl.ANY),) * 2 + (pl.BlockSpec(memory_space=pltpu.VMEM),),
        scratch_shapes=[
            pltpu.SemaphoreType.DMA,
            pltpu.SemaphoreType.DMA,
            pltpu.SemaphoreType.DMA((16,)),
            pltpu.SemaphoreType.DMA((16,)),
        ],
        compiler_params=pltpu.CompilerParams(collective_id=3, has_side_effects=True),
        name="gather_queries",
    )(queries, routes, *(table[None, :] for table in tables))


HEAD_STEPS = 1
SCALE2 = LOG2E * 128 ** (-0.5)
BY_ROW = (((1,), (1,)), ((), ()))


def node_kernel(
    root_owner_ref, branch_owner_ref, root_pages_ref, branch_pages_ref, root_len_ref, branch_len_ref,
    all_hbm, pages_hbm, code_row_ref,
    sum_ref, stat_ref,
    query_ref, acc_ref, max_ref, total_ref, node_sum_ref, node_stat_ref, picked_ref, all_ref, pages_ref,
    root_id_ref, branch_id_ref, load_sem,
):
    loads = [
        pltpu.make_async_copy(all_hbm, all_ref, load_sem.at[0]),
        pltpu.make_async_copy(pages_hbm, pages_ref, load_sem.at[1]),
    ]
    for load in loads:
        load.start()
    dp = lax.axis_index("dp")
    part = lax.axis_index("mp") % 2
    lane = lax.broadcasted_iota(jnp.int32, (1, 128), 1)
    for owner_ref, id_ref in ((root_owner_ref, root_id_ref), (branch_owner_ref, branch_id_ref)):

        def scan(i, found):
            owned = owner_ref[i] == dp

            @pl.when(owned)
            def _():
                id_ref[found] = i

            return found + owned.astype(jnp.int32)

        lax.fori_loop(0, owner_ref.shape[0], scan, 0)
    loads[0].wait()
    loads[1].wait()

    for kind in range(2):
        wanted = lax.broadcasted_iota(jnp.int32, (256, 1024), 0)
        chosen = (wanted == code_row_ref[kind : kind + 1, :]).astype(BF)
        picked_ref[kind * 256 : kind * 256 + 256, :] = jnp.dot(
            chosen, all_ref[...], preferred_element_type=F32
        ).astype(BF)

    def keep_stats(row, rows, stats):
        for i in range(3):
            piece = stats.astype(BF)
            node_stat_ref[i, pl.ds(row, rows), :] = piece
            stats = stats - piece.astype(F32)

    def put(row, rows):
        stats = jnp.zeros((rows, 128), F32)
        for h in range(4):
            span = pl.ds(h * rows, rows)
            node_sum_ref[pl.ds(row, rows), h * 128 : (h + 1) * 128] = acc_ref[span, :].astype(BF)
            stats = jnp.where(lane == h, max_ref[span, 0:1], stats)
            stats = jnp.where(lane == 4 + h, total_ref[span, 0:1], stats)
        keep_stats(row, rows, stats)

    chunk = 8
    for k in range(ROOT_DEV):
        root = root_id_ref[k]
        length = root_len_ref[root]
        for h in range(4):
            query_ref[h * 128 : (h + 1) * 128, :] = picked_ref[k * 128 : (k + 1) * 128, h * 128 : (h + 1) * 128]
        acc_ref[...] = jnp.zeros_like(acc_ref)
        max_ref[...] = jnp.full_like(max_ref, MASKED_SCORE)
        total_ref[...] = jnp.zeros_like(total_ref)
        used = (length - part * 64 + PAGE - 1) // PAGE
        steps = (used + chunk - 1) // chunk

        def body(i, _):
            ids = [root_pages_ref[root, i * chunk + j] for j in range(chunk)]
            keys = jnp.concatenate([pages_ref[0, page] for page in ids], axis=0)
            values = jnp.concatenate([pages_ref[1, page] for page in ids], axis=0)
            spot = lax.broadcasted_iota(jnp.int32, (1, chunk * 64), 1)
            spot = (i * chunk + spot // 64) * PAGE + part * 64 + spot % 64
            usable = spot < length
            for h in range(HEAD_STEPS):
                span = pl.ds(h * (512 // HEAD_STEPS), 512 // HEAD_STEPS)
                scores = lax.dot_general(query_ref[span, :], keys, BY_ROW, preferred_element_type=F32)
                scores = jnp.where(usable, scores * SCALE2, MASKED_SCORE)
                old = max_ref[span, :]
                new = jnp.maximum(old, jnp.max(scores, axis=1, keepdims=True))
                weights = jnp.exp2(scores - new[:, 0:1])
                fade = jnp.exp2(old - new)
                total_ref[span, :] = total_ref[span, :] * fade + jnp.sum(weights, axis=1, keepdims=True)
                acc_ref[span, :] = acc_ref[span, :] * fade + jnp.dot(
                    weights.astype(BF), values, preferred_element_type=F32
                )
                max_ref[span, :] = new
            return 0

        lax.fori_loop(0, steps, body, 0)
        put(k * 128, 128)

    def branch_work(b):
        branch = branch_id_ref[b]
        length = branch_len_ref[branch]
        row = pl.multiple_of(256 + b * 32, 32)
        picked = picked_ref[pl.ds(row, 32), :]
        stacked = jnp.concatenate([picked[:, h * 128 : (h + 1) * 128] for h in range(4)], axis=0)
        ids = [branch_pages_ref[j, branch] for j in range(4)]
        keys = jnp.concatenate([pages_ref[0, page] for page in ids], axis=0)
        values = jnp.concatenate([pages_ref[1, page] for page in ids], axis=0)
        spot = lax.broadcasted_iota(jnp.int32, (1, 256), 1)
        spot = (spot // 64) * PAGE + part * 64 + spot % 64
        usable = spot < length
        scores = lax.dot_general(stacked, keys, BY_ROW, preferred_element_type=F32)
        scores = jnp.where(usable, scores * SCALE2, MASKED_SCORE)
        top = jnp.max(scores, axis=1, keepdims=True)
        weights = jnp.where(usable, jnp.exp2(scores - top), 0.0)
        total = jnp.sum(weights, axis=1, keepdims=True)
        acc = jnp.dot(weights.astype(BF), values, preferred_element_type=F32)
        stats = jnp.zeros((32, 128), F32)
        for h in range(4):
            node_sum_ref[pl.ds(row, 32), h * 128 : (h + 1) * 128] = acc[h * 32 : (h + 1) * 32].astype(BF)
            stats = jnp.where(lane == h, top[h * 32 : (h + 1) * 32], stats)
            stats = jnp.where(lane == 4 + h, total[h * 32 : (h + 1) * 32], stats)
        keep_stats(row, 32, stats)

    def branch_body(i, _):
        for k in range(4):
            branch_work(i * 4 + k)
        return 0

    lax.fori_loop(0, BR_DEV // 4, branch_body, 0)

    unit = lax.broadcasted_iota(jnp.int32, (ROWS, ROWS), 0) == lax.broadcasted_iota(jnp.int32, (ROWS, ROWS), 1)
    unit = unit.astype(BF)

    def spread_work(block):
        parts = []
        wanted = lax.broadcasted_iota(jnp.int32, (ROWS, 256), 1)
        row = code_row_ref[:, pl.ds(pl.multiple_of(block * ROWS, ROWS), ROWS)].astype(F32).astype(BF)
        codes = lax.dot_general(unit, row, BY_ROW, preferred_element_type=F32).astype(jnp.int32)
        for kind in range(2):
            code = codes[:, kind : kind + 1]
            chosen = wanted == code
            rows = slice(kind * 256, kind * 256 + 256)
            sums = jnp.dot(chosen.astype(BF), node_sum_ref[rows, :], preferred_element_type=F32)
            stats = sum(
                jnp.dot(chosen.astype(BF), node_stat_ref[i, rows, :], preferred_element_type=F32)
                for i in (2, 1, 0)
            )
            stats = jnp.where((lane < 4) & (code < 0), MASKED_SCORE, stats)
            parts.append((sums, stats))
        merged, stats = merge_blocks(parts[0], parts[1], 4)
        sum_ref[block] = merged.astype(BF)
        stat_ref[block] = stats.T[0:8]

    def spread_body(i, _):
        for k in range(4):
            spread_work(i * 4 + k)
        return 0

    lax.fori_loop(0, 2, spread_body, 0)


def merge_blocks(one, two, heads):
    sums_one, stats_one = one
    sums_two, stats_two = two
    lane = lax.broadcasted_iota(jnp.int32, (1, 128), 1)
    top = jnp.maximum(stats_one, stats_two)
    factor_one, factor_two = jnp.exp2(stats_one - top), jnp.exp2(stats_two - top)
    total = stats_one * pltpu.roll(factor_one, 4, 1) + stats_two * pltpu.roll(factor_two, 4, 1)
    stats = jnp.where(lane < 4, top, jnp.where(lane < 8, total, 0.0))
    pieces = []
    for h in range(heads):
        span = slice(h * 128, (h + 1) * 128)
        pieces.append(
            sums_one[:, span].astype(F32) * factor_one[:, h : h + 1]
            + sums_two[:, span].astype(F32) * factor_two[:, h : h + 1]
        )
    return jnp.concatenate(pieces, axis=1), stats


def node_partials(tables, all_queries, pages, codes):
    vmem, hbm = pl.BlockSpec(memory_space=pltpu.VMEM), pl.BlockSpec(memory_space=pl.ANY)
    return pl.pallas_call(
        node_kernel,
        out_shape=(
            jax.ShapeDtypeStruct((8, ROWS, 512), BF),
            jax.ShapeDtypeStruct((8, 8, ROWS), F32),
        ),
        in_specs=[pl.BlockSpec(memory_space=pltpu.SMEM)] * 6 + [hbm, hbm, vmem],
        out_specs=(vmem, vmem),
        scratch_shapes=[
            pltpu.VMEM((512, 128), BF),
            pltpu.VMEM((512, 128), F32),
            pltpu.VMEM((512, 128), F32),
            pltpu.VMEM((512, 128), F32),
            pltpu.VMEM((512, 512), BF),
            pltpu.VMEM((3, 512, 128), BF),
            pltpu.VMEM((512, 512), BF),
            pltpu.VMEM(all_queries.shape, BF),
            pltpu.VMEM(pages.shape, BF),
            pltpu.SMEM((ROOT_DEV,), jnp.int32),
            pltpu.SMEM((BR_DEV,), jnp.int32),
            pltpu.SemaphoreType.DMA((2,)),
        ],
        compiler_params=pltpu.CompilerParams(vmem_limit_bytes=62 * 2**20),
        name="node_partials",
    )(*tables, all_queries, pages, codes)


def attend_kernel(
    at, begin,
    sum_hbm, stat_hbm, query_hbm, leaf_hbm, leaf_len_ref, fresh_hbm, weight_hbm, residual_ref,
    hidden_ref, narrow_ref,
    own_sum, own_stat, their_sum, their_stat, run_sum, run_stat, land_sum, land_stat,
    query_ref, wide_query, own_query_ref, leaf_ref, length_ref, fresh_ref, weight_ref,
    leaf_sum, leaf_stat, give_stat, side_sum, side_stat, give_sum,
    proj_ref, full1, full2, load_sem, send_sem, recv_sem,
):
    link = Link(at, (send_sem, recv_sem))
    send, arrive, sibling = link.send, link.arrive, link.sibling
    beside = {**at, "z": at["z"] + 1 - 2 * (at["z"] % 2)}
    x, core = at["x"], at["c"]
    part = at["z"] % 2
    mp = lax.axis_index("mp")
    kv_head = mp // 2

    def columns(ref, width, index):
        return ref.at[:, pl.ds(pl.multiple_of(index * width, width), width)]

    loads = [
        pltpu.make_async_copy(src, dst, load_sem.at[i])
        for i, (src, dst) in enumerate(
            (
                (columns(query_hbm, 512, kv_head), query_ref),
                (leaf_hbm.at[:, :, 0], leaf_ref),
                (sum_hbm.at[:, core], own_sum),
                (stat_hbm.at[:, core], own_stat),
                (columns(query_hbm, 256, mp), own_query_ref),
                (columns(fresh_hbm.at[0], 128, kv_head), fresh_ref.at[0]),
                (columns(fresh_hbm.at[1], 128, kv_head), fresh_ref.at[1]),
                (weight_hbm, weight_ref),
            )
        )
    ]
    for load in loads:
        load.start()
    greet(all_peers(at))
    send(sum_hbm.at[:, 1 - core], their_sum, 0, sibling)
    send(stat_hbm.at[:, 1 - core], their_stat, 1, sibling)
    lane = lax.broadcasted_iota(jnp.int32, (1, 128), 1)
    unit = lax.broadcasted_iota(jnp.int32, (ROWS, ROWS), 0) == lax.broadcasted_iota(
        jnp.int32, (ROWS, ROWS), 1
    )
    lengths_row = jnp.broadcast_to(leaf_len_ref[...], (ROWS, ROWS))
    length_ref[...] = jnp.broadcast_to(
        jnp.sum(jnp.where(unit, lengths_row, 0), axis=1, keepdims=True), (ROWS, ROWS)
    )

    def upright(stats):
        return jnp.concatenate([stats, jnp.zeros((ROWS - 8, ROWS), F32)], axis=0).T

    def leaf_group(base):
        span = pl.ds(base, 8)
        heads = [wide_query[span, h * 128 : (h + 1) * 128] for h in range(4)]
        stacked = jnp.concatenate(heads, axis=0)
        keys = leaf_ref[0, span].reshape(512, 128)
        values = leaf_ref[1, span].reshape(512, 128)
        scores = lax.dot_general(
            stacked.astype(BF), keys, BY_ROW, preferred_element_type=F32
        )
        row = lax.broadcasted_iota(jnp.int32, (32, 512), 0) % 8
        col = lax.broadcasted_iota(jnp.int32, (32, 512), 1)
        lengths = jnp.concatenate([length_ref[span, 0:1]] * 4, axis=0)
        usable = (row == col // 64) & (part * 64 + col % 64 < lengths)
        scores = jnp.where(usable, scores * SCALE2, MASKED_SCORE)
        top = jnp.max(scores, axis=1, keepdims=True)
        weights = jnp.where(usable, jnp.exp2(scores - top), 0.0)
        total = jnp.sum(weights, axis=1, keepdims=True)
        acc = jnp.dot(weights.astype(BF), values, preferred_element_type=F32)
        stats = jnp.zeros((8, 128), F32)
        for h in range(4):
            leaf_sum[span, h * 128 : (h + 1) * 128] = acc[h * 8 : (h + 1) * 8]
            stats = jnp.where(lane == h, top[h * 8 : (h + 1) * 8], stats)
            stats = jnp.where(lane == 4 + h, total[h * 8 : (h + 1) * 8], stats)
        leaf_stat[span, :] = stats

    def leaf_body(i, _):
        for k in range(4):
            leaf_group(pl.multiple_of(i * 32 + k * 8, 8))
        return 0

    loads[2].wait()
    loads[3].wait()
    arrive(their_sum, 0)
    arrive(their_stat, 1)
    for by in (2, 1, 3):
        value = (x + by) % 4
        merged, stats = merge_blocks(
            (own_sum[value], upright(own_stat[value])), (their_sum[value], upright(their_stat[value])), 4
        )
        run_sum[by - 1] = merged.astype(BF)
        run_stat[by - 1] = stats.T[0:8]
        device = step_along(at, "x", by)
        send(run_sum.at[by - 1], land_sum.at[by - 1], 2 * by, device)
        send(run_stat.at[by - 1], land_stat.at[by - 1], 2 * by + 1, device)
    loads[0].wait()
    loads[1].wait()
    begin()
    wide_query[...] = query_ref[...].astype(F32)
    lax.fori_loop(0, 4, leaf_body, 0)
    sums, stats = merge_blocks(
        (own_sum[x], upright(own_stat[x])), (their_sum[x], upright(their_stat[x])), 4
    )
    sums, stats = merge_blocks((sums, stats), (leaf_sum[...], leaf_stat[...]), 4)
    for load in loads[4:]:
        load.wait()
    fresh_key = fresh_ref[0].astype(F32)
    fresh_value = fresh_ref[1].astype(F32)
    own_scores = [
        jnp.sum(own_query_ref[:, h * 128 : (h + 1) * 128].astype(F32) * fresh_key, axis=1, keepdims=True)
        * SCALE2
        for h in range(2)
    ]
    for by in (1, 3, 2):
        arrive(land_sum.at[by - 1], 2 * by)
        arrive(land_stat.at[by - 1], 2 * by + 1)
        sums, stats = merge_blocks((sums, stats), (land_sum[by - 1], upright(land_stat[by - 1])), 4)
    first = part == 0
    give_sum[...] = jnp.where(first, sums[:, 256:], sums[:, :256]).astype(BF)
    give_stat[...] = stats.T[0:8]
    send(give_sum, side_sum, 10, device_of(beside))
    send(give_stat, side_stat, 11, device_of(beside))
    kept = jnp.where(first, sums[:, :256], sums[:, 256:])
    arrive(side_sum, 10)
    arrive(side_stat, 11)
    theirs = upright(side_stat[...])
    pieces = []
    for h in range(2):
        span = slice(h * 128, (h + 1) * 128)

        def column(from_stats, offset):
            return jnp.where(
                first,
                from_stats[:, offset + h : offset + h + 1],
                from_stats[:, offset + 2 + h : offset + 3 + h],
            )

        top_one, top_two = column(stats, 0), column(theirs, 0)
        top = jnp.maximum(jnp.maximum(top_one, top_two), own_scores[h])
        factor_one, factor_two = jnp.exp2(top_one - top), jnp.exp2(top_two - top)
        factor_own = jnp.exp2(own_scores[h] - top)
        weighted = (
            kept[:, span] * factor_one
            + side_sum[:, span].astype(F32) * factor_two
            + factor_own * fresh_value
        )
        total = column(stats, 4) * factor_one + column(theirs, 4) * factor_two + factor_own
        pieces.append((weighted / total).astype(BF))
    attended = jnp.concatenate(pieces, axis=1)
    for i in range(16):
        product = jnp.dot(
            attended, weight_ref[:, i * 256 : (i + 1) * 256], preferred_element_type=F32
        ).astype(BF)
        for half in range(2):
            proj_ref[i // 4, i % 4, half] = product[:, half * 128 : (half + 1) * 128]

    def finish(row, rows, half, total):
        cols = pl.ds(half * 128, 128)
        total += residual_ref[pl.ds(row, rows), cols].astype(F32)
        hidden_ref[pl.ds(row, rows), cols] = total
        narrow_ref[half, pl.ds(row, rows), :] = total.astype(BF)

    ring_reduce(
        at, link, proj_ref, ("y", "z"), (("y", "z"), ("z", "y")), ((0, 64), (64, 64)), 0,
        (full1, full2), 12, finish,
    )
    link.finish()


def layer_kernel(*refs):
    ins, out_ref = refs[:13], refs[13]
    attend_refs = refs[14 : 14 + ATTEND_SCRATCH]
    hidden_ref, narrow_ref, tables_sem, weight_sem = refs[14 + ATTEND_SCRATCH : 18 + ATTEND_SCRATCH]
    expert_refs = refs[18 + ATTEND_SCRATCH :]
    at = place()
    tables = [
        pltpu.make_async_copy(ins[8 + i], expert_refs[i], tables_sem.at[i]) for i in range(3)
    ]
    loads = [
        pltpu.make_async_copy(ins[11 + i], expert_refs[EXPERT_WEIGHTS + i], weight_sem.at[i]) for i in range(2)
    ]

    def begin():
        for load in tables + loads:
            load.start()

    attend_kernel(at, begin, *ins[:8], hidden_ref, narrow_ref, *attend_refs)
    expert_kernel(at, loads, tables, out_ref, hidden_ref, narrow_ref, *expert_refs)


ATTEND_SCRATCH = 27
EXPERT_WEIGHTS = 8


def attend_and_route(
    sums, stats, queries, leaf, leaf_len, fresh, out_weight, residual, routes, gain, router, expert_in, expert_out
):
    keys = GATHER_KEYS + 4 + 36
    vmem, hbm = pl.BlockSpec(memory_space=pltpu.VMEM), pl.BlockSpec(memory_space=pl.ANY)
    return pl.pallas_call(
        layer_kernel,
        out_shape=jax.ShapeDtypeStruct((ROWS, 256), BF),
        in_specs=[hbm, hbm, hbm, hbm, vmem, hbm, hbm, vmem] + [hbm] * 5,
        out_specs=vmem,
        scratch_shapes=[
            pltpu.VMEM((4, ROWS, 512), BF),
            pltpu.VMEM((4, 8, ROWS), F32),
            pltpu.VMEM((4, ROWS, 512), BF),
            pltpu.VMEM((4, 8, ROWS), F32),
            pltpu.VMEM((3, ROWS, 512), BF),
            pltpu.VMEM((3, 8, ROWS), F32),
            pltpu.VMEM((3, ROWS, 512), BF),
            pltpu.VMEM((3, 8, ROWS), F32),
            pltpu.VMEM((ROWS, 512), BF),
            pltpu.VMEM((ROWS, 512), F32),
            pltpu.VMEM((ROWS, 256), BF),
            pltpu.VMEM((2, ROWS, 64, 128), BF),
            pltpu.VMEM((ROWS, ROWS), jnp.int32),
            pltpu.VMEM((2, ROWS, 128), BF),
            pltpu.VMEM((256, 4096), BF),
            pltpu.VMEM((ROWS, 512), F32),
            pltpu.VMEM((ROWS, 128), F32),
            pltpu.VMEM((8, ROWS), F32),
            pltpu.VMEM((ROWS, 256), BF),
            pltpu.VMEM((8, ROWS), F32),
            pltpu.VMEM((ROWS, 256), BF),
            pltpu.VMEM((4, 4, 2, ROWS, 128), BF),
            pltpu.VMEM((3, 4, 2, ROWS, 128), BF),
            pltpu.VMEM((3, 2, ROWS, 128), BF),
            pltpu.SemaphoreType.DMA((8,)),
            pltpu.SemaphoreType.DMA((28,)),
            pltpu.SemaphoreType.DMA((28,)),
            pltpu.VMEM((ROWS, 256), F32),
            pltpu.VMEM((2, ROWS, 128), BF),
            pltpu.SemaphoreType.DMA((3,)),
            pltpu.SemaphoreType.DMA((2,)),
            pltpu.VMEM(routes.shape, jnp.int32),
            pltpu.VMEM(gain.shape, F32),
            pltpu.VMEM(router.shape, BF),
            pltpu.VMEM((4, 2, 4, 4, 2, ROWS, 128), BF),
            pltpu.VMEM((8, ROWS), jnp.int32),
            pltpu.VMEM((8, ROWS), jnp.int32),
            pltpu.VMEM((512, 4096), BF),
            pltpu.VMEM((512, 128), F32),
            pltpu.VMEM(expert_in.shape, BF),
            pltpu.VMEM(expert_out.shape, BF),
            pltpu.VMEM((512, 512), BF),
            pltpu.VMEM((16, 256, 256), BF),
            pltpu.VMEM((16, 256, 256), BF),
            pltpu.VMEM((4, 4, 4, 2, ROWS, 128), BF),
            pltpu.VMEM((2, 4, 4, ROWS, 128), BF),
            pltpu.VMEM((2, 4, 4, 2, ROWS, 128), BF),
            pltpu.VMEM((3, 4, 2, ROWS, 128), BF),
            pltpu.VMEM((3, 2, ROWS, 128), BF),
            pltpu.SemaphoreType.DMA,
            pltpu.SemaphoreType.DMA((keys,)),
            pltpu.SemaphoreType.DMA((keys,)),
        ],
        compiler_params=pltpu.CompilerParams(
            collective_id=1, has_side_effects=True, vmem_limit_bytes=62 * 2**20
        ),
        name="attend_and_route",
    )(sums, stats, queries, leaf, leaf_len, fresh, out_weight, residual, routes, gain, router, expert_in, expert_out)


def shards(
    queries,
    new_kv,
    residual,
    out_weight,
    norm_gain,
    router,
    expert_in,
    expert_out,
    node_cache,
    leaf_cache,
    slot_request,
    request_branch,
    branch_parent,
    root_owner,
    branch_owner,
    root_pages,
    branch_pages,
    root_len,
    branch_len,
    leaf_len,
    routes,
):
    all_queries, all_routes, codes = gather_queries(
        queries,
        routes.T,
        slot_request,
        request_branch,
        branch_parent,
        root_owner,
        branch_owner,
    )
    sums, stats = node_partials(
        (root_owner, branch_owner, root_pages, branch_pages.T, root_len, branch_len),
        all_queries.reshape(8 * ROWS, 512),
        node_cache[:, :, 0],
        codes,
    )
    return attend_and_route(
        sums.reshape(4, 2, ROWS, 512),
        stats.reshape(4, 2, 8, ROWS),
        queries,
        leaf_cache,
        leaf_len[None, :],
        new_kv,
        out_weight,
        residual,
        all_routes,
        norm_gain.reshape(16, 1, 256),
        router.T,
        expert_in[0],
        expert_out[0],
    )


def solution(mesh):
    placed = (
        P("dp", None),
        P(None, "dp", None),
        P("dp", "mp"),
        P("mp", None),
        P(),
        P(),
        P("dp", None, "mp", None),
        P("dp", "mp", None),
        P(None, "dp", "mp", None, None),
        P(None, "dp", "mp", None, None),
        P(),
        P(),
        P(),
        P(),
        P(),
        P(),
        P(),
        P(),
        P(),
        P("dp"),
        P("dp", None),
    )
    return jax.shard_map(
        shards, mesh=mesh, in_specs=placed, out_specs=P("dp", "mp"), check_vma=False
    )
```

```python
import jax
import jax.numpy as jnp
from jax import lax
from jax.experimental import pallas as pl
from jax.experimental.pallas import tpu as pltpu
from jax.sharding import PartitionSpec as P

EXPERTS = 8
PAGE = 128
ROOT_DEV = 2
BR_DEV = 8
BR_CAP = 32
E_CAP = 64

MASKED_SCORE = -1e30
NORM_EPS = 1e-05

BF = jnp.bfloat16
F32 = jnp.float32
MESH = pl.DeviceIdType.MESH
ROWS = 128
PART_ROWS = ((0, 48), (48, 48), (96, 32))
AXES = ("x", "y", "z")
ORDERS = tuple(AXES[part:] + AXES[:part] for part in range(3))


def place():
    dp = lax.axis_index("dp")
    mp = lax.axis_index("mp")
    return {"x": dp // 2, "c": dp % 2, "y": mp // 4, "z": mp % 4}


def device_of(at, **moved):
    at = {**at, **moved}
    return (at["x"] * 2 + at["c"], at["y"] * 4 + at["z"])


def step_along(at, axis, by):
    return device_of(at, **{axis: (at[axis] + by) % 4})


def greet(peers):
    barrier = pltpu.get_barrier_semaphore()
    for peer in peers:
        pl.semaphore_signal(barrier, inc=1, device_id=peer, device_id_type=MESH)
    pl.semaphore_wait(barrier, len(peers))


def remote(src, dst, sems, key, device):
    return pltpu.make_async_remote_copy(
        src_ref=src,
        dst_ref=dst,
        send_sem=sems[0].at[key],
        recv_sem=sems[1].at[key],
        device_id=device,
        device_id_type=MESH,
    )


def all_peers(at):
    return [step_along(at, axis, by) for axis in AXES for by in (1, 2, 3)] + [
        device_of(at, c=1 - at["c"])
    ]


class Link:
    def __init__(self, at, sems):
        self.sems = sems
        self.sibling = device_of(at, c=1 - at["c"])
        self.started = []

    def send(self, src, dst, key, device):
        copy = remote(src, dst, self.sems, key, device)
        copy.start()
        self.started.append(copy)

    def arrive(self, ref, key):
        remote(ref, ref, self.sems, key, self.sibling).wait_recv()

    def finish(self):
        for copy in self.started:
            copy.wait_send()


def gather_all(at, link, own_ref, buf_ref, local_sem, base, meanwhile):
    both = slice(None)
    core = at["c"]

    def slab(part, phase, value, half, plane):
        index = {"x": at["x"], "y": at["y"], "z": at["z"]}
        for axis in ORDERS[part][:phase]:
            index[axis] = slice(None)
        index[ORDERS[part][phase]] = value
        row, rows = PART_ROWS[part]
        return buf_ref.at[index["x"], plane, index["y"], index["z"], half, pl.ds(row, rows), :]

    local = pltpu.make_async_copy(own_ref, buf_ref.at[at["x"], core, at["y"], at["z"]], local_sem)
    local.start()
    for phase in range(2):
        for part in range(3):
            axis = ORDERS[part][phase]
            ref = slab(part, phase, at[axis], both, core)
            src = ref
            if phase == 0:
                row, rows = PART_ROWS[part]
                src = own_ref.at[:, pl.ds(row, rows), :]
            for by in (2, 1, 3):
                link.send(src, ref, base + (part * 2 + phase) * 3 + by - 1, step_along(at, axis, by))
        if phase == 0:
            local.wait()
        else:
            meanwhile()
        for part in range(3):
            axis = ORDERS[part][phase]
            for by in (1, 3, 2):
                ref = slab(part, phase, (at[axis] - by) % 4, both, core)
                link.arrive(ref, base + (part * 2 + phase) * 3 + by - 1)
    base += 18
    for part in range(3):
        axis = ORDERS[part][2]
        key = base + part * 8
        ref = slab(part, 2, at[axis], both, core)
        for side in range(2):
            for late in range(2):
                half = slab(part, 2, at[axis], side if late == 0 else 1 - side, core)
                spare = base + 24 + part * 2 + side
                link.send(half, half, spare if late else key + side, step_along(at, axis, 1 + 2 * side))
        link.send(ref, ref, key + 4, link.sibling)
    for part in range(3):
        axis = ORDERS[part][2]
        key = base + part * 8
        for side, by in ((0, 3), (1, 1)):
            value = (at[axis] + by) % 4
            half = slab(part, 2, value, side, core)
            link.arrive(half, key + side)
            link.send(half, half, key + 2 + side, step_along(at, axis, 1 + 2 * side))
    for part in range(3):
        axis = ORDERS[part][2]
        key = base + part * 8
        for side, by in ((0, 3), (1, 1)):
            value = (at[axis] + by) % 4
            link.arrive(slab(part, 2, value, 1 - side, core), base + 24 + part * 2 + side)
            ref = slab(part, 2, value, both, core)
            link.send(ref, ref, key + 5 + side, link.sibling)
    for part in range(3):
        axis = ORDERS[part][2]
        key = base + part * 8
        far = (at[axis] + 2) % 4
        for side in range(2):
            link.arrive(slab(part, 2, far, side, core), key + 2 + side)
        ref = slab(part, 2, far, both, core)
        link.send(ref, ref, key + 7, link.sibling)

    def others():
        for part in range(3):
            v = at[ORDERS[part][2]]
            for i, by in enumerate((0, 3, 1, 2)):
                link.arrive(slab(part, 2, (v + by) % 4, both, 1 - core), base + part * 8 + 4 + i)

    return others


GATHER_KEYS = 18 + 30


def ring_reduce(at, link, sum_ref, dims, orders, part_rows, relay, lands, base, finish):
    phases = len(dims)
    both = slice(None)
    parts = range(len(orders))

    def view(part, phase, value, half):
        index = dict(at)
        for axis in orders[part][phase + 1 :]:
            index[axis] = slice(None)
        index[orders[part][phase]] = value
        row, rows = part_rows[part]
        return tuple(index[axis] for axis in dims) + (half, pl.ds(row, rows), slice(None))

    def spot(part, phase, slot, *half):
        row, rows = part_rows[part]
        return (slot,) + (slice(None),) * (phases - 1 - phase) + half + (pl.ds(row, rows), slice(None))

    def accumulate(target, others):
        total = sum_ref[target].astype(F32)
        for ref, index in others:
            total += ref[index].astype(F32)
        return total

    for phase in range(phases):
        keys = [base + (part * phases + phase) * 4 for part in parts]
        if phase < relay:
            halves, fulls = lands[phase]
            for part in parts:
                axis = orders[part][phase]
                for side, by in ((0, 1), (1, 3)):
                    link.send(
                        sum_ref.at[view(part, phase, (at[axis] + 2) % 4, side)],
                        halves.at[spot(part, phase, side)],
                        keys[part] + side,
                        step_along(at, axis, by),
                    )
                for side, by in ((0, 1), (1, 3)):
                    link.send(
                        sum_ref.at[view(part, phase, (at[axis] + by) % 4, 1 - side)],
                        fulls.at[spot(part, phase, side, 1 - side)],
                        base + 12 * phases + part * 2 + side,
                        step_along(at, axis, by),
                    )
            for part in parts:
                axis = orders[part][phase]
                for side, by in ((0, 1), (1, 3)):
                    index = spot(part, phase, side)
                    link.arrive(halves.at[index], keys[part] + side)
                    target = view(part, phase, (at[axis] + by) % 4, side)
                    sum_ref[target] = accumulate(target, [(halves, index)]).astype(BF)
                    link.send(
                        sum_ref.at[target],
                        fulls.at[spot(part, phase, side, side)],
                        keys[part] + 2 + side,
                        step_along(at, axis, by),
                    )
            slots, first = 2, 2
        else:
            fulls = lands[phase]
            for part in parts:
                axis = orders[part][phase]
                for by in (2, 1, 3):
                    link.send(
                        sum_ref.at[view(part, phase, (at[axis] + by) % 4, both)],
                        fulls.at[spot(part, phase, by - 1, both)],
                        keys[part] + by - 1,
                        step_along(at, axis, by),
                    )
            slots, first = 3, 0
        for part in parts:
            axis = orders[part][phase]
            for slot in range(slots):
                if phase < relay:
                    link.arrive(fulls.at[spot(part, phase, slot, 1 - slot)], base + 12 * phases + part * 2 + slot)
                    link.arrive(fulls.at[spot(part, phase, slot, slot)], keys[part] + first + slot)
                else:
                    link.arrive(fulls.at[spot(part, phase, slot, both)], keys[part] + first + slot)
            for half in range(2):
                target = view(part, phase, at[axis], half)
                total = accumulate(target, [(fulls, spot(part, phase, slot, half)) for slot in range(slots)])
                if phase < phases - 1:
                    sum_ref[target] = total.astype(BF)
                else:
                    finish(*part_rows[part], half, total)


def expert_kernel(
    at, loads, tables_in,
    out_ref, kept_ref, own_ref,
    routes_ref, gain_ref, router_ref,
    buf_ref, code_ref, other_ref, rows_ref, gate_ref, up_ref, down_ref, act_ref, give_ref, theirs_ref, sum_ref,
    half0, full0, full1, full2,
    local_sem, send_sem, recv_sem,
):
    link = Link(at, (send_sem, recv_sem))
    core = at["c"]
    mine = lax.axis_index("dp")
    row_index = lax.broadcasted_iota(jnp.int32, (ROWS, ROWS), 0)
    lane_index = lax.broadcasted_iota(jnp.int32, (ROWS, ROWS), 1)
    upright = []

    def tables():
        for load in tables_in:
            load.wait()
        unit = (row_index == lane_index).astype(BF)
        later = (row_index < lane_index).astype(BF)
        earlier = (lane_index < row_index).astype(BF)
        first = jnp.concatenate([routes_ref[b // 2, b % 2, 0:1, :] for b in range(8)], axis=0)
        second = jnp.concatenate([routes_ref[b // 2, b % 2, 1:2, :] for b in range(8)], axis=0)
        shift = (lax.broadcasted_iota(jnp.int32, (8, ROWS), 0) // 2) % 2 * E_CAP
        hit = ((first == mine) | (second == mine)).astype(F32)
        rank = jnp.dot(hit.astype(BF), later, preferred_element_type=F32).astype(jnp.int32)
        code_ref[0:8, :] = jnp.where(hit > 0.5, rank + shift, -1)
        other_ref[...] = first + second - mine
        for expert in (mine, mine + 1 - 2 * core):
            hit = ((first == expert) | (second == expert)).astype(BF)
            there = lax.dot_general(unit, hit, BY_ROW, preferred_element_type=F32)
            rank = lax.dot_general(earlier, hit, BY_ROW, preferred_element_type=F32)
            codes = jnp.where(there > 0.5, rank, -1.0)
            upright.append(
                [jnp.where(core == 0, codes[:, 2 * b : 2 * b + 1], codes[:, 2 * b + 1 : 2 * b + 2]) for b in range(4)]
            )

    others = gather_all(at, link, own_ref, buf_ref, local_sem, 0, tables)

    def compact(plane):
        base = pl.multiple_of(plane * 256, 256)
        wanted = lax.broadcasted_iota(jnp.int32, (128, 256), 0)
        picks, answers = [], []
        for pair in range(2):
            blocks = [pl.ds(4 * pair + 2 * k + plane, 1) for k in range(2)]
            code = jnp.concatenate([code_ref[b, :] for b in blocks], axis=1)
            other = jnp.concatenate([other_ref[b, :] for b in blocks], axis=1)
            chosen = wanted == code
            picks.append(chosen.astype(BF))
            answers.append(jnp.sum(jnp.where(chosen, other, 0), axis=1, keepdims=True))
        answer = jnp.concatenate(answers, axis=0)

        def fill(y, squares):
            for z in range(4):
                pieces = []
                for pair in range(2):
                    whole = jnp.concatenate(
                        [
                            jnp.concatenate([buf_ref[2 * pair + k, plane, y, z, h] for h in range(2)], axis=1)
                            for k in range(2)
                        ],
                        axis=0,
                    )
                    pieces.append(jnp.dot(picks[pair], whole, preferred_element_type=F32))
                piece = jnp.concatenate(pieces, axis=0)
                cols = pl.ds(pl.multiple_of((y * 4 + z) * 256, 256), 256)
                rows_ref[pl.ds(base, 256), cols] = piece.astype(BF)
                piece = piece * piece
                squares += piece[:, :128] + piece[:, 128:]
            return squares

        squares = lax.fori_loop(0, 4, fill, jnp.zeros((256, 128), F32))
        scale = lax.rsqrt(jnp.sum(squares, axis=1, keepdims=True) / 4096.0 + NORM_EPS)

        def norm(y, _):
            for z in range(4):
                cols = pl.ds(pl.multiple_of((y * 4 + z) * 256, 256), 256)
                normed = rows_ref[pl.ds(base, 256), cols].astype(F32) * scale * gain_ref[y * 4 + z]
                rows_ref[pl.ds(base, 256), cols] = normed.astype(BF)
            return 0

        lax.fori_loop(0, 4, norm, 0)
        logits = lax.dot_general(
            rows_ref[pl.ds(base, 256), :], router_ref[...], BY_ROW, preferred_element_type=F32
        )
        lane = lax.broadcasted_iota(jnp.int32, logits.shape, 1)
        here = jnp.sum(jnp.where(lane == mine, logits, 0.0), axis=1, keepdims=True)
        there = jnp.sum(
            jnp.where(lane == answer, logits, 0.0), axis=1, keepdims=True
        )
        most = jnp.maximum(here, there)
        here = jnp.exp(here - most)
        there = jnp.exp(there - most)
        gate_ref[pl.ds(base, 256), :] = jnp.broadcast_to(here / (here + there), (256, 128))

    def activate(plane):
        base = pl.multiple_of(plane * 256, 256)
        for j in range(2):
            span = slice(j * 256, (j + 1) * 256)
            gate, up = [
                lax.dot_general(
                    rows_ref[pl.ds(base, 256), :], up_ref[k, span, :], BY_ROW, preferred_element_type=F32
                )
                for k in range(2)
            ]
            act_ref[pl.ds(base, 256), span] = (gate / (1.0 + jnp.exp(-gate)) * up).astype(BF)

    compact(core)
    for load in loads:
        load.wait()
    activate(core)
    others()
    compact(1 - core)
    activate(1 - core)

    def project(plane, i):
        base = pl.multiple_of(plane * 256, 256)
        cols = pl.ds(pl.multiple_of(i * 256, 256), 256)
        product = jnp.dot(act_ref[pl.ds(base, 256), :], down_ref[:, cols], preferred_element_type=F32)
        return (product * gate_ref[pl.ds(base, 256), 0:1]).astype(BF)

    for group in range(4):

        def hand(k, _):
            i = group * 4 + k
            give_ref[i] = project(1 - core, i)
            return 0

        lax.fori_loop(0, 4, hand, 0)
        link.send(
            give_ref.at[pl.ds(group * 4, 4)], theirs_ref.at[pl.ds(group * 4, 4)], GATHER_KEYS + group, link.sibling
        )
    spreads = []
    for pair in range(2):
        corners = []
        for k in range(2):
            empty = jnp.zeros((ROWS, E_CAP), BF)
            lane = lax.broadcasted_iota(jnp.int32, (ROWS, E_CAP), 1).astype(F32)
            for codes in upright:
                hit = (codes[2 * pair + k] == lane).astype(BF)
                corners.append(jnp.concatenate([hit, empty] if k == 0 else [empty, hit], axis=1))
        spreads.append(
            jnp.concatenate(
                [jnp.concatenate(corners[0:2], axis=1), jnp.concatenate(corners[2:4], axis=1)], axis=0
            )
        )
    for group in range(4):
        link.arrive(theirs_ref.at[pl.ds(group * 4, 4)], GATHER_KEYS + group)

        def merge(k, _):
            i = group * 4 + k
            ours = project(core, i)
            for pair in range(2):
                rows = slice(pair * 128, (pair + 1) * 128)
                stacked = jnp.concatenate([ours[rows], theirs_ref[i, rows]], axis=0)
                spread = jnp.dot(spreads[pair], stacked, preferred_element_type=F32).astype(BF)
                for x in range(2):
                    for half in range(2):
                        sum_ref[2 * pair + x, group, k, half] = spread[
                            x * 128 : (x + 1) * 128, half * 128 : (half + 1) * 128
                        ]
            return 0

        lax.fori_loop(0, 4, merge, 0)

    def finish(row, rows, half, total):
        spot = (pl.ds(row, rows), pl.ds(half * 128, 128))
        out_ref[spot] = (kept_ref[spot] + total).astype(BF)

    ring_reduce(
        at, link, sum_ref, AXES, ORDERS, PART_ROWS, 1, ((half0, full0), full1, full2), GATHER_KEYS + 4, finish
    )
    link.finish()


LOG2E = 1.4426950408889634


def member_codes(request_ref, request_branch_ref, parent_ref, root_owner_ref, branch_owner_ref, code_ref, dp):
    def grid(shape, dim):
        return lax.broadcasted_iota(jnp.int32, shape, dim)

    def wide(ref):
        return jnp.broadcast_to(ref[...], (8, ref.shape[1]))

    def stand(matrix, row):
        return lax.dot_general(matrix.astype(BF), row.astype(BF), BY_ROW, preferred_element_type=F32)[:, 0:1]

    roots, branches, slots = root_owner_ref.shape[1], parent_ref.shape[1], request_ref.shape[1]
    square = (branches, branches)
    unit = grid(square, 0) == grid(square, 1)
    earlier = grid(square, 1) < grid(square, 0)
    owned = (wide(branch_owner_ref) == dp).astype(F32)
    branch_owned, branch_place = stand(unit, owned), stand(earlier, owned)
    parent = stand(unit, wide(parent_ref).astype(F32)).astype(jnp.int32)
    kid = jnp.sum(jnp.where((parent == parent_ref[...]) & earlier, 1.0, 0.0), axis=1, keepdims=True)
    root_owned = (wide(root_owner_ref) == dp).astype(F32)
    before = grid((roots, roots), 0) < grid((roots, roots), 1)
    root_place = jnp.dot(root_owned.astype(BF), before.astype(BF), preferred_element_type=F32)
    chosen = parent == grid((branches, roots), 1)
    parent_place = jnp.sum(jnp.where(chosen, root_place[0:1], 0.0), axis=1, keepdims=True)
    parent_owned = jnp.sum(jnp.where(chosen, root_owned[0:1], 0.0), axis=1, keepdims=True)
    root_base = jnp.where(parent_owned > 0.5, parent_place * ROWS + kid * BR_CAP, -4096.0)
    branch_base = jnp.where(branch_owned > 0.5, branch_place * BR_CAP, -4096.0)
    branch_row = wide(request_branch_ref).astype(F32).astype(BF)
    later = (grid((ROWS, ROWS), 0) < grid((ROWS, ROWS), 1)).astype(BF)
    count = jnp.zeros((branches, 1), F32)
    for block in range(slots // ROWS):
        span = slice(block * ROWS, (block + 1) * ROWS)
        asked = (grid((slots, ROWS), 0) == request_ref[0:1, span]).astype(BF)
        branch = jnp.dot(branch_row, asked, preferred_element_type=F32).astype(jnp.int32)[0:1]
        member = grid((branches, ROWS), 0) == branch
        rank = jnp.dot(member.astype(BF), later, preferred_element_type=F32) + count
        count += jnp.sum(jnp.where(member, 1.0, 0.0), axis=1, keepdims=True)
        for kind, base in enumerate((root_base, branch_base)):
            code = jnp.sum(jnp.where(member, base + rank, 0.0), axis=0, keepdims=True)
            code_ref[kind : kind + 1, span] = jnp.maximum(code, -1.0).astype(jnp.int32)


def query_kernel(
    queries_ref, routes_ref, request_ref, request_branch_ref, parent_ref, root_owner_ref, branch_owner_ref,
    all_ref, all_routes_ref, code_ref, local_sem, route_sem, send_sem, recv_sem,
):
    at = place()
    link = Link(at, (send_sem, recv_sem))
    sibling = link.sibling
    right, left = step_along(at, "x", 1), step_along(at, "x", 3)
    x, core = at["x"], at["c"]
    peers = [(by, device_of(at, x=(x + by // 2) % 4, c=(core + by) % 2)) for by in range(1, 8)]
    greet([device for _, device in peers])
    kv_head = lax.axis_index("mp") // 2
    own = queries_ref.at[:, pl.ds(pl.multiple_of(kv_head * 512, 512), 512)]
    mine = all_ref.at[x, core]
    link.send(own, mine, 0, right)
    link.send(own, mine, 1, left)
    link.send(own, mine, 4, sibling)
    local = [
        pltpu.make_async_copy(own, mine, local_sem),
        pltpu.make_async_copy(routes_ref, all_routes_ref.at[x, core], route_sem),
    ]
    for copy in local:
        copy.start()
    for by, device in peers:
        link.send(routes_ref, all_routes_ref.at[x, core], 8 + by, device)
    low, high, far = (x + 3) % 4, (x + 1) % 4, (x + 2) % 4
    upper, lower = pl.ds(0, 64), pl.ds(64, 64)
    from_low, from_high = all_ref.at[low, core], all_ref.at[high, core]
    link.arrive(from_low, 0)
    first = all_ref.at[low, core, upper]
    link.send(first, first, 2, right)
    link.arrive(from_high, 1)
    second = all_ref.at[high, core, lower]
    link.send(second, second, 3, left)
    link.send(from_low, from_low, 5, sibling)
    link.send(from_high, from_high, 6, sibling)
    code_ref[...] = jnp.full_like(code_ref, -1)
    member_codes(
        request_ref, request_branch_ref, parent_ref, root_owner_ref, branch_owner_ref, code_ref, lax.axis_index("dp")
    )
    for key, rows in ((2, upper), (3, lower)):
        ref = all_ref.at[far, core, rows]
        link.arrive(ref, key)
        link.send(ref, ref, key + 5, sibling)
    for key, ref in (
        (4, all_ref.at[x, 1 - core]),
        (5, all_ref.at[low, 1 - core]),
        (6, all_ref.at[high, 1 - core]),
        (7, all_ref.at[far, 1 - core, upper]),
        (8, all_ref.at[far, 1 - core, lower]),
    ):
        link.arrive(ref, key)
    for by in range(1, 8):
        giver = all_routes_ref.at[(x + 4 - by // 2) % 4, (core + by) % 2]
        link.arrive(giver, 8 + by)
    for copy in local:
        copy.wait()
    link.finish()


def gather_queries(queries, routes, *tables):
    return pl.pallas_call(
        query_kernel,
        out_shape=(
            jax.ShapeDtypeStruct((4, 2, ROWS, 512), BF),
            jax.ShapeDtypeStruct((4, 2, 2, ROWS), jnp.int32),
            jax.ShapeDtypeStruct((8, 1024), jnp.int32),
        ),
        in_specs=[pl.BlockSpec(memory_space=pl.ANY)] * 2 + [pl.BlockSpec(memory_space=pltpu.VMEM)] * 5,
        out_specs=(pl.BlockSpec(memory_space=pl.ANY),) * 2 + (pl.BlockSpec(memory_space=pltpu.VMEM),),
        scratch_shapes=[
            pltpu.SemaphoreType.DMA,
            pltpu.SemaphoreType.DMA,
            pltpu.SemaphoreType.DMA((16,)),
            pltpu.SemaphoreType.DMA((16,)),
        ],
        compiler_params=pltpu.CompilerParams(collective_id=3, has_side_effects=True),
        name="gather_queries",
    )(queries, routes, *(table[None, :] for table in tables))


HEAD_STEPS = 1
SCALE2 = LOG2E * 128 ** (-0.5)
BY_ROW = (((1,), (1,)), ((), ()))


def node_kernel(
    root_owner_ref, branch_owner_ref, root_pages_ref, branch_pages_ref, root_len_ref, branch_len_ref,
    all_hbm, pages_hbm, code_row_ref,
    sum_ref, stat_ref,
    query_ref, acc_ref, max_ref, total_ref, node_sum_ref, node_stat_ref, picked_ref, all_ref, pages_ref,
    root_id_ref, branch_id_ref, load_sem,
):
    loads = [
        pltpu.make_async_copy(all_hbm, all_ref, load_sem.at[0]),
        pltpu.make_async_copy(pages_hbm, pages_ref, load_sem.at[1]),
    ]
    for load in loads:
        load.start()
    dp = lax.axis_index("dp")
    part = lax.axis_index("mp") % 2
    lane = lax.broadcasted_iota(jnp.int32, (1, 128), 1)
    for owner_ref, id_ref in ((root_owner_ref, root_id_ref), (branch_owner_ref, branch_id_ref)):

        def scan(i, found):
            owned = owner_ref[i] == dp

            @pl.when(owned)
            def _():
                id_ref[found] = i

            return found + owned.astype(jnp.int32)

        lax.fori_loop(0, owner_ref.shape[0], scan, 0)
    loads[0].wait()
    loads[1].wait()

    for kind in range(2):
        wanted = lax.broadcasted_iota(jnp.int32, (256, 1024), 0)
        chosen = (wanted == code_row_ref[kind : kind + 1, :]).astype(BF)
        picked_ref[kind * 256 : kind * 256 + 256, :] = jnp.dot(
            chosen, all_ref[...], preferred_element_type=F32
        ).astype(BF)

    def keep_stats(row, rows, stats):
        for i in range(3):
            piece = stats.astype(BF)
            node_stat_ref[i, pl.ds(row, rows), :] = piece
            stats = stats - piece.astype(F32)

    def put(row, rows):
        stats = jnp.zeros((rows, 128), F32)
        for h in range(4):
            span = pl.ds(h * rows, rows)
            node_sum_ref[pl.ds(row, rows), h * 128 : (h + 1) * 128] = acc_ref[span, :].astype(BF)
            stats = jnp.where(lane == h, max_ref[span, 0:1], stats)
            stats = jnp.where(lane == 4 + h, total_ref[span, 0:1], stats)
        keep_stats(row, rows, stats)

    chunk = 8
    for k in range(ROOT_DEV):
        root = root_id_ref[k]
        length = root_len_ref[root]
        for h in range(4):
            query_ref[h * 128 : (h + 1) * 128, :] = picked_ref[k * 128 : (k + 1) * 128, h * 128 : (h + 1) * 128]
        acc_ref[...] = jnp.zeros_like(acc_ref)
        max_ref[...] = jnp.full_like(max_ref, MASKED_SCORE)
        total_ref[...] = jnp.zeros_like(total_ref)
        used = (length - part * 64 + PAGE - 1) // PAGE
        steps = (used + chunk - 1) // chunk

        def body(i, _):
            ids = [root_pages_ref[root, i * chunk + j] for j in range(chunk)]
            keys = jnp.concatenate([pages_ref[0, page] for page in ids], axis=0)
            values = jnp.concatenate([pages_ref[1, page] for page in ids], axis=0)
            spot = lax.broadcasted_iota(jnp.int32, (1, chunk * 64), 1)
            spot = (i * chunk + spot // 64) * PAGE + part * 64 + spot % 64
            usable = spot < length
            for h in range(HEAD_STEPS):
                span = pl.ds(h * (512 // HEAD_STEPS), 512 // HEAD_STEPS)
                scores = lax.dot_general(query_ref[span, :], keys, BY_ROW, preferred_element_type=F32)
                scores = jnp.where(usable, scores * SCALE2, MASKED_SCORE)
                old = max_ref[span, :]
                new = jnp.maximum(old, jnp.max(scores, axis=1, keepdims=True))
                weights = jnp.exp2(scores - new[:, 0:1])
                fade = jnp.exp2(old - new)
                total_ref[span, :] = total_ref[span, :] * fade + jnp.sum(weights, axis=1, keepdims=True)
                acc_ref[span, :] = acc_ref[span, :] * fade + jnp.dot(
                    weights.astype(BF), values, preferred_element_type=F32
                )
                max_ref[span, :] = new
            return 0

        lax.fori_loop(0, steps, body, 0)
        put(k * 128, 128)

    def branch_work(b):
        branch = branch_id_ref[b]
        length = branch_len_ref[branch]
        row = pl.multiple_of(256 + b * 32, 32)
        picked = picked_ref[pl.ds(row, 32), :]
        stacked = jnp.concatenate([picked[:, h * 128 : (h + 1) * 128] for h in range(4)], axis=0)
        ids = [branch_pages_ref[j, branch] for j in range(4)]
        keys = jnp.concatenate([pages_ref[0, page] for page in ids], axis=0)
        values = jnp.concatenate([pages_ref[1, page] for page in ids], axis=0)
        spot = lax.broadcasted_iota(jnp.int32, (1, 256), 1)
        spot = (spot // 64) * PAGE + part * 64 + spot % 64
        usable = spot < length
        scores = lax.dot_general(stacked, keys, BY_ROW, preferred_element_type=F32)
        scores = jnp.where(usable, scores * SCALE2, MASKED_SCORE)
        top = jnp.max(scores, axis=1, keepdims=True)
        weights = jnp.where(usable, jnp.exp2(scores - top), 0.0)
        total = jnp.sum(weights, axis=1, keepdims=True)
        acc = jnp.dot(weights.astype(BF), values, preferred_element_type=F32)
        stats = jnp.zeros((32, 128), F32)
        for h in range(4):
            node_sum_ref[pl.ds(row, 32), h * 128 : (h + 1) * 128] = acc[h * 32 : (h + 1) * 32].astype(BF)
            stats = jnp.where(lane == h, top[h * 32 : (h + 1) * 32], stats)
            stats = jnp.where(lane == 4 + h, total[h * 32 : (h + 1) * 32], stats)
        keep_stats(row, 32, stats)

    def branch_body(i, _):
        for k in range(4):
            branch_work(i * 4 + k)
        return 0

    lax.fori_loop(0, BR_DEV // 4, branch_body, 0)

    unit = lax.broadcasted_iota(jnp.int32, (ROWS, ROWS), 0) == lax.broadcasted_iota(jnp.int32, (ROWS, ROWS), 1)
    unit = unit.astype(BF)

    def spread_work(block):
        parts = []
        wanted = lax.broadcasted_iota(jnp.int32, (ROWS, 256), 1)
        row = code_row_ref[:, pl.ds(pl.multiple_of(block * ROWS, ROWS), ROWS)].astype(F32).astype(BF)
        codes = lax.dot_general(unit, row, BY_ROW, preferred_element_type=F32).astype(jnp.int32)
        for kind in range(2):
            code = codes[:, kind : kind + 1]
            chosen = wanted == code
            rows = slice(kind * 256, kind * 256 + 256)
            sums = jnp.dot(chosen.astype(BF), node_sum_ref[rows, :], preferred_element_type=F32)
            stats = sum(
                jnp.dot(chosen.astype(BF), node_stat_ref[i, rows, :], preferred_element_type=F32)
                for i in (2, 1, 0)
            )
            stats = jnp.where((lane < 4) & (code < 0), MASKED_SCORE, stats)
            parts.append((sums, stats))
        merged, stats = merge_blocks(parts[0], parts[1], 4)
        sum_ref[block] = merged.astype(BF)
        stat_ref[block] = stats.T[0:8]

    def spread_body(i, _):
        for k in range(4):
            spread_work(i * 4 + k)
        return 0

    lax.fori_loop(0, 2, spread_body, 0)


def merge_blocks(one, two, heads):
    sums_one, stats_one = one
    sums_two, stats_two = two
    lane = lax.broadcasted_iota(jnp.int32, (1, 128), 1)
    top = jnp.maximum(stats_one, stats_two)
    factor_one, factor_two = jnp.exp2(stats_one - top), jnp.exp2(stats_two - top)
    total = stats_one * pltpu.roll(factor_one, 4, 1) + stats_two * pltpu.roll(factor_two, 4, 1)
    stats = jnp.where(lane < 4, top, jnp.where(lane < 8, total, 0.0))
    pieces = []
    for h in range(heads):
        span = slice(h * 128, (h + 1) * 128)
        pieces.append(
            sums_one[:, span].astype(F32) * factor_one[:, h : h + 1]
            + sums_two[:, span].astype(F32) * factor_two[:, h : h + 1]
        )
    return jnp.concatenate(pieces, axis=1), stats


def node_partials(tables, all_queries, pages, codes):
    vmem, hbm = pl.BlockSpec(memory_space=pltpu.VMEM), pl.BlockSpec(memory_space=pl.ANY)
    return pl.pallas_call(
        node_kernel,
        out_shape=(
            jax.ShapeDtypeStruct((8, ROWS, 512), BF),
            jax.ShapeDtypeStruct((8, 8, ROWS), F32),
        ),
        in_specs=[pl.BlockSpec(memory_space=pltpu.SMEM)] * 6 + [hbm, hbm, vmem],
        out_specs=(vmem, vmem),
        scratch_shapes=[
            pltpu.VMEM((512, 128), BF),
            pltpu.VMEM((512, 128), F32),
            pltpu.VMEM((512, 128), F32),
            pltpu.VMEM((512, 128), F32),
            pltpu.VMEM((512, 512), BF),
            pltpu.VMEM((3, 512, 128), BF),
            pltpu.VMEM((512, 512), BF),
            pltpu.VMEM(all_queries.shape, BF),
            pltpu.VMEM(pages.shape, BF),
            pltpu.SMEM((ROOT_DEV,), jnp.int32),
            pltpu.SMEM((BR_DEV,), jnp.int32),
            pltpu.SemaphoreType.DMA((2,)),
        ],
        compiler_params=pltpu.CompilerParams(vmem_limit_bytes=62 * 2**20),
        name="node_partials",
    )(*tables, all_queries, pages, codes)


def attend_kernel(
    at, begin,
    sum_hbm, stat_hbm, query_hbm, leaf_hbm, leaf_len_ref, fresh_hbm, weight_hbm, residual_ref,
    hidden_ref, narrow_ref,
    own_sum, own_stat, their_sum, their_stat, run_sum, run_stat, land_sum, land_stat,
    query_ref, wide_query, own_query_ref, leaf_ref, length_ref, fresh_ref, weight_ref,
    leaf_sum, leaf_stat, give_stat, side_sum, side_stat, give_sum,
    proj_ref, full1, full2, load_sem, send_sem, recv_sem,
):
    link = Link(at, (send_sem, recv_sem))
    send, arrive, sibling = link.send, link.arrive, link.sibling
    beside = {**at, "z": at["z"] + 1 - 2 * (at["z"] % 2)}
    x, core = at["x"], at["c"]
    part = at["z"] % 2
    mp = lax.axis_index("mp")
    kv_head = mp // 2

    def columns(ref, width, index):
        return ref.at[:, pl.ds(pl.multiple_of(index * width, width), width)]

    loads = [
        pltpu.make_async_copy(src, dst, load_sem.at[i])
        for i, (src, dst) in enumerate(
            (
                (columns(query_hbm, 512, kv_head), query_ref),
                (leaf_hbm.at[:, :, 0], leaf_ref),
                (sum_hbm.at[:, core], own_sum),
                (stat_hbm.at[:, core], own_stat),
                (columns(query_hbm, 256, mp), own_query_ref),
                (columns(fresh_hbm.at[0], 128, kv_head), fresh_ref.at[0]),
                (columns(fresh_hbm.at[1], 128, kv_head), fresh_ref.at[1]),
                (weight_hbm, weight_ref),
            )
        )
    ]
    for load in loads:
        load.start()
    greet(all_peers(at))
    send(sum_hbm.at[:, 1 - core], their_sum, 0, sibling)
    send(stat_hbm.at[:, 1 - core], their_stat, 1, sibling)
    lane = lax.broadcasted_iota(jnp.int32, (1, 128), 1)
    unit = lax.broadcasted_iota(jnp.int32, (ROWS, ROWS), 0) == lax.broadcasted_iota(
        jnp.int32, (ROWS, ROWS), 1
    )
    lengths_row = jnp.broadcast_to(leaf_len_ref[...], (ROWS, ROWS))
    length_ref[...] = jnp.broadcast_to(
        jnp.sum(jnp.where(unit, lengths_row, 0), axis=1, keepdims=True), (ROWS, ROWS)
    )

    def upright(stats):
        return jnp.concatenate([stats, jnp.zeros((ROWS - 8, ROWS), F32)], axis=0).T

    def leaf_group(base):
        span = pl.ds(base, 8)
        heads = [wide_query[span, h * 128 : (h + 1) * 128] for h in range(4)]
        stacked = jnp.concatenate(heads, axis=0)
        keys = leaf_ref[0, span].reshape(512, 128)
        values = leaf_ref[1, span].reshape(512, 128)
        scores = lax.dot_general(
            stacked.astype(BF), keys, BY_ROW, preferred_element_type=F32
        )
        row = lax.broadcasted_iota(jnp.int32, (32, 512), 0) % 8
        col = lax.broadcasted_iota(jnp.int32, (32, 512), 1)
        lengths = jnp.concatenate([length_ref[span, 0:1]] * 4, axis=0)
        usable = (row == col // 64) & (part * 64 + col % 64 < lengths)
        scores = jnp.where(usable, scores * SCALE2, MASKED_SCORE)
        top = jnp.max(scores, axis=1, keepdims=True)
        weights = jnp.where(usable, jnp.exp2(scores - top), 0.0)
        total = jnp.sum(weights, axis=1, keepdims=True)
        acc = jnp.dot(weights.astype(BF), values, preferred_element_type=F32)
        stats = jnp.zeros((8, 128), F32)
        for h in range(4):
            leaf_sum[span, h * 128 : (h + 1) * 128] = acc[h * 8 : (h + 1) * 8]
            stats = jnp.where(lane == h, top[h * 8 : (h + 1) * 8], stats)
            stats = jnp.where(lane == 4 + h, total[h * 8 : (h + 1) * 8], stats)
        leaf_stat[span, :] = stats

    def leaf_body(i, _):
        for k in range(4):
            leaf_group(pl.multiple_of(i * 32 + k * 8, 8))
        return 0

    loads[2].wait()
    loads[3].wait()
    arrive(their_sum, 0)
    arrive(their_stat, 1)
    for by in (2, 1, 3):
        value = (x + by) % 4
        merged, stats = merge_blocks(
            (own_sum[value], upright(own_stat[value])), (their_sum[value], upright(their_stat[value])), 4
        )
        run_sum[by - 1] = merged.astype(BF)
        run_stat[by - 1] = stats.T[0:8]
        device = step_along(at, "x", by)
        send(run_sum.at[by - 1], land_sum.at[by - 1], 2 * by, device)
        send(run_stat.at[by - 1], land_stat.at[by - 1], 2 * by + 1, device)
    loads[0].wait()
    loads[1].wait()
    begin()
    wide_query[...] = query_ref[...].astype(F32)
    lax.fori_loop(0, 4, leaf_body, 0)
    sums, stats = merge_blocks(
        (own_sum[x], upright(own_stat[x])), (their_sum[x], upright(their_stat[x])), 4
    )
    sums, stats = merge_blocks((sums, stats), (leaf_sum[...], leaf_stat[...]), 4)
    for load in loads[4:]:
        load.wait()
    fresh_key = fresh_ref[0].astype(F32)
    fresh_value = fresh_ref[1].astype(F32)
    own_scores = [
        jnp.sum(own_query_ref[:, h * 128 : (h + 1) * 128].astype(F32) * fresh_key, axis=1, keepdims=True)
        * SCALE2
        for h in range(2)
    ]
    for by in (1, 3, 2):
        arrive(land_sum.at[by - 1], 2 * by)
        arrive(land_stat.at[by - 1], 2 * by + 1)
        sums, stats = merge_blocks((sums, stats), (land_sum[by - 1], upright(land_stat[by - 1])), 4)
    first = part == 0
    give_sum[...] = jnp.where(first, sums[:, 256:], sums[:, :256]).astype(BF)
    give_stat[...] = stats.T[0:8]
    send(give_sum, side_sum, 10, device_of(beside))
    send(give_stat, side_stat, 11, device_of(beside))
    kept = jnp.where(first, sums[:, :256], sums[:, 256:])
    arrive(side_sum, 10)
    arrive(side_stat, 11)
    theirs = upright(side_stat[...])
    pieces = []
    for h in range(2):
        span = slice(h * 128, (h + 1) * 128)

        def column(from_stats, offset):
            return jnp.where(
                first,
                from_stats[:, offset + h : offset + h + 1],
                from_stats[:, offset + 2 + h : offset + 3 + h],
            )

        top_one, top_two = column(stats, 0), column(theirs, 0)
        top = jnp.maximum(jnp.maximum(top_one, top_two), own_scores[h])
        factor_one, factor_two = jnp.exp2(top_one - top), jnp.exp2(top_two - top)
        factor_own = jnp.exp2(own_scores[h] - top)
        weighted = (
            kept[:, span] * factor_one
            + side_sum[:, span].astype(F32) * factor_two
            + factor_own * fresh_value
        )
        total = column(stats, 4) * factor_one + column(theirs, 4) * factor_two + factor_own
        pieces.append((weighted / total).astype(BF))
    attended = jnp.concatenate(pieces, axis=1)
    for i in range(16):
        product = jnp.dot(
            attended, weight_ref[:, i * 256 : (i + 1) * 256], preferred_element_type=F32
        ).astype(BF)
        for half in range(2):
            proj_ref[i // 4, i % 4, half] = product[:, half * 128 : (half + 1) * 128]

    def finish(row, rows, half, total):
        cols = pl.ds(half * 128, 128)
        total += residual_ref[pl.ds(row, rows), cols].astype(F32)
        hidden_ref[pl.ds(row, rows), cols] = total
        narrow_ref[half, pl.ds(row, rows), :] = total.astype(BF)

    ring_reduce(
        at, link, proj_ref, ("y", "z"), (("y", "z"), ("z", "y")), ((0, 64), (64, 64)), 0,
        (full1, full2), 12, finish,
    )
    link.finish()


def layer_kernel(*refs):
    ins, out_ref = refs[:13], refs[13]
    attend_refs = refs[14 : 14 + ATTEND_SCRATCH]
    hidden_ref, narrow_ref, tables_sem, weight_sem = refs[14 + ATTEND_SCRATCH : 18 + ATTEND_SCRATCH]
    expert_refs = refs[18 + ATTEND_SCRATCH :]
    at = place()
    tables = [
        pltpu.make_async_copy(ins[8 + i], expert_refs[i], tables_sem.at[i]) for i in range(3)
    ]
    loads = [
        pltpu.make_async_copy(ins[11 + i], expert_refs[EXPERT_WEIGHTS + i], weight_sem.at[i]) for i in range(2)
    ]

    def begin():
        for load in tables + loads:
            load.start()

    attend_kernel(at, begin, *ins[:8], hidden_ref, narrow_ref, *attend_refs)
    expert_kernel(at, loads, tables, out_ref, hidden_ref, narrow_ref, *expert_refs)


ATTEND_SCRATCH = 27
EXPERT_WEIGHTS = 8


def attend_and_route(
    sums, stats, queries, leaf, leaf_len, fresh, out_weight, residual, routes, gain, router, expert_in, expert_out
):
    keys = GATHER_KEYS + 4 + 42
    vmem, hbm = pl.BlockSpec(memory_space=pltpu.VMEM), pl.BlockSpec(memory_space=pl.ANY)
    return pl.pallas_call(
        layer_kernel,
        out_shape=jax.ShapeDtypeStruct((ROWS, 256), BF),
        in_specs=[hbm, hbm, hbm, hbm, vmem, hbm, hbm, vmem] + [hbm] * 5,
        out_specs=vmem,
        scratch_shapes=[
            pltpu.VMEM((4, ROWS, 512), BF),
            pltpu.VMEM((4, 8, ROWS), F32),
            pltpu.VMEM((4, ROWS, 512), BF),
            pltpu.VMEM((4, 8, ROWS), F32),
            pltpu.VMEM((3, ROWS, 512), BF),
            pltpu.VMEM((3, 8, ROWS), F32),
            pltpu.VMEM((3, ROWS, 512), BF),
            pltpu.VMEM((3, 8, ROWS), F32),
            pltpu.VMEM((ROWS, 512), BF),
            pltpu.VMEM((ROWS, 512), F32),
            pltpu.VMEM((ROWS, 256), BF),
            pltpu.VMEM((2, ROWS, 64, 128), BF),
            pltpu.VMEM((ROWS, ROWS), jnp.int32),
            pltpu.VMEM((2, ROWS, 128), BF),
            pltpu.VMEM((256, 4096), BF),
            pltpu.VMEM((ROWS, 512), F32),
            pltpu.VMEM((ROWS, 128), F32),
            pltpu.VMEM((8, ROWS), F32),
            pltpu.VMEM((ROWS, 256), BF),
            pltpu.VMEM((8, ROWS), F32),
            pltpu.VMEM((ROWS, 256), BF),
            pltpu.VMEM((4, 4, 2, ROWS, 128), BF),
            pltpu.VMEM((3, 4, 2, ROWS, 128), BF),
            pltpu.VMEM((3, 2, ROWS, 128), BF),
            pltpu.SemaphoreType.DMA((8,)),
            pltpu.SemaphoreType.DMA((28,)),
            pltpu.SemaphoreType.DMA((28,)),
            pltpu.VMEM((ROWS, 256), F32),
            pltpu.VMEM((2, ROWS, 128), BF),
            pltpu.SemaphoreType.DMA((3,)),
            pltpu.SemaphoreType.DMA((2,)),
            pltpu.VMEM(routes.shape, jnp.int32),
            pltpu.VMEM(gain.shape, F32),
            pltpu.VMEM(router.shape, BF),
            pltpu.VMEM((4, 2, 4, 4, 2, ROWS, 128), BF),
            pltpu.VMEM((8, ROWS), jnp.int32),
            pltpu.VMEM((8, ROWS), jnp.int32),
            pltpu.VMEM((512, 4096), BF),
            pltpu.VMEM((512, 128), F32),
            pltpu.VMEM(expert_in.shape, BF),
            pltpu.VMEM(expert_out.shape, BF),
            pltpu.VMEM((512, 512), BF),
            pltpu.VMEM((16, 256, 256), BF),
            pltpu.VMEM((16, 256, 256), BF),
            pltpu.VMEM((4, 4, 4, 2, ROWS, 128), BF),
            pltpu.VMEM((2, 4, 4, ROWS, 128), BF),
            pltpu.VMEM((2, 4, 4, 2, ROWS, 128), BF),
            pltpu.VMEM((3, 4, 2, ROWS, 128), BF),
            pltpu.VMEM((3, 2, ROWS, 128), BF),
            pltpu.SemaphoreType.DMA,
            pltpu.SemaphoreType.DMA((keys,)),
            pltpu.SemaphoreType.DMA((keys,)),
        ],
        compiler_params=pltpu.CompilerParams(
            collective_id=1, has_side_effects=True, vmem_limit_bytes=62 * 2**20
        ),
        name="attend_and_route",
    )(sums, stats, queries, leaf, leaf_len, fresh, out_weight, residual, routes, gain, router, expert_in, expert_out)


def shards(
    queries,
    new_kv,
    residual,
    out_weight,
    norm_gain,
    router,
    expert_in,
    expert_out,
    node_cache,
    leaf_cache,
    slot_request,
    request_branch,
    branch_parent,
    root_owner,
    branch_owner,
    root_pages,
    branch_pages,
    root_len,
    branch_len,
    leaf_len,
    routes,
):
    all_queries, all_routes, codes = gather_queries(
        queries,
        routes.T,
        slot_request,
        request_branch,
        branch_parent,
        root_owner,
        branch_owner,
    )
    sums, stats = node_partials(
        (root_owner, branch_owner, root_pages, branch_pages.T, root_len, branch_len),
        all_queries.reshape(8 * ROWS, 512),
        node_cache[:, :, 0],
        codes,
    )
    return attend_and_route(
        sums.reshape(4, 2, ROWS, 512),
        stats.reshape(4, 2, 8, ROWS),
        queries,
        leaf_cache,
        leaf_len[None, :],
        new_kv,
        out_weight,
        residual,
        all_routes,
        norm_gain.reshape(16, 1, 256),
        router.T,
        expert_in[0],
        expert_out[0],
    )


def solution(mesh):
    placed = (
        P("dp", None),
        P(None, "dp", None),
        P("dp", "mp"),
        P("mp", None),
        P(),
        P(),
        P("dp", None, "mp", None),
        P("dp", "mp", None),
        P(None, "dp", "mp", None, None),
        P(None, "dp", "mp", None, None),
        P(),
        P(),
        P(),
        P(),
        P(),
        P(),
        P(),
        P(),
        P(),
        P("dp"),
        P("dp", None),
    )
    return jax.shard_map(
        shards, mesh=mesh, in_specs=placed, out_specs=P("dp", "mp"), check_vma=False
    )
```
